512 devices in a mesh: dom: 256 (over x, z, y_hi, core), band: 2 (over y_lo).
Axes of the slice: x: 4, y: 4 (y_hi: 2, y_lo: 2; y = y_hi * 2 + y_lo), z: 16, core: 2. Of those that a mesh axis runs over, the one named last changes fastest.
Arguments:
- residual: float32 [16, 2048, 8, 128], P('band', 'dom'), may hold values from -24 to 24
- potential: float32 [2048, 8, 128], P(('dom', 'band')), may hold values from 0.05 to 1
- shifts: float32 [16], P('band'), may hold values from 0.05 to 0.5
Outputs:
- correction: float32 [16, 2048, 8, 128], P('band', 'dom')
The draws below stay inside these ranges and needn't reach their ends.
All inputs are finite; a program needn't handle non-finite values.
Results may differ from the reference program's by a relative error of at most 0.00002.
Values sent between devices are 32-bit elements; how exact they have to be, the bound alone decides.
No kernel may reach another device: no remote copies, remote signals or barrier semaphores. Data moves between devices by JAX's collectives and lax.ppermute only.
A program may use at most 64 MiB of HBM per device.

```python
import math
import jax
import jax.numpy as jnp
from jax import lax

ORBS = 16
CX = 8
CY = 8
CZ = 128
SWEEPS = 2
COARSE = 4
PZ = 2
PY = 16
PX = 8
N_DOM = 256


def levels(own_key, dims, pieces, low, top_value):
    gain = 1.0
    for dim, shards_of in pieces:
        draws = jax.random.uniform(jax.random.fold_in(jax.random.fold_in(own_key, 6), dim), (shards_of,), jnp.float32, low / len(pieces), top_value / len(pieces))
        gain = gain * jnp.repeat(jnp.exp(draws), dims[dim] // shards_of).reshape((-1,) + (1,) * (len(dims) - 1 - dim))
    return gain


def scatter_about(own_key, shape, deviation, most, pieces=(), dtype=jnp.bfloat16):
    gain = levels(own_key, shape, pieces, -0.22, 0.18) if pieces else 1.0
    drawn = jax.random.normal(own_key, shape, jnp.float32) * deviation * gain
    return jnp.minimum(jnp.maximum(drawn, -most), most).astype(dtype)


def setup_inputs(seed: int = 0) -> dict:
    arg_keys = jax.random.split(jax.random.key(seed), 4)
    residual = scatter_about(arg_keys[0], (ORBS, N_DOM * CX, CY, CZ), 4.0, 24.0, ((0, 2), (1, 256)), jnp.float32)
    potential = jnp.clip(jnp.exp(math.log(1.0) - 2.9957323 * jax.random.uniform(arg_keys[1], (N_DOM * CX, CY, CZ), jnp.float32) ** levels(arg_keys[1], (N_DOM * CX, CY, CZ), ((0, 512),), -0.2, 0.2)), 0.05, 1.0)
    shifts = jnp.clip(jnp.exp(math.log(0.5) - 2.3025851 * jax.random.uniform(arg_keys[2], (ORBS,), jnp.float32) ** levels(arg_keys[2], (ORBS,), ((0, 2),), -0.2, 0.2)), 0.05, 0.5)
    return dict(residual=residual, potential=potential, shifts=shifts)


OMEGA = 0.7
KINETIC = 2.0


def neighbour_sums(padded):
    faces = (padded[:, 2:, 1:-1, 1:-1] + padded[:, :-2, 1:-1, 1:-1]
             + padded[:, 1:-1, 2:, 1:-1] + padded[:, 1:-1, :-2, 1:-1]
             + padded[:, 1:-1, 1:-1, 2:] + padded[:, 1:-1, 1:-1, :-2])
    edges = (padded[:, 2:, 2:, 1:-1] + padded[:, 2:, :-2, 1:-1]
             + padded[:, :-2, 2:, 1:-1] + padded[:, :-2, :-2, 1:-1]
             + padded[:, 2:, 1:-1, 2:] + padded[:, 2:, 1:-1, :-2]
             + padded[:, :-2, 1:-1, 2:] + padded[:, :-2, 1:-1, :-2]
             + padded[:, 1:-1, 2:, 2:] + padded[:, 1:-1, 2:, :-2]
             + padded[:, 1:-1, :-2, 2:] + padded[:, 1:-1, :-2, :-2])
    return faces, edges


def operator(field, weight, kinetic, padder):
    faces, edges = neighbour_sums(padder(field))
    return -(kinetic / 6.0) * (2.0 * faces + edges - 24.0 * field) + weight * field


def smooth(field, source, weight, kinetic, padder):
    return field + OMEGA * (source - operator(field, weight, kinetic, padder)) / (4.0 * kinetic + weight)


def restrict(field):
    leading, size_x, size_y, size_z = field.shape
    cubes = field.reshape(leading, size_x // 2, 2, size_y // 2, 2, size_z // 2, 2)
    return cubes.mean(axis=(2, 4, 6))


def prolong(field):
    return jnp.repeat(jnp.repeat(jnp.repeat(field, 2, axis=1), 2, axis=2), 2, axis=3)


def coarse_sweeps(source, potential_coarse, shift_field, kinetic, padder):
    weight = potential_coarse + shift_field
    field = OMEGA * source / (4.0 * kinetic + weight)
    for sweep in range(COARSE - 1):
        field = smooth(field, source, weight, kinetic, padder)
    return field


def vcycle(residual, potential, shift_field, padder, solve_coarse):
    kinetic_fine = KINETIC
    kinetic_middle = KINETIC / 4.0
    kinetic_coarse = KINETIC / 16.0
    weight_fine = potential[None] + shift_field
    potential_middle = restrict(potential[None])
    weight_middle = potential_middle + shift_field
    potential_coarse = restrict(potential_middle)
    faces, edges = neighbour_sums(padder(residual))
    source = 0.5 * residual + faces / 12.0
    fine = OMEGA * source / (4.0 * kinetic_fine + weight_fine)
    for sweep in range(SWEEPS - 1):
        fine = smooth(fine, source, weight_fine, kinetic_fine, padder)
    source_middle = restrict(source - operator(fine, weight_fine, kinetic_fine, padder))
    middle = OMEGA * source_middle / (4.0 * kinetic_middle + weight_middle)
    for sweep in range(SWEEPS - 1):
        middle = smooth(middle, source_middle, weight_middle, kinetic_middle, padder)
    source_coarse = restrict(source_middle - operator(middle, weight_middle, kinetic_middle, padder))
    coarse = solve_coarse(source_coarse, potential_coarse, shift_field, kinetic_coarse)
    middle = middle + prolong(coarse)
    for sweep in range(SWEEPS):
        middle = smooth(middle, source_middle, weight_middle, kinetic_middle, padder)
    fine = fine + prolong(middle)
    for sweep in range(SWEEPS):
        fine = smooth(fine, source, weight_fine, kinetic_fine, padder)
    return fine


def zero_pad(field):
    return jnp.pad(field, ((0, 0), (1, 1), (1, 1), (1, 1)))


def zero_coarse(source, potential_coarse, shift_field, kinetic):
    return coarse_sweeps(source, potential_coarse, shift_field, kinetic, zero_pad)


def to_grid(blocked):
    leading = blocked.shape[0]
    cubes = blocked.reshape(leading, PX, PY, PZ, CX, CY, CZ).transpose(0, 1, 4, 2, 5, 3, 6)
    return cubes.reshape(leading, PX * CX, PY * CY, PZ * CZ)


def from_grid(grid):
    leading = grid.shape[0]
    cubes = grid.reshape(leading, PX, CX, PY, CY, PZ, CZ).transpose(0, 1, 3, 5, 2, 4, 6)
    return cubes.reshape(leading, N_DOM * CX, CY, CZ)


def reference(residual, potential, shifts):
    grid_potential = to_grid(potential[None])[0]
    grid_residual = to_grid(residual)

    def one_orbital(pair):
        orbital, shift_value = pair
        shift_field = shift_value.reshape(1, 1, 1, 1)
        return vcycle(orbital[None], grid_potential, shift_field, zero_pad, zero_coarse)[0]

    result = lax.map(one_orbital, (grid_residual, shifts))
    return from_grid(result)
```

```python
import jax
import jax.numpy as jnp
from jax import lax
from jax.experimental import pallas as pl
from jax.experimental.pallas import tpu as pltpu
from jax.sharding import PartitionSpec as P


OMEGA = 0.7
KEEP = 0.3
FINE, MIDDLE, COARSE = 2.0, 0.5, 0.125
PX, PZ = 8, 2
REACH = 3
F32 = jnp.float32
HIGHEST = lax.Precision.HIGHEST


def place():
    position = lax.axis_index("dom")
    size_y = lax.axis_size("dom") // (PX * PZ)
    return position // (size_y * PZ), position // PZ % size_y, position % PZ


def dom_of(px, py, pz, size_y):
    return (px * size_y + py) * PZ + pz


def iota(shape, dimension):
    return lax.broadcasted_iota(jnp.int32, shape, dimension)


def along_x(planes):
    sublane = iota(planes[0].shape, 0)
    first = jnp.where(sublane == 0, 0.0, pltpu.roll(planes[-1], 1, 0))
    last = jnp.where(sublane == PX - 1, 0.0, pltpu.roll(planes[0], PX - 1, 0))
    below = [first] + planes[:-1]
    above = planes[1:] + [last]
    return [b + a for b, a in zip(below, above)]


def along_z(plane, open_end):
    width = plane.shape[1]
    left, right = pltpu.roll(plane, 1, 1), pltpu.roll(plane, width - 1, 1)
    if not open_end:
        lane = iota(plane.shape, 1)
        left = jnp.where(lane == 0, 0.0, left)
        right = jnp.where(lane == width - 1, 0.0, right)
    return left + right


def stencil(below, here, above, open_end=False):
    across = [a + b for a, b in zip(below, above)]
    wide = [a + (h + h) for a, h in zip(across, here)]
    turned = [e + w for e, w in zip(along_x(here), wide)]
    return [
        along_z(t, open_end) + (x + (a + a)) for t, x, a in zip(turned, along_x(wide), across)
    ]


def each(count, chunk, step):
    whole = count // chunk

    def body(index, carry):
        step(index * chunk, chunk)
        return carry

    if whole == 1:
        step(0, chunk)
    else:
        lax.fori_loop(0, whole, body, 0)
    if count % chunk:
        step(whole * chunk, count % chunk)


def take(ref, row):
    return [ref[row, i] for i in range(ref.shape[1])]


def sweep_row(rows, source, inverse, kinetic, open_end=False):
    total = stencil(*rows, open_end)
    return [
        KEEP * u + v * (s + (kinetic / 6.0) * t)
        for u, s, v, t in zip(rows[1], source, inverse, total)
    ]


def sweep(start, source, inverse, target, kinetic, count, chunk, offsets, open_end=False):
    to, of, at = offsets

    def step(base, rows):
        held = [take(start, base + (of + r - 1)) for r in range(rows + 2)]
        for r in range(rows):
            row = base + (at + r)
            new = sweep_row(held[r : r + 3], take(source, row), take(inverse, row), kinetic, open_end)
            for i, plane in enumerate(new):
                target[base + (to + r), i] = plane

    each(count, chunk, step)


def pooling(rows, columns):
    return jnp.where(iota((rows, columns), 0) // 2 == iota((rows, columns), 1), 0.5, 0.0).astype(F32)


def spreading(rows, columns):
    return jnp.where(iota((rows, columns), 0) == iota((rows, columns), 1) // 2, 1.0, 0.0).astype(F32)


def times(value, matrix):
    return jnp.dot(value, matrix, precision=HIGHEST, preferred_element_type=F32)


def cubes(low, high):
    return [
        0.25 * ((low[2 * i] + low[2 * i + 1]) + (high[2 * i] + high[2 * i + 1]))
        for i in range(len(low) // 2)
    ]


def pack(residual, own, mate, out):
    band = lax.axis_index("band")
    planes = [jnp.where(band == 0, own[i], mate[i]) for i in range(4)]
    planes += [jnp.where(band == 0, mate[i], own[i]) for i in range(4)]
    for c in range(PZ):
        rows = slice(4 * c, 4 * c + 4)
        for p in range(4):
            both = jnp.concatenate([planes[2 * p][rows], planes[2 * p + 1][rows]], axis=0)
            for orbital in range(PX):
                base = (orbital * PZ + c) * 64 + p * 8
                out[base : base + 4] = residual[orbital, 2 * p, rows]
                out[base + 4 : base + 8] = residual[orbital, 2 * p + 1, rows]
                out[base + 32 : base + 40] = both


def down(shifts, own, mate, beside, fine_out, source_out, inverse_out, cut, field, potential, source, inverse, start):
    px, py, c = place()
    size_y = lax.axis_size("dom") // (PX * PZ)
    shift = shifts[px]

    def unpack(blocks):
        for row in range(12):
            ref = blocks[row // 4]
            for i in range(8):
                at = (i // 2) * 8 + (i % 2) * 4 + row % 4
                for half in range(PZ):
                    lanes = slice(128 * half, 128 * half + 128)
                    field[row, i, :, lanes] = ref[pl.ds(half * 64 + at, PX, stride=128), :]
                    if 1 <= row <= 10:
                        potential[row - 1, i, :, lanes] = ref[pl.ds(half * 64 + 32 + at, PX, stride=128), :]

    pl.when(c == 0)(lambda: unpack((beside, own, mate)))
    pl.when(c == 1)(lambda: unpack((mate, own, beside)))

    def first(base, rows):
        for r in range(rows):
            row = base + r
            y = py * 8 + 4 * c + row - 3
            inside = jnp.where((y >= 0) & (y < 8 * size_y), OMEGA, 0.0).astype(F32)
            below, here, above = [take(field, row + d) for d in range(3)]
            for i, (b, h, a, x) in enumerate(zip(below, here, above, along_x(here))):
                s = 0.5 * h + ((b + a) + (x + along_z(h, False))) * (1.0 / 12.0)
                v = inside / (potential[row, i] + (4.0 * FINE + shift))
                source[row, i] = s
                inverse[row, i] = v
                start[row, i] = v * s

    each(10, 2, first)
    sweep(start, source, inverse, fine_out, FINE, 8, 2, (0, 1, 1))

    def keep(base, rows):
        for r in range(rows):
            for i in range(8):
                source_out[base + r, i] = source[base + (r + 2), i]
                inverse_out[base + r, i] = inverse[base + (r + 2), i]

    each(6, 2, keep)
    pool = pooling(256, 128)
    for pair in range(2):
        left = []
        for row in (2 * pair, 2 * pair + 1):
            rows = [take(fine_out, row + d) for d in (1, 2, 3)]
            weight = [v + (4.0 * FINE + shift) for v in take(potential, row + 3)]
            total = stencil(*rows)
            left.append(
                [s + (FINE / 6.0) * t - w * u for s, t, w, u in zip(take(source, row + 3), total, weight, rows[1])]
            )
        mean = cubes(*left) + cubes(take(potential, 2 * pair + 3), take(potential, 2 * pair + 4))
        small = times(jnp.concatenate(mean, axis=0), pool)
        for i in range(8):
            cut[pair, i] = small[8 * i : 8 * i + 8]


def up(shifts, fine, source, inverse, block, around, out, weight1, source1, inverse1, middle, other, source2, inverse2, coarse, coarser, work):
    px, py, c = place()
    size_y = lax.axis_size("dom") // (PX * PZ)
    shift = shifts[px]

    def inside(distance):
        return jnp.where((py + distance >= 0) & (py + distance < size_y), OMEGA, 0.0).astype(F32)

    for row in range(28):
        distance = row // 4 - REACH
        if distance == 0:
            at = lambda i: block[row % 4, i]
        else:
            side, step = (0, -distance - 1) if distance < 0 else (1, distance - 1)
            at = lambda i: around[side, step, row % 4, i]
        for i in range(4):
            s = at(i)
            w = at(4 + i) + (4.0 * MIDDLE + shift)
            v = inside(distance) / w
            source1[row, i] = s
            weight1[row, i] = w
            inverse1[row, i] = v
            other[row, i] = v * s

    sweep(other, source1, inverse1, middle, MIDDLE, 26, 4, (1, 1, 1))

    pool = pooling(128, 128)
    spread = spreading(128, 128)
    lane = iota((8, 128), 1)

    def shrink(base, pairs):
        for pair in range(pairs):
            low = 2 * base + (2 * pair + 2)
            left, weights = [], []
            for row in (low, low + 1):
                rows = [take(middle, row + d) for d in (-1, 0, 1)]
                w = take(weight1, row)
                total = stencil(*rows)
                left.append(
                    [s + (MIDDLE / 6.0) * t - x * u for s, t, x, u in zip(take(source1, row), total, w, rows[1])]
                )
                weights.append(w)
            mean = cubes(*left) + cubes(*weights)
            small = times(jnp.concatenate(mean, axis=0), pool)
            distance = (base + (pair + 1)) // 2 - REACH
            for i in range(2):
                s = small[8 * i : 8 * i + 8]
                w = small[16 + 8 * i : 24 + 8 * i] + (4.0 * COARSE - 4.0 * MIDDLE)
                v = jnp.where(lane < 64, inside(distance) / jnp.where(lane < 64, w, 1.0), 0.0)
                source2[base + pair, i] = s
                inverse2[base + pair, i] = v
                coarse[base + pair, i] = v * s

    each(12, 4, shrink)
    sweep(coarse, source2, inverse2, coarser, COARSE, 10, 10, (1, 1, 1), True)
    sweep(coarser, source2, inverse2, coarse, COARSE, 8, 8, (2, 2, 2), True)
    sweep(coarse, source2, inverse2, coarser, COARSE, 6, 6, (3, 3, 3), True)

    for row in range(3, 9):
        wide = times(jnp.concatenate(take(coarser, row), axis=0), spread)
        for fine_row in (2 * row + 2, 2 * row + 3):
            for i in range(4):
                other[fine_row, i] = middle[fine_row, i] + wide[8 * (i // 2) : 8 * (i // 2) + 8]

    sweep(other, source1, inverse1, middle, MIDDLE, 8, 4, (10, 10, 10))
    sweep(middle, source1, inverse1, other, MIDDLE, 6, 6, (11, 11, 11))

    spread = spreading(128, 256)
    for row in range(4):
        wide = times(jnp.concatenate(take(other, 11 + 2 * c + row), axis=0), spread)
        for fine_row in (2 * row, 2 * row + 1):
            for i in range(8):
                work[fine_row, i] = fine[fine_row, i] + wide[8 * (i // 2) : 8 * (i // 2) + 8]

    final = work.at[8:14]
    sweep(work, source, inverse, final, FINE, 6, 2, (0, 1, 0))
    for row in range(4):
        new = sweep_row(
            [take(final, row + d) for d in range(3)], take(source, row + 1), take(inverse, row + 1), FINE
        )
        for i, plane in enumerate(new):
            at = (i // 2) * 8 + (i % 2) * 4 + row
            for half in range(PZ):
                out[pl.ds(half * 32 + at, PX, stride=64), :] = plane[:, 128 * half : 128 * half + 128]


def unpack(blocks, out):
    for orbital in range(PX):
        for c in range(PZ):
            for i in range(8):
                base = (orbital * PZ + c) * 32 + (i // 2) * 8 + (i % 2) * 4
                out[orbital, i, 4 * c : 4 * c + 4] = blocks[base : base + 4]


def call(kernel, outs, scratch=(), smem=False):
    shapes = [jax.ShapeDtypeStruct(shape, F32) for shape in outs]
    specs = [pl.BlockSpec(memory_space=pltpu.VMEM)] * len(outs)

    def run(*args):
        given = [pl.BlockSpec(memory_space=pltpu.VMEM)] * len(args)
        if smem:
            given[0] = pl.BlockSpec(memory_space=pltpu.SMEM)
        return pl.pallas_call(
            kernel,
            out_shape=shapes,
            in_specs=given,
            out_specs=specs,
            scratch_shapes=[pltpu.VMEM(shape, F32) for shape in scratch],
            compiler_params=pltpu.CompilerParams(vmem_limit_bytes=40 * 1024 * 1024),
        )(*args)

    return run


def body(residual, potential, shifts):
    size_y = lax.axis_size("dom") // (PX * PZ)
    blocks = [(px, py, c) for px in range(PX) for py in range(size_y) for c in range(PZ)]
    lines = [
        [dom_of(px, py, c, size_y) for px in range(PX) for c in range(PZ)] for py in range(size_y)
    ]
    cores = [
        [dom_of(px, py, c, size_y) for c in range(PZ)] for px in range(PX) for py in range(size_y)
    ]

    def pairs(target):
        found = [((px, py, c), target(px, py, c)) for px, py, c in blocks]
        return [
            (dom_of(*a, size_y), dom_of(*b, size_y)) for a, b in found if 0 <= b[1] < size_y
        ]

    def swap_lines(value):
        return lax.all_to_all(value, "dom", 0, 0, axis_index_groups=lines, tiled=True)

    mate_planes = lax.ppermute(potential, "band", [(0, 1), (1, 0)])
    (packed,) = call(pack, [(1024, 128)])(residual, potential, mate_planes)
    own = swap_lines(packed)
    beside = lax.ppermute(
        own, "dom", pairs(lambda px, py, c: (px, py - 1, 1) if c == 0 else (px, py + 1, 0))
    )
    mate = lax.ppermute(own, "dom", pairs(lambda px, py, c: (px, py, 1 - c)))
    fine, source, inverse, cut = call(
        down,
        [(8, 8, 8, 256), (6, 8, 8, 256), (6, 8, 8, 256), (2, 8, 8, 128)],
        [(12, 8, 8, 256)] + [(10, 8, 8, 256)] * 4,
        smem=True,
    )(shifts, own, mate, beside)
    block = lax.all_gather(cut, "dom", axis_index_groups=cores, axis=0, tiled=True)
    sent = [
        lax.ppermute(
            block,
            "dom",
            pairs(lambda px, py, c, k=k: (px, py + k, 0) if c == 0 else (px, py - k, 1)),
        )
        for k in range(1, REACH + 1)
    ]
    around = lax.all_gather(jnp.stack(sent), "dom", axis_index_groups=cores, axis=0)
    (final,) = call(
        up,
        [(512, 128)],
        [(28, 4, 8, 128)] * 5 + [(12, 2, 8, 128)] * 4 + [(14, 8, 8, 256)],
        smem=True,
    )(shifts, fine, source, inverse, block, around)
    (correction,) = call(unpack, [(8, 8, 8, 128)])(swap_lines(final))
    return correction


def solution(mesh):
    return jax.shard_map(
        body,
        mesh=mesh,
        in_specs=(P("band", "dom", None, None), P(("dom", "band"), None, None), P("band")),
        out_specs=P("band", "dom", None, None),
        check_vma=False,
    )
```

```python
import jax
import jax.numpy as jnp
from jax import lax
from jax.experimental import pallas as pl
from jax.experimental.pallas import tpu as pltpu
from jax.sharding import PartitionSpec as P


OMEGA = 0.7
KEEP = 0.3
FINE, MIDDLE, COARSE = 2.0, 0.5, 0.125
PX, PZ = 8, 2
REACH = 3
F32 = jnp.float32
HIGHEST = lax.Precision.HIGHEST


def place():
    position = lax.axis_index("dom")
    size_y = lax.axis_size("dom") // (PX * PZ)
    return position // (size_y * PZ), position // PZ % size_y, position % PZ


def dom_of(px, py, pz, size_y):
    return (px * size_y + py) * PZ + pz


def iota(shape, dimension):
    return lax.broadcasted_iota(jnp.int32, shape, dimension)


def along_x(planes):
    sublane = iota(planes[0].shape, 0)
    first = jnp.where(sublane == 0, 0.0, pltpu.roll(planes[-1], 1, 0))
    last = jnp.where(sublane == PX - 1, 0.0, pltpu.roll(planes[0], PX - 1, 0))
    below = [first] + planes[:-1]
    above = planes[1:] + [last]
    return [b + a for b, a in zip(below, above)]


def along_z(plane, open_end):
    width = plane.shape[1]
    left, right = pltpu.roll(plane, 1, 1), pltpu.roll(plane, width - 1, 1)
    if not open_end:
        lane = iota(plane.shape, 1)
        left = jnp.where(lane == 0, 0.0, left)
        right = jnp.where(lane == width - 1, 0.0, right)
    return left + right


def stencil(below, here, above, open_end=False):
    across = [a + b for a, b in zip(below, above)]
    wide = [a + (h + h) for a, h in zip(across, here)]
    turned = [e + w for e, w in zip(along_x(here), wide)]
    return [
        along_z(t, open_end) + (x + (a + a)) for t, x, a in zip(turned, along_x(wide), across)
    ]


def each(count, chunk, step):
    whole = count // chunk

    def body(index, carry):
        step(index * chunk, chunk)
        return carry

    if whole == 1:
        step(0, chunk)
    else:
        lax.fori_loop(0, whole, body, 0)
    if count % chunk:
        step(whole * chunk, count % chunk)


def take(ref, row):
    return [ref[row, i] for i in range(ref.shape[1])]


def sweep_row(rows, source, inverse, kinetic, open_end=False):
    total = stencil(*rows, open_end)
    return [
        KEEP * u + v * (s + (kinetic / 6.0) * t)
        for u, s, v, t in zip(rows[1], source, inverse, total)
    ]


def sweep(start, source, inverse, target, kinetic, count, chunk, offsets, open_end=False):
    to, of, at = offsets

    def step(base, rows):
        held = [take(start, base + (of + r - 1)) for r in range(rows + 2)]
        for r in range(rows):
            row = base + (at + r)
            new = sweep_row(held[r : r + 3], take(source, row), take(inverse, row), kinetic, open_end)
            for i, plane in enumerate(new):
                target[base + (to + r), i] = plane

    each(count, chunk, step)


def pooling(rows, columns):
    return jnp.where(iota((rows, columns), 0) // 2 == iota((rows, columns), 1), 0.5, 0.0).astype(F32)


def spreading(rows, columns):
    return jnp.where(iota((rows, columns), 0) == iota((rows, columns), 1) // 2, 1.0, 0.0).astype(F32)


def times(value, matrix):
    return jnp.dot(value, matrix, precision=HIGHEST, preferred_element_type=F32)


def cubes(low, high):
    return [
        0.25 * ((low[2 * i] + low[2 * i + 1]) + (high[2 * i] + high[2 * i + 1]))
        for i in range(len(low) // 2)
    ]


def pack(residual, potential, out):
    for c in range(PZ):
        rows = slice(4 * c, 4 * c + 4)
        for orbital in range(PX):
            base = (orbital * PZ + c) * 48
            for i in range(8):
                out[base + 4 * i : base + 4 * i + 4] = residual[orbital, i, rows]
            for i in range(4):
                out[base + 32 + 4 * i : base + 36 + 4 * i] = potential[i, rows]


def down(shifts, own, mate, beside, own_half, mate_half, beside_half, fine_out, source_out, inverse_out, cut, field, potential, source, inverse, start):
    px, py, c = place()
    size_y = lax.axis_size("dom") // (PX * PZ)
    shift = shifts[px]

    band = lax.axis_index("band")

    def unpack(blocks, halves):
        for row in range(12):
            block, other_half = blocks[row // 4], halves[row // 4]
            for half in range(PZ):
                lanes = slice(128 * half, 128 * half + 128)
                for i in range(8):
                    at = 48 * half + 4 * i + row % 4
                    field[row, i, :, lanes] = block[pl.ds(at, PX, stride=96), :]
                if 1 <= row <= 10:
                    for i in range(4):
                        at = 48 * half + 32 + 4 * i + row % 4
                        potential[row - 1, 4 * band + i, :, lanes] = block[pl.ds(at, PX, stride=96), :]
                        at = 16 * half + 4 * i + row % 4
                        potential[row - 1, 4 * (1 - band) + i, :, lanes] = other_half[pl.ds(at, PX, stride=32), :]

    pl.when(c == 0)(lambda: unpack((beside, own, mate), (beside_half, own_half, mate_half)))
    pl.when(c == 1)(lambda: unpack((mate, own, beside), (mate_half, own_half, beside_half)))

    def first(base, rows):
        for r in range(rows):
            row = base + r
            y = py * 8 + 4 * c + row - 3
            inside = jnp.where((y >= 0) & (y < 8 * size_y), OMEGA, 0.0).astype(F32)
            below, here, above = [take(field, row + d) for d in range(3)]
            for i, (b, h, a, x) in enumerate(zip(below, here, above, along_x(here))):
                s = 0.5 * h + ((b + a) + (x + along_z(h, False))) * (1.0 / 12.0)
                v = inside / (potential[row, i] + (4.0 * FINE + shift))
                source[row, i] = s
                inverse[row, i] = v
                start[row, i] = v * s

    each(10, 2, first)
    sweep(start, source, inverse, fine_out, FINE, 8, 2, (0, 1, 1))

    def keep(base, rows):
        for r in range(rows):
            for i in range(8):
                source_out[base + r, i] = source[base + (r + 2), i]
                inverse_out[base + r, i] = inverse[base + (r + 2), i]

    each(6, 2, keep)
    pool = pooling(256, 128)
    for pair in range(2):
        left = []
        for row in (2 * pair, 2 * pair + 1):
            rows = [take(fine_out, row + d) for d in (1, 2, 3)]
            weight = [v + (4.0 * FINE + shift) for v in take(potential, row + 3)]
            total = stencil(*rows)
            left.append(
                [s + (FINE / 6.0) * t - w * u for s, t, w, u in zip(take(source, row + 3), total, weight, rows[1])]
            )
        mean = cubes(*left) + cubes(take(potential, 2 * pair + 3), take(potential, 2 * pair + 4))
        small = times(jnp.concatenate(mean, axis=0), pool)
        for i in range(8):
            cut[pair, i] = small[8 * i : 8 * i + 8]


def up(shifts, fine, source, inverse, block, around, out, weight1, source1, inverse1, middle, other, source2, inverse2, coarse, coarser, work):
    px, py, c = place()
    size_y = lax.axis_size("dom") // (PX * PZ)
    shift = shifts[px]

    def inside(distance):
        return jnp.where((py + distance >= 0) & (py + distance < size_y), OMEGA, 0.0).astype(F32)

    for row in range(28):
        distance = row // 4 - REACH
        if distance == 0:
            at = lambda i: block[row % 4, i]
        else:
            side, step = (0, -distance - 1) if distance < 0 else (1, distance - 1)
            at = lambda i: around[side, step, row % 4, i]
        for i in range(4):
            s = at(i)
            w = at(4 + i) + (4.0 * MIDDLE + shift)
            v = inside(distance) / w
            source1[row, i] = s
            weight1[row, i] = w
            inverse1[row, i] = v
            other[row, i] = v * s

    sweep(other, source1, inverse1, middle, MIDDLE, 26, 4, (1, 1, 1))

    pool = pooling(128, 128)
    spread = spreading(128, 128)
    lane = iota((8, 128), 1)

    def shrink(base, pairs):
        for pair in range(pairs):
            low = 2 * base + (2 * pair + 2)
            left, weights = [], []
            for row in (low, low + 1):
                rows = [take(middle, row + d) for d in (-1, 0, 1)]
                w = take(weight1, row)
                total = stencil(*rows)
                left.append(
                    [s + (MIDDLE / 6.0) * t - x * u for s, t, x, u in zip(take(source1, row), total, w, rows[1])]
                )
                weights.append(w)
            mean = cubes(*left) + cubes(*weights)
            small = times(jnp.concatenate(mean, axis=0), pool)
            distance = (base + (pair + 1)) // 2 - REACH
            for i in range(2):
                s = small[8 * i : 8 * i + 8]
                w = small[16 + 8 * i : 24 + 8 * i] + (4.0 * COARSE - 4.0 * MIDDLE)
                v = jnp.where(lane < 64, inside(distance) / jnp.where(lane < 64, w, 1.0), 0.0)
                source2[base + pair, i] = s
                inverse2[base + pair, i] = v
                coarse[base + pair, i] = v * s

    each(12, 4, shrink)
    sweep(coarse, source2, inverse2, coarser, COARSE, 10, 10, (1, 1, 1), True)
    sweep(coarser, source2, inverse2, coarse, COARSE, 8, 8, (2, 2, 2), True)
    sweep(coarse, source2, inverse2, coarser, COARSE, 6, 6, (3, 3, 3), True)

    for row in range(3, 9):
        wide = times(jnp.concatenate(take(coarser, row), axis=0), spread)
        for fine_row in (2 * row + 2, 2 * row + 3):
            for i in range(4):
                other[fine_row, i] = middle[fine_row, i] + wide[8 * (i // 2) : 8 * (i // 2) + 8]

    sweep(other, source1, inverse1, middle, MIDDLE, 8, 4, (10, 10, 10))
    sweep(middle, source1, inverse1, other, MIDDLE, 6, 6, (11, 11, 11))

    spread = spreading(128, 256)
    for row in range(4):
        wide = times(jnp.concatenate(take(other, 11 + 2 * c + row), axis=0), spread)
        for fine_row in (2 * row, 2 * row + 1):
            for i in range(8):
                work[fine_row, i] = fine[fine_row, i] + wide[8 * (i // 2) : 8 * (i // 2) + 8]

    final = work.at[8:14]
    sweep(work, source, inverse, final, FINE, 6, 2, (0, 1, 0))
    for row in range(4):
        new = sweep_row(
            [take(final, row + d) for d in range(3)], take(source, row + 1), take(inverse, row + 1), FINE
        )
        for i, plane in enumerate(new):
            at = (i // 2) * 8 + (i % 2) * 4 + row
            for half in range(PZ):
                out[pl.ds(half * 32 + at, PX, stride=64), :] = plane[:, 128 * half : 128 * half + 128]


def unpack(blocks, out):
    for orbital in range(PX):
        for c in range(PZ):
            for i in range(8):
                base = (orbital * PZ + c) * 32 + (i // 2) * 8 + (i % 2) * 4
                out[orbital, i, 4 * c : 4 * c + 4] = blocks[base : base + 4]


def call(kernel, outs, scratch=(), smem=False):
    shapes = [jax.ShapeDtypeStruct(shape, F32) for shape in outs]
    specs = [pl.BlockSpec(memory_space=pltpu.VMEM)] * len(outs)

    def run(*args):
        given = [pl.BlockSpec(memory_space=pltpu.VMEM)] * len(args)
        if smem:
            given[0] = pl.BlockSpec(memory_space=pltpu.SMEM)
        return pl.pallas_call(
            kernel,
            out_shape=shapes,
            in_specs=given,
            out_specs=specs,
            scratch_shapes=[pltpu.VMEM(shape, F32) for shape in scratch],
            compiler_params=pltpu.CompilerParams(vmem_limit_bytes=40 * 1024 * 1024),
        )(*args)

    return run


def body(residual, potential, shifts):
    size_y = lax.axis_size("dom") // (PX * PZ)
    blocks = [(px, py, c) for px in range(PX) for py in range(size_y) for c in range(PZ)]
    lines = [
        [dom_of(px, py, c, size_y) for px in range(PX) for c in range(PZ)] for py in range(size_y)
    ]
    cores = [
        [dom_of(px, py, c, size_y) for c in range(PZ)] for px in range(PX) for py in range(size_y)
    ]

    def pairs(target, bands=False):
        found = [((px, py, c), target(px, py, c)) for px, py, c in blocks]
        found = [(dom_of(*a, size_y), dom_of(*b, size_y)) for a, b in found if 0 <= b[1] < size_y]
        return [(2 * a + n, 2 * b + 1 - n) for a, b in found for n in range(2)] if bands else found

    def swap_lines(value):
        return lax.all_to_all(value, "dom", 0, 0, axis_index_groups=lines, tiled=True)

    def to_beside(px, py, c):
        return (px, py - 1, 1) if c == 0 else (px, py + 1, 0)

    def to_mate(px, py, c):
        return (px, py, 1 - c)

    (packed,) = call(pack, [(768, 128)])(residual, potential)
    own = swap_lines(packed)
    half = own.reshape(16, 48, 128)[:, 32:].reshape(256, 128)
    both = ("dom", "band")
    beside = lax.ppermute(own, "dom", pairs(to_beside))
    beside_half = lax.ppermute(half, both, pairs(to_beside, True))
    mate = lax.ppermute(own, "dom", pairs(to_mate))
    own_half = lax.ppermute(half, "band", [(0, 1), (1, 0)])
    mate_half = lax.ppermute(half, both, pairs(to_mate, True))
    fine, source, inverse, cut = call(
        down,
        [(8, 8, 8, 256), (6, 8, 8, 256), (6, 8, 8, 256), (2, 8, 8, 128)],
        [(12, 8, 8, 256)] + [(10, 8, 8, 256)] * 4,
        smem=True,
    )(shifts, own, mate, beside, own_half, mate_half, beside_half)
    block = lax.all_gather(cut, "dom", axis_index_groups=cores, axis=0, tiled=True)
    sent = [
        lax.ppermute(
            block,
            "dom",
            pairs(lambda px, py, c, k=k: (px, py + k, 0) if c == 0 else (px, py - k, 1)),
        )
        for k in range(1, REACH + 1)
    ]
    around = lax.all_gather(jnp.stack(sent), "dom", axis_index_groups=cores, axis=0)
    (final,) = call(
        up,
        [(512, 128)],
        [(28, 4, 8, 128)] * 5 + [(12, 2, 8, 128)] * 4 + [(14, 8, 8, 256)],
        smem=True,
    )(shifts, fine, source, inverse, block, around)
    (correction,) = call(unpack, [(8, 8, 8, 128)])(swap_lines(final))
    return correction


def solution(mesh):
    return jax.shard_map(
        body,
        mesh=mesh,
        in_specs=(P("band", "dom", None, None), P(("dom", "band"), None, None), P("band")),
        out_specs=P("band", "dom", None, None),
        check_vma=False,
    )
```

```python
import jax
import jax.numpy as jnp
from jax import lax
from jax.experimental import pallas as pl
from jax.experimental.pallas import tpu as pltpu
from jax.sharding import PartitionSpec as P


OMEGA = 0.7
KEEP = 0.3
FINE, MIDDLE, COARSE = 2.0, 0.5, 0.125
PX, PZ = 8, 2
REACH = 3
F32 = jnp.float32
HIGHEST = lax.Precision.HIGHEST


def place():
    position = lax.axis_index("dom")
    size_y = lax.axis_size("dom") // (PX * PZ)
    return position // (size_y * PZ), position // PZ % size_y, position % PZ


def dom_of(px, py, pz, size_y):
    return (px * size_y + py) * PZ + pz


def iota(shape, dimension):
    return lax.broadcasted_iota(jnp.int32, shape, dimension)


def along_x(planes):
    sublane = iota(planes[0].shape, 0)
    first = jnp.where(sublane == 0, 0.0, pltpu.roll(planes[-1], 1, 0))
    last = jnp.where(sublane == PX - 1, 0.0, pltpu.roll(planes[0], PX - 1, 0))
    below = [first] + planes[:-1]
    above = planes[1:] + [last]
    return [b + a for b, a in zip(below, above)]


def along_z(plane, open_end):
    width = plane.shape[1]
    left, right = pltpu.roll(plane, 1, 1), pltpu.roll(plane, width - 1, 1)
    if not open_end:
        lane = iota(plane.shape, 1)
        left = jnp.where(lane == 0, 0.0, left)
        right = jnp.where(lane == width - 1, 0.0, right)
    return left + right


def stencil(below, here, above, open_end=False):
    across = [a + b for a, b in zip(below, above)]
    wide = [a + (h + h) for a, h in zip(across, here)]
    turned = [e + w for e, w in zip(along_x(here), wide)]
    return [
        along_z(t, open_end) + (x + (a + a)) for t, x, a in zip(turned, along_x(wide), across)
    ]


def each(count, chunk, step):
    whole = count // chunk

    def body(index, carry):
        step(index * chunk, chunk)
        return carry

    if whole == 1:
        step(0, chunk)
    else:
        lax.fori_loop(0, whole, body, 0)
    if count % chunk:
        step(whole * chunk, count % chunk)


def take(ref, row):
    return [ref[row, i] for i in range(ref.shape[1])]


def sweep_row(rows, source, inverse, kinetic, open_end=False):
    total = stencil(*rows, open_end)
    return [
        KEEP * u + v * (s + (kinetic / 6.0) * t)
        for u, s, v, t in zip(rows[1], source, inverse, total)
    ]


def sweep(start, source, inverse, target, kinetic, count, chunk, offsets, open_end=False):
    to, of, at = offsets

    def step(base, rows):
        held = [take(start, base + (of + r - 1)) for r in range(rows + 2)]
        for r in range(rows):
            row = base + (at + r)
            new = sweep_row(held[r : r + 3], take(source, row), take(inverse, row), kinetic, open_end)
            for i, plane in enumerate(new):
                target[base + (to + r), i] = plane

    each(count, chunk, step)


def pooling(rows, columns):
    return jnp.where(iota((rows, columns), 0) // 2 == iota((rows, columns), 1), 0.5, 0.0).astype(F32)


def spreading(rows, columns):
    return jnp.where(iota((rows, columns), 0) == iota((rows, columns), 1) // 2, 1.0, 0.0).astype(F32)


def times(value, matrix):
    return jnp.dot(value, matrix, precision=HIGHEST, preferred_element_type=F32)


def cubes(low, high):
    return [
        0.25 * ((low[2 * i] + low[2 * i + 1]) + (high[2 * i] + high[2 * i + 1]))
        for i in range(len(low) // 2)
    ]


def pack(residual, potential, out):
    for c in range(PZ):
        rows = slice(4 * c, 4 * c + 4)
        for orbital in range(PX):
            base = (orbital * PZ + c) * 48
            for i in range(8):
                out[base + 4 * i : base + 4 * i + 4] = residual[orbital, i, rows]
            for i in range(4):
                out[base + 32 + 4 * i : base + 36 + 4 * i] = potential[i, rows]


def down(shifts, cores, beside, cores_half, beside_half, fine_out, source_out, inverse_out, cut, field, potential, source, inverse, start):
    px, py, c = place()
    size_y = lax.axis_size("dom") // (PX * PZ)
    shift = shifts[px]

    band = lax.axis_index("band")

    def unpack(blocks, halves):
        for row in range(12):
            block, other_half = blocks[row // 4], halves[row // 4]
            for half in range(PZ):
                lanes = slice(128 * half, 128 * half + 128)
                for i in range(8):
                    at = 48 * half + 4 * i + row % 4
                    field[row, i, :, lanes] = block[pl.ds(at, PX, stride=96), :]
                if 1 <= row <= 10:
                    for i in range(4):
                        at = 48 * half + 32 + 4 * i + row % 4
                        potential[row - 1, 4 * band + i, :, lanes] = block[pl.ds(at, PX, stride=96), :]
                        at = 16 * half + 4 * i + row % 4
                        potential[row - 1, 4 * (1 - band) + i, :, lanes] = other_half[pl.ds(at, PX, stride=32), :]

    here = (cores.at[0], cores.at[1])
    here_half = (cores_half.at[0], cores_half.at[1])
    pl.when(c == 0)(lambda: unpack((beside, *here), (beside_half, *here_half)))
    pl.when(c == 1)(lambda: unpack((*here, beside), (*here_half, beside_half)))

    def first(base, rows):
        for r in range(rows):
            row = base + r
            y = py * 8 + 4 * c + row - 3
            inside = jnp.where((y >= 0) & (y < 8 * size_y), OMEGA, 0.0).astype(F32)
            below, here, above = [take(field, row + d) for d in range(3)]
            for i, (b, h, a, x) in enumerate(zip(below, here, above, along_x(here))):
                s = 0.5 * h + ((b + a) + (x + along_z(h, False))) * (1.0 / 12.0)
                v = inside / (potential[row, i] + (4.0 * FINE + shift))
                source[row, i] = s
                inverse[row, i] = v
                start[row, i] = v * s

    each(10, 2, first)
    sweep(start, source, inverse, fine_out, FINE, 8, 2, (0, 1, 1))

    def keep(base, rows):
        for r in range(rows):
            for i in range(8):
                source_out[base + r, i] = source[base + (r + 2), i]
                inverse_out[base + r, i] = inverse[base + (r + 2), i]

    each(6, 2, keep)
    pool = pooling(256, 128)
    for pair in range(2):
        left = []
        for row in (2 * pair, 2 * pair + 1):
            rows = [take(fine_out, row + d) for d in (1, 2, 3)]
            weight = [v + (4.0 * FINE + shift) for v in take(potential, row + 3)]
            total = stencil(*rows)
            left.append(
                [s + (FINE / 6.0) * t - w * u for s, t, w, u in zip(take(source, row + 3), total, weight, rows[1])]
            )
        mean = cubes(*left) + cubes(take(potential, 2 * pair + 3), take(potential, 2 * pair + 4))
        small = times(jnp.concatenate(mean, axis=0), pool)
        for i in range(8):
            cut[pair, i] = small[8 * i : 8 * i + 8]


def up(shifts, fine, source, inverse, block, around, out, weight1, source1, inverse1, middle, other, source2, inverse2, coarse, coarser, work):
    px, py, c = place()
    size_y = lax.axis_size("dom") // (PX * PZ)
    shift = shifts[px]

    def inside(distance):
        return jnp.where((py + distance >= 0) & (py + distance < size_y), OMEGA, 0.0).astype(F32)

    for row in range(28):
        distance = row // 4 - REACH
        if distance == 0:
            at = lambda i: block[row % 4, i]
        else:
            side, step = (0, -distance - 1) if distance < 0 else (1, distance - 1)
            at = lambda i: around[side, step, row % 4, i]
        for i in range(4):
            s = at(i)
            w = at(4 + i) + (4.0 * MIDDLE + shift)
            v = inside(distance) / w
            source1[row, i] = s
            weight1[row, i] = w
            inverse1[row, i] = v
            other[row, i] = v * s

    sweep(other, source1, inverse1, middle, MIDDLE, 26, 4, (1, 1, 1))

    pool = pooling(128, 128)
    spread = spreading(128, 128)
    lane = iota((8, 128), 1)

    def shrink(base, pairs):
        for pair in range(pairs):
            low = 2 * base + (2 * pair + 2)
            left, weights = [], []
            for row in (low, low + 1):
                rows = [take(middle, row + d) for d in (-1, 0, 1)]
                w = take(weight1, row)
                total = stencil(*rows)
                left.append(
                    [s + (MIDDLE / 6.0) * t - x * u for s, t, x, u in zip(take(source1, row), total, w, rows[1])]
                )
                weights.append(w)
            mean = cubes(*left) + cubes(*weights)
            small = times(jnp.concatenate(mean, axis=0), pool)
            distance = (base + (pair + 1)) // 2 - REACH
            for i in range(2):
                s = small[8 * i : 8 * i + 8]
                w = small[16 + 8 * i : 24 + 8 * i] + (4.0 * COARSE - 4.0 * MIDDLE)
                v = jnp.where(lane < 64, inside(distance) / jnp.where(lane < 64, w, 1.0), 0.0)
                source2[base + pair, i] = s
                inverse2[base + pair, i] = v
                coarse[base + pair, i] = v * s

    each(12, 4, shrink)
    sweep(coarse, source2, inverse2, coarser, COARSE, 10, 10, (1, 1, 1), True)
    sweep(coarser, source2, inverse2, coarse, COARSE, 8, 8, (2, 2, 2), True)
    sweep(coarse, source2, inverse2, coarser, COARSE, 6, 6, (3, 3, 3), True)

    for row in range(3, 9):
        wide = times(jnp.concatenate(take(coarser, row), axis=0), spread)
        for fine_row in (2 * row + 2, 2 * row + 3):
            for i in range(4):
                other[fine_row, i] = middle[fine_row, i] + wide[8 * (i // 2) : 8 * (i // 2) + 8]

    sweep(other, source1, inverse1, middle, MIDDLE, 8, 4, (10, 10, 10))
    sweep(middle, source1, inverse1, other, MIDDLE, 6, 6, (11, 11, 11))

    spread = spreading(128, 256)
    for row in range(4):
        wide = times(jnp.concatenate(take(other, 11 + 2 * c + row), axis=0), spread)
        for fine_row in (2 * row, 2 * row + 1):
            for i in range(8):
                work[fine_row, i] = fine[fine_row, i] + wide[8 * (i // 2) : 8 * (i // 2) + 8]

    final = work.at[8:14]
    sweep(work, source, inverse, final, FINE, 6, 2, (0, 1, 0))
    for row in range(4):
        new = sweep_row(
            [take(final, row + d) for d in range(3)], take(source, row + 1), take(inverse, row + 1), FINE
        )
        for i, plane in enumerate(new):
            at = (i // 2) * 8 + (i % 2) * 4 + row
            for half in range(PZ):
                out[pl.ds(half * 32 + at, PX, stride=64), :] = plane[:, 128 * half : 128 * half + 128]


def unpack(blocks, out):
    for orbital in range(PX):
        for c in range(PZ):
            for i in range(8):
                base = (orbital * PZ + c) * 32 + (i // 2) * 8 + (i % 2) * 4
                out[orbital, i, 4 * c : 4 * c + 4] = blocks[base : base + 4]


def call(kernel, outs, scratch=(), smem=False):
    shapes = [jax.ShapeDtypeStruct(shape, F32) for shape in outs]
    specs = [pl.BlockSpec(memory_space=pltpu.VMEM)] * len(outs)

    def run(*args):
        given = [pl.BlockSpec(memory_space=pltpu.VMEM)] * len(args)
        if smem:
            given[0] = pl.BlockSpec(memory_space=pltpu.SMEM)
        return pl.pallas_call(
            kernel,
            out_shape=shapes,
            in_specs=given,
            out_specs=specs,
            scratch_shapes=[pltpu.VMEM(shape, F32) for shape in scratch],
            compiler_params=pltpu.CompilerParams(vmem_limit_bytes=40 * 1024 * 1024),
        )(*args)

    return run


def body(residual, potential, shifts):
    size_y = lax.axis_size("dom") // (PX * PZ)
    blocks = [(px, py, c) for px in range(PX) for py in range(size_y) for c in range(PZ)]
    lines = [
        [dom_of(px, py, c, size_y) for px in range(PX) for c in range(PZ)] for py in range(size_y)
    ]
    cores = [
        [dom_of(px, py, c, size_y) for c in range(PZ)] for px in range(PX) for py in range(size_y)
    ]

    def pairs(target, bands=False):
        found = [((px, py, c), target(px, py, c)) for px, py, c in blocks]
        found = [(dom_of(*a, size_y), dom_of(*b, size_y)) for a, b in found if 0 <= b[1] < size_y]
        return [(2 * a + n, 2 * b + 1 - n) for a, b in found for n in range(2)] if bands else found

    def swap_lines(value):
        return lax.all_to_all(value, "dom", 0, 0, axis_index_groups=lines, tiled=True)

    def to_beside(px, py, c):
        return (px, py - 1, 1) if c == 0 else (px, py + 1, 0)

    (packed,) = call(pack, [(768, 128)])(residual, potential)
    own = swap_lines(packed)
    half = own.reshape(16, 48, 128)[:, 32:].reshape(256, 128)
    both = ("dom", "band")
    own_half = lax.ppermute(half, "band", [(0, 1), (1, 0)])
    beside = lax.ppermute(own, "dom", pairs(to_beside))
    beside_half = lax.ppermute(half, both, pairs(to_beside, True))
    of_cores = lax.all_gather(own, "dom", axis_index_groups=cores, axis=0)
    of_cores_half = lax.all_gather(own_half, "dom", axis_index_groups=cores, axis=0)
    fine, source, inverse, cut = call(
        down,
        [(8, 8, 8, 256), (6, 8, 8, 256), (6, 8, 8, 256), (2, 8, 8, 128)],
        [(12, 8, 8, 256)] + [(10, 8, 8, 256)] * 4,
        smem=True,
    )(shifts, of_cores, beside, of_cores_half, beside_half)
    block = lax.all_gather(cut, "dom", axis_index_groups=cores, axis=0, tiled=True)
    sent = [
        lax.ppermute(
            block,
            "dom",
            pairs(lambda px, py, c, k=k: (px, py + k, 0) if c == 0 else (px, py - k, 1)),
        )
        for k in range(1, REACH + 1)
    ]
    around = lax.all_gather(jnp.stack(sent), "dom", axis_index_groups=cores, axis=0)
    (final,) = call(
        up,
        [(512, 128)],
        [(28, 4, 8, 128)] * 5 + [(12, 2, 8, 128)] * 4 + [(14, 8, 8, 256)],
        smem=True,
    )(shifts, fine, source, inverse, block, around)
    (correction,) = call(unpack, [(8, 8, 8, 128)])(swap_lines(final))
    return correction


def solution(mesh):
    return jax.shard_map(
        body,
        mesh=mesh,
        in_specs=(P("band", "dom", None, None), P(("dom", "band"), None, None), P("band")),
        out_specs=P("band", "dom", None, None),
        check_vma=False,
    )
```

```python
import jax
import jax.numpy as jnp
from jax import lax
from jax.experimental import pallas as pl
from jax.experimental.pallas import tpu as pltpu
from jax.sharding import PartitionSpec as P


OMEGA = 0.7
KEEP = 0.3
FINE, MIDDLE, COARSE = 2.0, 0.5, 0.125
PX, PZ = 8, 2
REACH = 3
F32 = jnp.float32
HIGHEST = lax.Precision.HIGHEST


def place():
    position = lax.axis_index("dom")
    size_y = lax.axis_size("dom") // (PX * PZ)
    return position // (size_y * PZ), position // PZ % size_y, position % PZ


def dom_of(px, py, pz, size_y):
    return (px * size_y + py) * PZ + pz


def iota(shape, dimension):
    return lax.broadcasted_iota(jnp.int32, shape, dimension)


def along_x(planes):
    sublane = iota(planes[0].shape, 0)
    first = jnp.where(sublane == 0, 0.0, pltpu.roll(planes[-1], 1, 0))
    last = jnp.where(sublane == PX - 1, 0.0, pltpu.roll(planes[0], PX - 1, 0))
    below = [first] + planes[:-1]
    above = planes[1:] + [last]
    return [b + a for b, a in zip(below, above)]


def along_z(plane, open_end):
    width = plane.shape[1]
    left, right = pltpu.roll(plane, 1, 1), pltpu.roll(plane, width - 1, 1)
    if not open_end:
        lane = iota(plane.shape, 1)
        left = jnp.where(lane == 0, 0.0, left)
        right = jnp.where(lane == width - 1, 0.0, right)
    return left + right


def stencil(below, here, above, open_end=False):
    across = [a + b for a, b in zip(below, above)]
    wide = [a + (h + h) for a, h in zip(across, here)]
    turned = [e + w for e, w in zip(along_x(here), wide)]
    return [
        along_z(t, open_end) + (x + (a + a)) for t, x, a in zip(turned, along_x(wide), across)
    ]


def each(count, chunk, step):
    for base in range(0, count, chunk):
        step(base, min(chunk, count - base))


def take(ref, row):
    return [ref[row, i] for i in range(ref.shape[1])]


def sweep_row(rows, source, inverse, kinetic, open_end=False):
    total = stencil(*rows, open_end)
    return [
        KEEP * u + v * (s + (kinetic / 6.0) * t)
        for u, s, v, t in zip(rows[1], source, inverse, total)
    ]


def sweep(start, source, inverse, target, kinetic, count, chunk, offsets, open_end=False):
    to, of, at = offsets

    def step(base, rows):
        held = [take(start, base + (of + r - 1)) for r in range(rows + 2)]
        for r in range(rows):
            row = base + (at + r)
            new = sweep_row(held[r : r + 3], take(source, row), take(inverse, row), kinetic, open_end)
            for i, plane in enumerate(new):
                target[base + (to + r), i] = plane

    each(count, chunk, step)


def pooling(rows, columns):
    return jnp.where(iota((rows, columns), 0) // 2 == iota((rows, columns), 1), 0.5, 0.0).astype(F32)


def spreading(rows, columns):
    return jnp.where(iota((rows, columns), 0) == iota((rows, columns), 1) // 2, 1.0, 0.0).astype(F32)


def times(value, matrix):
    return jnp.dot(value, matrix, precision=HIGHEST, preferred_element_type=F32)


def cubes(low, high):
    return [
        0.25 * ((low[2 * i] + low[2 * i + 1]) + (high[2 * i] + high[2 * i + 1]))
        for i in range(len(low) // 2)
    ]


def pack(residual, potential, shifts, out, shift, held, planes, numbers, arrived):
    copies = [
        pltpu.make_async_copy(source, target, arrived.at[i])
        for i, (source, target) in enumerate([(residual, held), (potential, planes), (shifts, numbers)])
    ]
    for copy in copies:
        copy.start()
    for copy in copies:
        copy.wait()
    shift[...] = jnp.full((8, 128), numbers[place()[0]], F32)
    for c in range(PZ):
        rows = slice(4 * c, 4 * c + 4)
        for orbital in range(PX):
            base = (orbital * PZ + c) * 48
            for i in range(8):
                out[base + 4 * i : base + 4 * i + 4] = held[orbital, i, rows]
            for i in range(4):
                out[base + 32 + 4 * i : base + 36 + 4 * i] = planes[i, rows]


def down(shifts, cores, beside, cores_half, beside_half, fine_out, source, inverse, cut, field, potential, start):
    px, py, c = place()
    size_y = lax.axis_size("dom") // (PX * PZ)
    shift = jnp.concatenate([shifts[...]] * 2, axis=1)
    band = lax.axis_index("band")

    def unpack(blocks, halves):
        for row in range(12):
            block, other_half = blocks[row // 4], halves[row // 4]
            for half in range(PZ):
                lanes = slice(128 * half, 128 * half + 128)
                for i in range(8):
                    at = 48 * half + 4 * i + row % 4
                    field[row, i, :, lanes] = block[pl.ds(at, PX, stride=96), :]
                if 1 <= row <= 10:
                    for i in range(4):
                        at = 48 * half + 32 + 4 * i + row % 4
                        potential[row - 1, 4 * band + i, :, lanes] = block[pl.ds(at, PX, stride=96), :]
                        at = 16 * half + 4 * i + row % 4
                        potential[row - 1, 4 * (1 - band) + i, :, lanes] = other_half[pl.ds(at, PX, stride=32), :]

    here = (cores.at[0], cores.at[1])
    here_half = (cores_half.at[0], cores_half.at[1])
    pl.when(c == 0)(lambda: unpack((beside, *here), (beside_half, *here_half)))
    pl.when(c == 1)(lambda: unpack((*here, beside), (*here_half, beside_half)))

    def first(base, rows):
        for r in range(rows):
            row = base + r
            y = py * 8 + 4 * c + row - 3
            inside = jnp.where((y >= 0) & (y < 8 * size_y), OMEGA, 0.0).astype(F32)
            below, here, above = [take(field, row + d) for d in range(3)]
            for i, (b, h, a, x) in enumerate(zip(below, here, above, along_x(here))):
                s = 0.5 * h + ((b + a) + (x + along_z(h, False))) * (1.0 / 12.0)
                v = inside / (potential[row, i] + (4.0 * FINE + shift))
                source[row, i] = s
                inverse[row, i] = v
                start[row, i] = v * s

    each(10, 2, first)
    sweep(start, source, inverse, fine_out, FINE, 8, 2, (0, 1, 1))

    pool = pooling(256, 128)
    means = []
    for pair in range(2):
        left = []
        for row in (2 * pair, 2 * pair + 1):
            rows = [take(fine_out, row + d) for d in (1, 2, 3)]
            weight = [v + (4.0 * FINE + shift) for v in take(potential, row + 3)]
            total = stencil(*rows)
            left.append(
                [s + (FINE / 6.0) * t - w * u for s, t, w, u in zip(take(source, row + 3), total, weight, rows[1])]
            )
        means += cubes(*left) + cubes(take(potential, 2 * pair + 3), take(potential, 2 * pair + 4))
    small = times(jnp.concatenate(means, axis=0), pool)
    for pair in range(2):
        for i in range(8):
            cut[pair, i] = small[64 * pair + 8 * i : 64 * pair + 8 * i + 8]


def up(shifts, fine, source, inverse, block, around, out, weight1, source1, inverse1, middle, other, source2, inverse2, coarse, coarser, work):
    px, py, c = place()
    size_y = lax.axis_size("dom") // (PX * PZ)
    shift = shifts[...]

    def inside(distance):
        return jnp.where((py + distance >= 0) & (py + distance < size_y), OMEGA, 0.0).astype(F32)

    for row in range(28):
        distance = row // 4 - REACH
        if distance == 0:
            at = lambda i: block[row % 4, i]
        else:
            side, step = (0, -distance - 1) if distance < 0 else (1, distance - 1)
            at = lambda i: around[side, step, row % 4, i]
        for i in range(4):
            s = at(i)
            w = at(4 + i) + (4.0 * MIDDLE + shift)
            v = inside(distance) / w
            source1[row, i] = s
            weight1[row, i] = w
            inverse1[row, i] = v
            other[row, i] = v * s

    sweep(other, source1, inverse1, middle, MIDDLE, 26, 4, (1, 1, 1))

    pool = pooling(128, 128)
    spread = spreading(128, 128)
    lane = iota((8, 128), 1)

    means = []
    for pair in range(12):
        left, weights = [], []
        for row in (2 * pair + 2, 2 * pair + 3):
            rows = [take(middle, row + d) for d in (-1, 0, 1)]
            w = take(weight1, row)
            total = stencil(*rows)
            left.append(
                [s + (MIDDLE / 6.0) * t - x * u for s, t, x, u in zip(take(source1, row), total, w, rows[1])]
            )
            weights.append(w)
        means += cubes(*left) + cubes(*weights)
    small = times(jnp.concatenate(means, axis=0), pool)
    for pair in range(12):
        for i in range(2):
            s = small[32 * pair + 8 * i : 32 * pair + 8 * i + 8]
            w = small[32 * pair + 8 * i + 16 : 32 * pair + 8 * i + 24] + (4.0 * COARSE - 4.0 * MIDDLE)
            v = jnp.where(lane < 64, inside((pair + 1) // 2 - REACH) / jnp.where(lane < 64, w, 1.0), 0.0)
            source2[pair, i] = s
            inverse2[pair, i] = v
            coarse[pair, i] = v * s

    sweep(coarse, source2, inverse2, coarser, COARSE, 10, 10, (1, 1, 1), True)
    sweep(coarser, source2, inverse2, coarse, COARSE, 8, 8, (2, 2, 2), True)
    sweep(coarse, source2, inverse2, coarser, COARSE, 6, 6, (3, 3, 3), True)

    wide = times(jnp.concatenate([p for row in range(3, 9) for p in take(coarser, row)], axis=0), spread)
    for row in range(8, 20):
        for i in range(4):
            at = 16 * (row // 2 - 4) + 8 * (i // 2)
            other[row, i] = middle[row, i] + wide[at : at + 8]

    sweep(other, source1, inverse1, middle, MIDDLE, 8, 4, (10, 10, 10))
    sweep(middle, source1, inverse1, other, MIDDLE, 6, 6, (11, 11, 11))

    spread = spreading(128, 256)
    wide = times(jnp.concatenate([p for row in range(4) for p in take(other, 11 + 2 * c + row)], axis=0), spread)
    for row in range(8):
        for i in range(8):
            at = 32 * (row // 2) + 8 * (i // 2)
            work[row, i] = fine[row, i] + wide[at : at + 8]

    final = work.at[8:14]
    sweep(work, source, inverse, final, FINE, 6, 2, (0, 1, 2))
    for row in range(4):
        new = sweep_row(
            [take(final, row + d) for d in range(3)], take(source, row + 3), take(inverse, row + 3), FINE
        )
        for i, plane in enumerate(new):
            at = (i // 2) * 8 + (i % 2) * 4 + row
            for half in range(PZ):
                out[pl.ds(half * 32 + at, PX, stride=64), :] = plane[:, 128 * half : 128 * half + 128]


def unpack(blocks, out):
    for orbital in range(PX):
        for c in range(PZ):
            for i in range(8):
                base = (orbital * PZ + c) * 32 + (i // 2) * 8 + (i % 2) * 4
                out[orbital, i, 4 * c : 4 * c + 4] = blocks[base : base + 4]


def call(kernel, outs, scratch=(), anywhere=False, others=()):
    vmem = pl.BlockSpec(memory_space=pltpu.VMEM)

    def run(*args):
        return pl.pallas_call(
            kernel,
            out_shape=[jax.ShapeDtypeStruct(shape, F32) for shape in outs],
            in_specs=[pl.BlockSpec(memory_space=pl.ANY) if anywhere else vmem] * len(args),
            out_specs=[vmem] * len(outs),
            scratch_shapes=[pltpu.VMEM(shape, F32) for shape in scratch] + list(others),
            compiler_params=pltpu.CompilerParams(vmem_limit_bytes=40 * 1024 * 1024),
        )(*args)

    return run


def run_down(*args):
    return call(
        down,
        [(8, 8, 8, 256), (10, 8, 8, 256), (10, 8, 8, 256), (2, 8, 8, 128)],
        [(12, 8, 8, 256)] + [(10, 8, 8, 256)] * 2,
    )(*args)


def run_up(*args):
    return call(
        up,
        [(512, 128)],
        [(28, 4, 8, 128)] * 5 + [(12, 2, 8, 128)] * 4 + [(14, 8, 8, 256)],
    )(*args)[0]


def body(residual, potential, shifts):
    size_y = lax.axis_size("dom") // (PX * PZ)
    blocks = [(px, py, c) for px in range(PX) for py in range(size_y) for c in range(PZ)]
    lines = [
        [dom_of(px, py, c, size_y) for px in range(PX) for c in range(PZ)] for py in range(size_y)
    ]
    cores = [
        [dom_of(px, py, c, size_y) for c in range(PZ)] for px in range(PX) for py in range(size_y)
    ]

    def pairs(target, bands=False):
        found = [((px, py, c), target(px, py, c)) for px, py, c in blocks]
        found = [(dom_of(*a, size_y), dom_of(*b, size_y)) for a, b in found if 0 <= b[1] < size_y]
        return [(2 * a + n, 2 * b + 1 - n) for a, b in found for n in range(2)] if bands else found

    def swap_lines(value):
        return lax.all_to_all(value, "dom", 0, 0, axis_index_groups=lines, tiled=True)

    def to_beside(px, py, c):
        return (px, py - 1, 1) if c == 0 else (px, py + 1, 0)

    packed, shift = call(
        pack,
        [(768, 128), (8, 128)],
        [(8, 8, 8, 128), (4, 8, 128)],
        anywhere=True,
        others=[pltpu.SMEM((8,), F32), pltpu.SemaphoreType.DMA((3,))],
    )(residual, potential, shifts)
    own = swap_lines(packed)
    half = own.reshape(16, 48, 128)[:, 32:].reshape(256, 128)
    both = ("dom", "band")
    own_half = lax.ppermute(half, "band", [(0, 1), (1, 0)])
    beside = lax.ppermute(own, "dom", pairs(to_beside))
    beside_half = lax.ppermute(half, both, pairs(to_beside, True))
    of_cores = lax.all_gather(own, "dom", axis_index_groups=cores, axis=0)
    of_cores_half = lax.all_gather(own_half, "dom", axis_index_groups=cores, axis=0)
    fine, source, inverse, cut = run_down(shift, of_cores, beside, of_cores_half, beside_half)
    block = lax.all_gather(cut, "dom", axis_index_groups=cores, axis=0, tiled=True)
    sent = [
        lax.ppermute(
            block,
            "dom",
            pairs(lambda px, py, c, k=k: (px, py + k, 0) if c == 0 else (px, py - k, 1)),
        )
        for k in range(1, REACH + 1)
    ]
    around = lax.all_gather(jnp.stack(sent), "dom", axis_index_groups=cores, axis=0)
    final = run_up(shift, fine, source, inverse, block, around)
    (correction,) = call(unpack, [(8, 8, 8, 128)])(swap_lines(final))
    return correction


def solution(mesh):
    return jax.shard_map(
        body,
        mesh=mesh,
        in_specs=(P("band", "dom", None, None), P(("dom", "band"), None, None), P("band")),
        out_specs=P("band", "dom", None, None),
        check_vma=False,
    )
```

```python
import jax
import jax.numpy as jnp
from jax import lax
from jax.experimental import pallas as pl
from jax.experimental.pallas import tpu as pltpu
from jax.sharding import PartitionSpec as P


OMEGA = 0.7
KEEP = 0.3
FINE, MIDDLE, COARSE = 2.0, 0.5, 0.125
PX, PZ = 8, 2
REACH = 3
F32 = jnp.float32
HIGHEST = lax.Precision.HIGHEST


def place():
    position = lax.axis_index("dom")
    size_y = lax.axis_size("dom") // (PX * PZ)
    return position // (size_y * PZ), position // PZ % size_y, position % PZ


def dom_of(px, py, pz, size_y):
    return (px * size_y + py) * PZ + pz


def iota(shape, dimension):
    return lax.broadcasted_iota(jnp.int32, shape, dimension)


def along_x(planes):
    sublane = iota(planes[0].shape, 0)
    first = jnp.where(sublane == 0, 0.0, pltpu.roll(planes[-1], 1, 0))
    last = jnp.where(sublane == PX - 1, 0.0, pltpu.roll(planes[0], PX - 1, 0))
    below = [first] + planes[:-1]
    above = planes[1:] + [last]
    return [b + a for b, a in zip(below, above)]


def along_z(plane, open_end):
    width = plane.shape[1]
    left, right = pltpu.roll(plane, 1, 1), pltpu.roll(plane, width - 1, 1)
    if not open_end:
        lane = iota(plane.shape, 1)
        left = jnp.where(lane == 0, 0.0, left)
        right = jnp.where(lane == width - 1, 0.0, right)
    return left + right


def stencil(below, here, above, open_end=False):
    across = [a + b for a, b in zip(below, above)]
    wide = [a + (h + h) for a, h in zip(across, here)]
    turned = [e + w for e, w in zip(along_x(here), wide)]
    return [
        along_z(t, open_end) + (x + (a + a)) for t, x, a in zip(turned, along_x(wide), across)
    ]


def each(count, chunk, step):
    for base in range(0, count, chunk):
        step(base, min(chunk, count - base))


def take(ref, row):
    return [ref[row, i] for i in range(ref.shape[1])]


def sweep_row(rows, source, inverse, kinetic, open_end=False):
    total = stencil(*rows, open_end)
    return [
        KEEP * u + v * (s + (kinetic / 6.0) * t)
        for u, s, v, t in zip(rows[1], source, inverse, total)
    ]


def sweep(start, source, inverse, target, kinetic, count, chunk, offsets, open_end=False):
    to, of, at = offsets

    def step(base, rows):
        held = [take(start, base + (of + r - 1)) for r in range(rows + 2)]
        for r in range(rows):
            row = base + (at + r)
            new = sweep_row(held[r : r + 3], take(source, row), take(inverse, row), kinetic, open_end)
            for i, plane in enumerate(new):
                target[base + (to + r), i] = plane

    each(count, chunk, step)


def pooling(rows, columns):
    return jnp.where(iota((rows, columns), 0) // 2 == iota((rows, columns), 1), 0.5, 0.0).astype(F32)


def spreading(rows, columns):
    return jnp.where(iota((rows, columns), 0) == iota((rows, columns), 1) // 2, 1.0, 0.0).astype(F32)


def times(value, matrix):
    return jnp.dot(value, matrix, precision=HIGHEST, preferred_element_type=F32)


def cubes(low, high):
    return [
        0.25 * ((low[2 * i] + low[2 * i + 1]) + (high[2 * i] + high[2 * i + 1]))
        for i in range(len(low) // 2)
    ]


def pack(residual, potential, shifts, out, shift, held, planes, numbers, arrived):
    copies = [
        pltpu.make_async_copy(source, target, arrived.at[i])
        for i, (source, target) in enumerate([(residual, held), (potential, planes), (shifts, numbers)])
    ]
    for copy in copies:
        copy.start()
    for copy in copies:
        copy.wait()
    shift[...] = jnp.full((8, 128), numbers[place()[0]], F32)
    for c in range(PZ):
        rows = slice(4 * c, 4 * c + 4)
        for orbital in range(PX):
            base = (orbital * PZ + c) * 48
            for i in range(8):
                out[base + 4 * i : base + 4 * i + 4] = held[orbital, i, rows]
            for i in range(4):
                out[base + 32 + 4 * i : base + 36 + 4 * i] = planes[i, rows]


def down(shifts, cores, beside, cores_half, beside_half, fine_out, source, inverse, cut, field, potential, start):
    px, py, c = place()
    size_y = lax.axis_size("dom") // (PX * PZ)
    shift = jnp.concatenate([shifts[...]] * 2, axis=1)
    band = lax.axis_index("band")

    def unpack(blocks, halves):
        for row in range(12):
            block, other_half = blocks[row // 4], halves[row // 4]
            for half in range(PZ):
                lanes = slice(128 * half, 128 * half + 128)
                for i in range(8):
                    at = 48 * half + 4 * i + row % 4
                    field[row, i, :, lanes] = block[pl.ds(at, PX, stride=96), :]
                if 1 <= row <= 10:
                    for i in range(4):
                        at = 48 * half + 32 + 4 * i + row % 4
                        potential[row - 1, 4 * band + i, :, lanes] = block[pl.ds(at, PX, stride=96), :]
                        at = 16 * half + 4 * i + row % 4
                        potential[row - 1, 4 * (1 - band) + i, :, lanes] = other_half[pl.ds(at, PX, stride=32), :]

    here = (cores.at[0], cores.at[1])
    here_half = (cores_half.at[0], cores_half.at[1])
    pl.when(c == 0)(lambda: unpack((beside, *here), (beside_half, *here_half)))
    pl.when(c == 1)(lambda: unpack((*here, beside), (*here_half, beside_half)))

    def first(base, rows):
        for r in range(rows):
            row = base + r
            y = py * 8 + 4 * c + row - 3
            inside = jnp.where((y >= 0) & (y < 8 * size_y), OMEGA, 0.0).astype(F32)
            below, here, above = [take(field, row + d) for d in range(3)]
            for i, (b, h, a, x) in enumerate(zip(below, here, above, along_x(here))):
                s = 0.5 * h + ((b + a) + (x + along_z(h, False))) * (1.0 / 12.0)
                v = inside / (potential[row, i] + (4.0 * FINE + shift))
                source[row, i] = s
                inverse[row, i] = v
                start[row, i] = v * s

    each(10, 2, first)
    sweep(start, source, inverse, fine_out, FINE, 8, 2, (0, 1, 1))

    pool = pooling(256, 128)
    means = []
    for pair in range(2):
        left = []
        for row in (2 * pair, 2 * pair + 1):
            rows = [take(fine_out, row + d) for d in (1, 2, 3)]
            weight = [v + (4.0 * FINE + shift) for v in take(potential, row + 3)]
            total = stencil(*rows)
            left.append(
                [s + (FINE / 6.0) * t - w * u for s, t, w, u in zip(take(source, row + 3), total, weight, rows[1])]
            )
        means += cubes(*left) + cubes(take(potential, 2 * pair + 3), take(potential, 2 * pair + 4))
    small = times(jnp.concatenate(means, axis=0), pool)
    for pair in range(2):
        for i in range(8):
            cut[pair, i] = small[64 * pair + 8 * i : 64 * pair + 8 * i + 8]


def up(shifts, fine, source, inverse, block, around, out, weight1, source1, inverse1, middle, other, source2, inverse2, coarse, coarser, work):
    px, py, c = place()
    size_y = lax.axis_size("dom") // (PX * PZ)
    shift = shifts[...]

    def inside(distance):
        return jnp.where((py + distance >= 0) & (py + distance < size_y), OMEGA, 0.0).astype(F32)

    for row in range(28):
        distance = row // 4 - REACH
        if distance == 0:
            at = lambda i: block[row % 4, i]
        else:
            side, step = (0, -distance - 1) if distance < 0 else (1, distance - 1)
            at = lambda i: around[side, step, row % 4, i]
        for i in range(4):
            s = at(i)
            w = at(4 + i) + (4.0 * MIDDLE + shift)
            v = inside(distance) / w
            source1[row, i] = s
            weight1[row, i] = w
            inverse1[row, i] = v
            other[row, i] = v * s

    sweep(other, source1, inverse1, middle, MIDDLE, 26, 4, (1, 1, 1))

    pool = pooling(128, 128)
    spread = spreading(128, 128)
    lane = iota((8, 128), 1)

    means = []
    for pair in range(12):
        left, weights = [], []
        for row in (2 * pair + 2, 2 * pair + 3):
            rows = [take(middle, row + d) for d in (-1, 0, 1)]
            w = take(weight1, row)
            total = stencil(*rows)
            left.append(
                [s + (MIDDLE / 6.0) * t - x * u for s, t, x, u in zip(take(source1, row), total, w, rows[1])]
            )
            weights.append(w)
        means += cubes(*left) + cubes(*weights)
    small = times(jnp.concatenate(means, axis=0), pool)
    for pair in range(12):
        for i in range(2):
            s = small[32 * pair + 8 * i : 32 * pair + 8 * i + 8]
            w = small[32 * pair + 8 * i + 16 : 32 * pair + 8 * i + 24] + (4.0 * COARSE - 4.0 * MIDDLE)
            v = jnp.where(lane < 64, inside((pair + 1) // 2 - REACH) / jnp.where(lane < 64, w, 1.0), 0.0)
            source2[pair, i] = s
            inverse2[pair, i] = v
            coarse[pair, i] = v * s

    sweep(coarse, source2, inverse2, coarser, COARSE, 10, 10, (1, 1, 1), True)
    sweep(coarser, source2, inverse2, coarse, COARSE, 8, 8, (2, 2, 2), True)
    sweep(coarse, source2, inverse2, coarser, COARSE, 6, 6, (3, 3, 3), True)

    wide = times(jnp.concatenate([p for row in range(3, 9) for p in take(coarser, row)], axis=0), spread)
    for row in range(8, 20):
        for i in range(4):
            at = 16 * (row // 2 - 4) + 8 * (i // 2)
            other[row, i] = middle[row, i] + wide[at : at + 8]

    sweep(other, source1, inverse1, middle, MIDDLE, 8, 4, (10, 10, 10))
    sweep(middle, source1, inverse1, other, MIDDLE, 6, 6, (11, 11, 11))

    spread = spreading(128, 256)
    wide = times(jnp.concatenate([p for row in range(4) for p in take(other, 11 + 2 * c + row)], axis=0), spread)
    for row in range(8):
        for i in range(8):
            at = 32 * (row // 2) + 8 * (i // 2)
            work[row, i] = fine[row, i] + wide[at : at + 8]

    final = work.at[8:14]
    sweep(work, source, inverse, final, FINE, 6, 2, (0, 1, 2))
    for row in range(4):
        new = sweep_row(
            [take(final, row + d) for d in range(3)], take(source, row + 3), take(inverse, row + 3), FINE
        )
        for i, plane in enumerate(new):
            at = (i // 2) * 8 + (i % 2) * 4 + row
            for half in range(PZ):
                out[pl.ds(half * 32 + at, PX, stride=64), :] = plane[:, 128 * half : 128 * half + 128]


def unpack(blocks, out):
    for orbital in range(PX):
        for c in range(PZ):
            for i in range(8):
                base = (orbital * PZ + c) * 32 + (i // 2) * 8 + (i % 2) * 4
                out[orbital, i, 4 * c : 4 * c + 4] = blocks[base : base + 4]


def call(kernel, outs, scratch=(), anywhere=False, others=()):
    vmem = pl.BlockSpec(memory_space=pltpu.VMEM)

    def run(*args):
        return pl.pallas_call(
            kernel,
            out_shape=[jax.ShapeDtypeStruct(shape, F32) for shape in outs],
            in_specs=[pl.BlockSpec(memory_space=pltpu.HBM) if anywhere else vmem] * len(args),
            out_specs=[vmem] * len(outs),
            scratch_shapes=[pltpu.VMEM(shape, F32) for shape in scratch] + list(others),
            compiler_params=pltpu.CompilerParams(vmem_limit_bytes=(56 if anywhere else 40) * 1024 * 1024),
        )(*args)

    return run


def run_down(*args):
    return call(
        down,
        [(8, 8, 8, 256), (10, 8, 8, 256), (10, 8, 8, 256), (2, 8, 8, 128)],
        [(12, 8, 8, 256)] + [(10, 8, 8, 256)] * 2,
    )(*args)


def run_up(*args):
    return call(
        up,
        [(512, 128)],
        [(28, 4, 8, 128)] * 5 + [(12, 2, 8, 128)] * 4 + [(14, 8, 8, 256)],
    )(*args)[0]


def body(residual, potential, shifts):
    size_y = lax.axis_size("dom") // (PX * PZ)
    blocks = [(px, py, c) for px in range(PX) for py in range(size_y) for c in range(PZ)]
    lines = [
        [dom_of(px, py, c, size_y) for px in range(PX) for c in range(PZ)] for py in range(size_y)
    ]
    cores = [
        [dom_of(px, py, c, size_y) for c in range(PZ)] for px in range(PX) for py in range(size_y)
    ]

    def pairs(target):
        found = [((px, py, c), target(px, py, c)) for px, py, c in blocks]
        return [(dom_of(*a, size_y), dom_of(*b, size_y)) for a, b in found if 0 <= b[1] < size_y]

    def swap_lines(value):
        return lax.all_to_all(value, "dom", 0, 0, axis_index_groups=lines, tiled=True)

    def to_beside(px, py, c):
        return (px, py - 1, 1) if c == 0 else (px, py + 1, 0)

    packed, shift = call(
        pack,
        [(768, 128), (8, 128)],
        [(8, 8, 8, 128), (4, 8, 128)],
        anywhere=True,
        others=[pltpu.SMEM((8,), F32), pltpu.SemaphoreType.DMA((3,))],
    )(residual, potential, shifts)
    own = swap_lines(packed)
    half = own.reshape(16, 48, 128)[:, 32:].reshape(256, 128)
    beside = lax.ppermute(own, "dom", pairs(to_beside))
    own_half = lax.ppermute(half, "band", [(0, 1), (1, 0)])
    beside_half = lax.ppermute(own_half, "dom", pairs(to_beside))
    of_cores = lax.all_gather(own, "dom", axis_index_groups=cores, axis=0)
    of_cores_half = lax.all_gather(own_half, "dom", axis_index_groups=cores, axis=0)
    fine, source, inverse, cut = run_down(shift, of_cores, beside, of_cores_half, beside_half)
    block = lax.all_gather(cut, "dom", axis_index_groups=cores, axis=0, tiled=True)
    sent = [
        lax.ppermute(
            block,
            "dom",
            pairs(lambda px, py, c, k=k: (px, py + k, 0) if c == 0 else (px, py - k, 1)),
        )
        for k in range(REACH, 0, -1)
    ]
    around = lax.all_gather(jnp.stack(sent[::-1]), "dom", axis_index_groups=cores, axis=0)
    final = run_up(shift, fine, source, inverse, block, around)
    (correction,) = call(unpack, [(8, 8, 8, 128)])(swap_lines(final))
    return correction


def solution(mesh):
    return jax.shard_map(
        body,
        mesh=mesh,
        in_specs=(P("band", "dom", None, None), P(("dom", "band"), None, None), P("band")),
        out_specs=P("band", "dom", None, None),
        check_vma=False,
    )
```

```python
import jax
import jax.numpy as jnp
from jax import lax
from jax.experimental import pallas as pl
from jax.experimental.pallas import tpu as pltpu
from jax.sharding import PartitionSpec as P


OMEGA = 0.7
KEEP = 0.3
FINE, MIDDLE, COARSE = 2.0, 0.5, 0.125
PX, PZ = 8, 2
REACH = 3
F32 = jnp.float32
HIGHEST = lax.Precision.HIGHEST


def place():
    position = lax.axis_index("dom")
    size_y = lax.axis_size("dom") // (PX * PZ)
    return position // (size_y * PZ), position // PZ % size_y, position % PZ


def dom_of(px, py, pz, size_y):
    return (px * size_y + py) * PZ + pz


def iota(shape, dimension):
    return lax.broadcasted_iota(jnp.int32, shape, dimension)


def along_x(planes):
    sublane = iota(planes[0].shape, 0)
    first = jnp.where(sublane == 0, 0.0, pltpu.roll(planes[-1], 1, 0))
    last = jnp.where(sublane == PX - 1, 0.0, pltpu.roll(planes[0], PX - 1, 0))
    below = [first] + planes[:-1]
    above = planes[1:] + [last]
    return [b + a for b, a in zip(below, above)]


def along_z(plane, open_end):
    width = plane.shape[1]
    left, right = pltpu.roll(plane, 1, 1), pltpu.roll(plane, width - 1, 1)
    if not open_end:
        lane = iota(plane.shape, 1)
        left = jnp.where(lane == 0, 0.0, left)
        right = jnp.where(lane == width - 1, 0.0, right)
    return left + right


def stencil(below, here, above, open_end=False):
    across = [a + b for a, b in zip(below, above)]
    wide = [a + (h + h) for a, h in zip(across, here)]
    turned = [e + w for e, w in zip(along_x(here), wide)]
    return [
        along_z(t, open_end) + (x + (a + a)) for t, x, a in zip(turned, along_x(wide), across)
    ]


def each(count, chunk, step):
    for base in range(0, count, chunk):
        step(base, min(chunk, count - base))


def take(ref, row):
    return [ref[row, i] for i in range(ref.shape[1])]


def sweep_row(rows, source, inverse, kinetic, open_end=False):
    total = stencil(*rows, open_end)
    return [
        KEEP * u + v * (s + (kinetic / 6.0) * t)
        for u, s, v, t in zip(rows[1], source, inverse, total)
    ]


def sweep(start, source, inverse, target, kinetic, count, chunk, offsets, open_end=False):
    to, of, at = offsets

    def step(base, rows):
        held = [take(start, base + (of + r - 1)) for r in range(rows + 2)]
        for r in range(rows):
            row = base + (at + r)
            new = sweep_row(held[r : r + 3], take(source, row), take(inverse, row), kinetic, open_end)
            for i, plane in enumerate(new):
                target[base + (to + r), i] = plane

    each(count, chunk, step)


def pooling(rows, columns):
    return jnp.where(iota((rows, columns), 0) // 2 == iota((rows, columns), 1), 0.5, 0.0).astype(F32)


def spreading(rows, columns):
    return jnp.where(iota((rows, columns), 0) == iota((rows, columns), 1) // 2, 1.0, 0.0).astype(F32)


def times(value, matrix):
    return jnp.dot(value, matrix, precision=HIGHEST, preferred_element_type=F32)


def cubes(low, high):
    return [
        0.25 * ((low[2 * i] + low[2 * i + 1]) + (high[2 * i] + high[2 * i + 1]))
        for i in range(len(low) // 2)
    ]


def pack(residual, potential, shifts, out, shift, held, planes, numbers, arrived):
    copies = [
        pltpu.make_async_copy(potential, planes, arrived.at[PX]),
        pltpu.make_async_copy(shifts, numbers, arrived.at[PX + 1]),
    ]
    copies += [
        pltpu.make_async_copy(residual.at[i], held.at[i], arrived.at[i]) for i in range(PX)
    ]
    for copy in copies:
        copy.start()
    copies[0].wait()
    for c in range(PZ):
        for i in range(4):
            both = planes[i, 4 * c : 4 * c + 4]
            for orbital in range(PX):
                base = (orbital * PZ + c) * 48 + 32 + 4 * i
                out[base : base + 4] = both
    copies[1].wait()
    shift[...] = jnp.full((8, 128), numbers[place()[0]], F32)
    for orbital in range(PX):
        copies[2 + orbital].wait()
        for c in range(PZ):
            base = (orbital * PZ + c) * 48
            for i in range(8):
                out[base + 4 * i : base + 4 * i + 4] = held[orbital, i, 4 * c : 4 * c + 4]


def down(shifts, cores, beside, cores_half, beside_half, fine_out, source, inverse, cut, field, potential, start):
    px, py, c = place()
    size_y = lax.axis_size("dom") // (PX * PZ)
    shift = jnp.concatenate([shifts[...]] * 2, axis=1)
    band = lax.axis_index("band")

    def unpack(blocks, halves):
        for row in range(12):
            block, other_half = blocks[row // 4], halves[row // 4]
            for half in range(PZ):
                lanes = slice(128 * half, 128 * half + 128)
                for i in range(8):
                    at = 48 * half + 4 * i + row % 4
                    field[row, i, :, lanes] = block[pl.ds(at, PX, stride=96), :]
                if 1 <= row <= 10:
                    for i in range(4):
                        at = 48 * half + 32 + 4 * i + row % 4
                        potential[row - 1, 4 * band + i, :, lanes] = block[pl.ds(at, PX, stride=96), :]
                        at = 16 * half + 4 * i + row % 4
                        potential[row - 1, 4 * (1 - band) + i, :, lanes] = other_half[pl.ds(at, PX, stride=32), :]

    here = (cores.at[0], cores.at[1])
    here_half = (cores_half.at[0], cores_half.at[1])
    pl.when(c == 0)(lambda: unpack((beside, *here), (beside_half, *here_half)))
    pl.when(c == 1)(lambda: unpack((*here, beside), (*here_half, beside_half)))

    def first(base, rows):
        for r in range(rows):
            row = base + r
            y = py * 8 + 4 * c + row - 3
            inside = jnp.where((y >= 0) & (y < 8 * size_y), OMEGA, 0.0).astype(F32)
            below, here, above = [take(field, row + d) for d in range(3)]
            for i, (b, h, a, x) in enumerate(zip(below, here, above, along_x(here))):
                s = 0.5 * h + ((b + a) + (x + along_z(h, False))) * (1.0 / 12.0)
                v = inside / (potential[row, i] + (4.0 * FINE + shift))
                source[row, i] = s
                inverse[row, i] = v
                start[row, i] = v * s

    each(10, 2, first)
    sweep(start, source, inverse, fine_out, FINE, 8, 2, (0, 1, 1))

    pool = pooling(256, 128)
    means = []
    for pair in range(2):
        left = []
        for row in (2 * pair, 2 * pair + 1):
            rows = [take(fine_out, row + d) for d in (1, 2, 3)]
            weight = [v + (4.0 * FINE + shift) for v in take(potential, row + 3)]
            total = stencil(*rows)
            left.append(
                [s + (FINE / 6.0) * t - w * u for s, t, w, u in zip(take(source, row + 3), total, weight, rows[1])]
            )
        means += cubes(*left) + cubes(take(potential, 2 * pair + 3), take(potential, 2 * pair + 4))
    small = times(jnp.concatenate(means, axis=0), pool)
    for pair in range(2):
        for i in range(8):
            cut[pair, i] = small[64 * pair + 8 * i : 64 * pair + 8 * i + 8]


def up(shifts, fine, source, inverse, block, around, out, weight1, source1, inverse1, middle, other, source2, inverse2, coarse, coarser, work):
    px, py, c = place()
    size_y = lax.axis_size("dom") // (PX * PZ)
    shift = shifts[...]

    def inside(distance):
        return jnp.where((py + distance >= 0) & (py + distance < size_y), OMEGA, 0.0).astype(F32)

    for row in range(28):
        distance = row // 4 - REACH
        if distance == 0:
            at = lambda i: block[row % 4, i]
        else:
            side, step = (0, -distance - 1) if distance < 0 else (1, distance - 1)
            at = lambda i: around[side, step, row % 4, i]
        for i in range(4):
            s = at(i)
            w = at(4 + i) + (4.0 * MIDDLE + shift)
            v = inside(distance) / w
            source1[row, i] = s
            weight1[row, i] = w
            inverse1[row, i] = v
            other[row, i] = v * s

    sweep(other, source1, inverse1, middle, MIDDLE, 26, 4, (1, 1, 1))

    pool = pooling(128, 128)
    spread = spreading(128, 128)
    lane = iota((8, 128), 1)

    means = []
    for pair in range(12):
        left, weights = [], []
        for row in (2 * pair + 2, 2 * pair + 3):
            rows = [take(middle, row + d) for d in (-1, 0, 1)]
            w = take(weight1, row)
            total = stencil(*rows)
            left.append(
                [s + (MIDDLE / 6.0) * t - x * u for s, t, x, u in zip(take(source1, row), total, w, rows[1])]
            )
            weights.append(w)
        means += cubes(*left) + cubes(*weights)
    small = times(jnp.concatenate(means, axis=0), pool)
    for pair in range(12):
        for i in range(2):
            s = small[32 * pair + 8 * i : 32 * pair + 8 * i + 8]
            w = small[32 * pair + 8 * i + 16 : 32 * pair + 8 * i + 24] + (4.0 * COARSE - 4.0 * MIDDLE)
            v = jnp.where(lane < 64, inside((pair + 1) // 2 - REACH) / jnp.where(lane < 64, w, 1.0), 0.0)
            source2[pair, i] = s
            inverse2[pair, i] = v
            coarse[pair, i] = v * s

    sweep(coarse, source2, inverse2, coarser, COARSE, 10, 10, (1, 1, 1), True)
    sweep(coarser, source2, inverse2, coarse, COARSE, 8, 8, (2, 2, 2), True)
    sweep(coarse, source2, inverse2, coarser, COARSE, 6, 6, (3, 3, 3), True)

    wide = times(jnp.concatenate([p for row in range(3, 9) for p in take(coarser, row)], axis=0), spread)
    for row in range(8, 20):
        for i in range(4):
            at = 16 * (row // 2 - 4) + 8 * (i // 2)
            other[row, i] = middle[row, i] + wide[at : at + 8]

    sweep(other, source1, inverse1, middle, MIDDLE, 8, 4, (10, 10, 10))
    sweep(middle, source1, inverse1, other, MIDDLE, 6, 6, (11, 11, 11))

    spread = spreading(128, 256)
    wide = times(jnp.concatenate([p for row in range(4) for p in take(other, 11 + 2 * c + row)], axis=0), spread)
    for row in range(8):
        for i in range(8):
            at = 32 * (row // 2) + 8 * (i // 2)
            work[row, i] = fine[row, i] + wide[at : at + 8]

    final = work.at[8:14]
    sweep(work, source, inverse, final, FINE, 6, 2, (0, 1, 2))
    for row in range(4):
        new = sweep_row(
            [take(final, row + d) for d in range(3)], take(source, row + 3), take(inverse, row + 3), FINE
        )
        for i, plane in enumerate(new):
            at = (i // 2) * 8 + (i % 2) * 4 + row
            for half in range(PZ):
                out[pl.ds(half * 32 + at, PX, stride=64), :] = plane[:, 128 * half : 128 * half + 128]


def unpack(blocks, out):
    for orbital in range(PX):
        for c in range(PZ):
            for i in range(8):
                base = (orbital * PZ + c) * 32 + (i // 2) * 8 + (i % 2) * 4
                out[orbital, i, 4 * c : 4 * c + 4] = blocks[base : base + 4]


def call(kernel, outs, scratch=(), anywhere=False, others=()):
    vmem = pl.BlockSpec(memory_space=pltpu.VMEM)

    def run(*args):
        return pl.pallas_call(
            kernel,
            out_shape=[(pltpu.VMEM if anywhere else jax.ShapeDtypeStruct)(shape, F32) for shape in outs],
            in_specs=[pl.BlockSpec(memory_space=pl.ANY) if anywhere else vmem] * len(args),
            out_specs=[vmem] * len(outs),
            scratch_shapes=[pltpu.VMEM(shape, F32) for shape in scratch] + list(others),
            compiler_params=pltpu.CompilerParams(vmem_limit_bytes=40 * 1024 * 1024),
        )(*args)

    return run


def run_down(*args):
    return call(
        down,
        [(8, 8, 8, 256), (10, 8, 8, 256), (10, 8, 8, 256), (2, 8, 8, 128)],
        [(12, 8, 8, 256)] + [(10, 8, 8, 256)] * 2,
    )(*args)


def run_up(*args):
    return call(
        up,
        [(512, 128)],
        [(28, 4, 8, 128)] * 5 + [(12, 2, 8, 128)] * 4 + [(14, 8, 8, 256)],
    )(*args)[0]


def body(residual, potential, shifts):
    size_y = lax.axis_size("dom") // (PX * PZ)
    blocks = [(px, py, c) for px in range(PX) for py in range(size_y) for c in range(PZ)]
    lines = [
        [dom_of(px, py, c, size_y) for px in range(PX) for c in range(PZ)] for py in range(size_y)
    ]
    cores = [
        [dom_of(px, py, c, size_y) for c in range(PZ)] for px in range(PX) for py in range(size_y)
    ]

    def pairs(target, bands=False):
        found = [((px, py, c), target(px, py, c)) for px, py, c in blocks]
        found = [(dom_of(*a, size_y), dom_of(*b, size_y)) for a, b in found if 0 <= b[1] < size_y]
        return [(2 * a + n, 2 * b + 1 - n) for a, b in found for n in range(2)] if bands else found

    def swap_lines(value):
        return lax.all_to_all(value, "dom", 0, 0, axis_index_groups=lines, tiled=True)

    def to_beside(px, py, c):
        return (px, py - 1, 1) if c == 0 else (px, py + 1, 0)

    packed, shift = call(
        pack,
        [(768, 128), (8, 128)],
        [(8, 8, 8, 128), (4, 8, 128)],
        anywhere=True,
        others=[pltpu.SMEM((8,), F32), pltpu.SemaphoreType.DMA((PX + 2,))],
    )(*[pltpu.with_memory_space_constraint(x, pltpu.HBM) for x in (residual, potential, shifts)])
    own = swap_lines(packed)
    half = own.reshape(16, 48, 128)[:, 32:].reshape(256, 128)
    both = ("dom", "band")
    own_half = lax.ppermute(half, "band", [(0, 1), (1, 0)])
    beside = lax.ppermute(own, "dom", pairs(to_beside))
    beside_half = lax.ppermute(half, both, pairs(to_beside, True))
    of_cores = lax.all_gather(own, "dom", axis_index_groups=cores, axis=0)
    of_cores_half = lax.all_gather(own_half, "dom", axis_index_groups=cores, axis=0)
    fine, source, inverse, cut = run_down(shift, of_cores, beside, of_cores_half, beside_half)
    block = lax.all_gather(cut, "dom", axis_index_groups=cores, axis=0, tiled=True)
    sent = [
        lax.ppermute(
            block,
            "dom",
            pairs(lambda px, py, c, k=k: (px, py + k, 0) if c == 0 else (px, py - k, 1)),
        )
        for k in range(1, REACH + 1)
    ]
    around = lax.all_gather(jnp.stack(sent), "dom", axis_index_groups=cores, axis=0)
    final = run_up(shift, fine, source, inverse, block, around)
    (correction,) = call(unpack, [(8, 8, 8, 128)])(swap_lines(final))
    return correction


def solution(mesh):
    return jax.shard_map(
        body,
        mesh=mesh,
        in_specs=(P("band", "dom", None, None), P(("dom", "band"), None, None), P("band")),
        out_specs=P("band", "dom", None, None),
        check_vma=False,
    )
```

```python
import jax
import jax.numpy as jnp
from jax import lax
from jax.experimental import pallas as pl
from jax.experimental.pallas import tpu as pltpu
from jax.sharding import PartitionSpec as P


OMEGA = 0.7
KEEP = 0.3
FINE, MIDDLE, COARSE = 2.0, 0.5, 0.125
PX, PZ = 8, 2
REACH = 3
F32 = jnp.float32
HIGHEST = lax.Precision.HIGHEST


def place():
    position = lax.axis_index("dom")
    size_y = lax.axis_size("dom") // (PX * PZ)
    return position // (size_y * PZ), position // PZ % size_y, position % PZ


def dom_of(px, py, pz, size_y):
    return (px * size_y + py) * PZ + pz


def iota(shape, dimension):
    return lax.broadcasted_iota(jnp.int32, shape, dimension)


def along_x(planes):
    sublane = iota(planes[0].shape, 0)
    first = jnp.where(sublane == 0, 0.0, pltpu.roll(planes[-1], 1, 0))
    last = jnp.where(sublane == PX - 1, 0.0, pltpu.roll(planes[0], PX - 1, 0))
    below = [first] + planes[:-1]
    above = planes[1:] + [last]
    return [b + a for b, a in zip(below, above)]


def along_z(plane, open_end):
    width = plane.shape[1]
    left, right = pltpu.roll(plane, 1, 1), pltpu.roll(plane, width - 1, 1)
    if not open_end:
        lane = iota(plane.shape, 1)
        left = jnp.where(lane == 0, 0.0, left)
        right = jnp.where(lane == width - 1, 0.0, right)
    return left + right


def stencil(below, here, above, open_end=False):
    across = [a + b for a, b in zip(below, above)]
    wide = [a + (h + h) for a, h in zip(across, here)]
    turned = [e + w for e, w in zip(along_x(here), wide)]
    return [
        along_z(t, open_end) + (x + (a + a)) for t, x, a in zip(turned, along_x(wide), across)
    ]


def each(count, chunk, step):
    for base in range(0, count, chunk):
        step(base, min(chunk, count - base))


def take(ref, row):
    return [ref[row, i] for i in range(ref.shape[1])]


def sweep_row(rows, source, inverse, kinetic, open_end=False):
    total = stencil(*rows, open_end)
    return [
        KEEP * u + v * (s + (kinetic / 6.0) * t)
        for u, s, v, t in zip(rows[1], source, inverse, total)
    ]


def sweep(start, source, inverse, target, kinetic, count, chunk, offsets, open_end=False):
    to, of, at = offsets

    def step(base, rows):
        held = [take(start, base + (of + r - 1)) for r in range(rows + 2)]
        for r in range(rows):
            row = base + (at + r)
            new = sweep_row(held[r : r + 3], take(source, row), take(inverse, row), kinetic, open_end)
            for i, plane in enumerate(new):
                target[base + (to + r), i] = plane

    each(count, chunk, step)


def pooling(rows, columns):
    return jnp.where(iota((rows, columns), 0) // 2 == iota((rows, columns), 1), 0.5, 0.0).astype(F32)


def spreading(rows, columns):
    return jnp.where(iota((rows, columns), 0) == iota((rows, columns), 1) // 2, 1.0, 0.0).astype(F32)


def times(value, matrix):
    return jnp.dot(value, matrix, precision=HIGHEST, preferred_element_type=F32)


def cubes(low, high):
    return [
        0.25 * ((low[2 * i] + low[2 * i + 1]) + (high[2 * i] + high[2 * i + 1]))
        for i in range(len(low) // 2)
    ]


def pack(residual, potential, shifts, out, shift, held, planes, numbers, arrived):
    copies = [
        pltpu.make_async_copy(potential, planes, arrived.at[PX]),
        pltpu.make_async_copy(shifts, numbers, arrived.at[PX + 1]),
    ]
    copies += [
        pltpu.make_async_copy(residual.at[i], held.at[i], arrived.at[i]) for i in range(PX)
    ]
    for copy in copies:
        copy.start()
    copies[0].wait()
    for c in range(PZ):
        for i in range(4):
            both = planes[i, 4 * c : 4 * c + 4]
            for orbital in range(PX):
                base = (orbital * PZ + c) * 48 + 32 + 4 * i
                out[base : base + 4] = both
    copies[1].wait()
    shift[...] = jnp.full((8, 128), numbers[place()[0]], F32)
    for orbital in range(PX):
        copies[2 + orbital].wait()
        for c in range(PZ):
            base = (orbital * PZ + c) * 48
            for i in range(8):
                out[base + 4 * i : base + 4 * i + 4] = held[orbital, i, 4 * c : 4 * c + 4]


def cut_out(slab, out):
    for piece in range(16):
        out[16 * piece : 16 * piece + 16] = slab[48 * piece + 32 : 48 * piece + 48]


def cut_own(slabs, out):
    _, _, c = place()
    for piece in range(16):
        out[16 * piece : 16 * piece + 16] = slabs[c, 48 * piece + 32 : 48 * piece + 48]


def down(shifts, cores, beside, cores_half, beside_half, fine_out, source, inverse, cut, field, potential, start):
    px, py, c = place()
    size_y = lax.axis_size("dom") // (PX * PZ)
    shift = jnp.concatenate([shifts[...]] * 2, axis=1)
    band = lax.axis_index("band")

    def unpack(blocks, halves):
        for row in range(12):
            block, other_half = blocks[row // 4], halves[row // 4]
            for half in range(PZ):
                lanes = slice(128 * half, 128 * half + 128)
                for i in range(8):
                    at = 48 * half + 4 * i + row % 4
                    field[row, i, :, lanes] = block[pl.ds(at, PX, stride=96), :]
                if 1 <= row <= 10:
                    for i in range(4):
                        at = 48 * half + 32 + 4 * i + row % 4
                        potential[row - 1, 4 * band + i, :, lanes] = block[pl.ds(at, PX, stride=96), :]
                        at = 16 * half + 4 * i + row % 4
                        potential[row - 1, 4 * (1 - band) + i, :, lanes] = other_half[pl.ds(at, PX, stride=32), :]

    here = (cores.at[0], cores.at[1])
    here_half = (cores_half.at[0], cores_half.at[1])
    pl.when(c == 0)(lambda: unpack((beside, *here), (beside_half, *here_half)))
    pl.when(c == 1)(lambda: unpack((*here, beside), (*here_half, beside_half)))

    def first(base, rows):
        for r in range(rows):
            row = base + r
            y = py * 8 + 4 * c + row - 3
            inside = jnp.where((y >= 0) & (y < 8 * size_y), OMEGA, 0.0).astype(F32)
            below, here, above = [take(field, row + d) for d in range(3)]
            for i, (b, h, a, x) in enumerate(zip(below, here, above, along_x(here))):
                s = 0.5 * h + ((b + a) + (x + along_z(h, False))) * (1.0 / 12.0)
                v = inside / (potential[row, i] + (4.0 * FINE + shift))
                source[row, i] = s
                inverse[row, i] = v
                start[row, i] = v * s

    each(10, 2, first)
    sweep(start, source, inverse, fine_out, FINE, 8, 2, (0, 1, 1))

    pool = pooling(256, 128)
    means = []
    for pair in range(2):
        left = []
        for row in (2 * pair, 2 * pair + 1):
            rows = [take(fine_out, row + d) for d in (1, 2, 3)]
            weight = [v + (4.0 * FINE + shift) for v in take(potential, row + 3)]
            total = stencil(*rows)
            left.append(
                [s + (FINE / 6.0) * t - w * u for s, t, w, u in zip(take(source, row + 3), total, weight, rows[1])]
            )
        means += cubes(*left) + cubes(take(potential, 2 * pair + 3), take(potential, 2 * pair + 4))
    small = times(jnp.concatenate(means, axis=0), pool)
    for pair in range(2):
        for i in range(8):
            cut[pair, i] = small[64 * pair + 8 * i : 64 * pair + 8 * i + 8]


def up(shifts, fine, source, inverse, block, around, out, weight1, source1, inverse1, middle, other, source2, inverse2, coarse, coarser, work):
    px, py, c = place()
    size_y = lax.axis_size("dom") // (PX * PZ)
    shift = shifts[...]

    def inside(distance):
        return jnp.where((py + distance >= 0) & (py + distance < size_y), OMEGA, 0.0).astype(F32)

    for row in range(28):
        distance = row // 4 - REACH
        if distance == 0:
            at = lambda i: block[row % 4, i]
        else:
            side, step = (0, -distance - 1) if distance < 0 else (1, distance - 1)
            at = lambda i: around[side, step, row % 4, i]
        for i in range(4):
            s = at(i)
            w = at(4 + i) + (4.0 * MIDDLE + shift)
            v = inside(distance) / w
            source1[row, i] = s
            weight1[row, i] = w
            inverse1[row, i] = v
            other[row, i] = v * s

    sweep(other, source1, inverse1, middle, MIDDLE, 26, 4, (1, 1, 1))

    pool = pooling(128, 128)
    spread = spreading(128, 128)
    lane = iota((8, 128), 1)

    means = []
    for pair in range(12):
        left, weights = [], []
        for row in (2 * pair + 2, 2 * pair + 3):
            rows = [take(middle, row + d) for d in (-1, 0, 1)]
            w = take(weight1, row)
            total = stencil(*rows)
            left.append(
                [s + (MIDDLE / 6.0) * t - x * u for s, t, x, u in zip(take(source1, row), total, w, rows[1])]
            )
            weights.append(w)
        means += cubes(*left) + cubes(*weights)
    small = times(jnp.concatenate(means, axis=0), pool)
    for pair in range(12):
        for i in range(2):
            s = small[32 * pair + 8 * i : 32 * pair + 8 * i + 8]
            w = small[32 * pair + 8 * i + 16 : 32 * pair + 8 * i + 24] + (4.0 * COARSE - 4.0 * MIDDLE)
            v = jnp.where(lane < 64, inside((pair + 1) // 2 - REACH) / jnp.where(lane < 64, w, 1.0), 0.0)
            source2[pair, i] = s
            inverse2[pair, i] = v
            coarse[pair, i] = v * s

    sweep(coarse, source2, inverse2, coarser, COARSE, 10, 10, (1, 1, 1), True)
    sweep(coarser, source2, inverse2, coarse, COARSE, 8, 8, (2, 2, 2), True)
    sweep(coarse, source2, inverse2, coarser, COARSE, 6, 6, (3, 3, 3), True)

    wide = times(jnp.concatenate([p for row in range(3, 9) for p in take(coarser, row)], axis=0), spread)
    for row in range(8, 20):
        for i in range(4):
            at = 16 * (row // 2 - 4) + 8 * (i // 2)
            other[row, i] = middle[row, i] + wide[at : at + 8]

    sweep(other, source1, inverse1, middle, MIDDLE, 8, 4, (10, 10, 10))
    sweep(middle, source1, inverse1, other, MIDDLE, 6, 6, (11, 11, 11))

    spread = spreading(128, 256)
    wide = times(jnp.concatenate([p for row in range(4) for p in take(other, 11 + 2 * c + row)], axis=0), spread)
    for row in range(8):
        for i in range(8):
            at = 32 * (row // 2) + 8 * (i // 2)
            work[row, i] = fine[row, i] + wide[at : at + 8]

    final = work.at[8:14]
    sweep(work, source, inverse, final, FINE, 6, 2, (0, 1, 2))
    for row in range(4):
        new = sweep_row(
            [take(final, row + d) for d in range(3)], take(source, row + 3), take(inverse, row + 3), FINE
        )
        for i, plane in enumerate(new):
            at = (i // 2) * 8 + (i % 2) * 4 + row
            for half in range(PZ):
                out[pl.ds(half * 32 + at, PX, stride=64), :] = plane[:, 128 * half : 128 * half + 128]


def unpack(blocks, out):
    for orbital in range(PX):
        for c in range(PZ):
            for i in range(8):
                base = (orbital * PZ + c) * 32 + (i // 2) * 8 + (i % 2) * 4
                out[orbital, i, 4 * c : 4 * c + 4] = blocks[base : base + 4]


def call(kernel, outs, scratch=(), anywhere=False, others=()):
    vmem = pl.BlockSpec(memory_space=pltpu.VMEM)

    def run(*args):
        return pl.pallas_call(
            kernel,
            out_shape=[(pltpu.VMEM if anywhere else jax.ShapeDtypeStruct)(shape, F32) for shape in outs],
            in_specs=[pl.BlockSpec(memory_space=pl.ANY) if anywhere else vmem] * len(args),
            out_specs=[vmem] * len(outs),
            scratch_shapes=[pltpu.VMEM(shape, F32) for shape in scratch] + list(others),
            compiler_params=pltpu.CompilerParams(vmem_limit_bytes=40 * 1024 * 1024),
        )(*args)

    return run


def run_down(*args):
    return call(
        down,
        [(8, 8, 8, 256), (10, 8, 8, 256), (10, 8, 8, 256), (2, 8, 8, 128)],
        [(12, 8, 8, 256)] + [(10, 8, 8, 256)] * 2,
    )(*args)


def run_up(*args):
    return call(
        up,
        [(512, 128)],
        [(28, 4, 8, 128)] * 5 + [(12, 2, 8, 128)] * 4 + [(14, 8, 8, 256)],
    )(*args)[0]


def body(residual, potential, shifts):
    size_y = lax.axis_size("dom") // (PX * PZ)
    blocks = [(px, py, c) for px in range(PX) for py in range(size_y) for c in range(PZ)]
    lines = [
        [dom_of(px, py, c, size_y) for px in range(PX) for c in range(PZ)] for py in range(size_y)
    ]
    cores = [
        [dom_of(px, py, c, size_y) for c in range(PZ)] for px in range(PX) for py in range(size_y)
    ]

    def pairs(target, bands=False):
        found = [((px, py, c), target(px, py, c)) for px, py, c in blocks]
        found = [(dom_of(*a, size_y), dom_of(*b, size_y)) for a, b in found if 0 <= b[1] < size_y]
        return [(2 * a + n, 2 * b + 1 - n) for a, b in found for n in range(2)] if bands else found

    def swap_lines(value):
        return lax.all_to_all(value, "dom", 0, 0, axis_index_groups=lines, tiled=True)

    def to_beside(px, py, c):
        return (px, py - 1, 1) if c == 0 else (px, py + 1, 0)

    packed, shift = call(
        pack,
        [(768, 128), (8, 128)],
        [(8, 8, 8, 128), (4, 8, 128)],
        anywhere=True,
        others=[pltpu.SMEM((8,), F32), pltpu.SemaphoreType.DMA((PX + 2,))],
    )(*[pltpu.with_memory_space_constraint(x, pltpu.HBM) for x in (residual, potential, shifts)])
    own = swap_lines(packed)
    half = own.reshape(16, 48, 128)[:, 32:].reshape(256, 128)
    both = ("dom", "band")
    own_half = lax.ppermute(half, "band", [(0, 1), (1, 0)])
    beside = lax.ppermute(own, "dom", pairs(to_beside))
    (half,) = call(cut_out, [(256, 128)])(own)
    beside_half = lax.ppermute(half, both, pairs(to_beside, True))
    of_cores = lax.all_gather(own, "dom", axis_index_groups=cores, axis=0)
    of_cores_half = lax.all_gather(own_half, "dom", axis_index_groups=cores, axis=0)
    fine, source, inverse, cut = run_down(shift, of_cores, beside, of_cores_half, beside_half)
    block = lax.all_gather(cut, "dom", axis_index_groups=cores, axis=0, tiled=True)
    sent = [
        lax.ppermute(
            block,
            "dom",
            pairs(lambda px, py, c, k=k: (px, py + k, 0) if c == 0 else (px, py - k, 1)),
        )
        for k in range(1, REACH + 1)
    ]
    around = lax.all_gather(jnp.stack(sent), "dom", axis_index_groups=cores, axis=0)
    final = run_up(shift, fine, source, inverse, block, around)
    (correction,) = call(unpack, [(8, 8, 8, 128)])(swap_lines(final))
    return correction


def solution(mesh):
    return jax.shard_map(
        body,
        mesh=mesh,
        in_specs=(P("band", "dom", None, None), P(("dom", "band"), None, None), P("band")),
        out_specs=P("band", "dom", None, None),
        check_vma=False,
    )
```

```python
import jax
import jax.numpy as jnp
from jax import lax
from jax.experimental import pallas as pl
from jax.experimental.pallas import tpu as pltpu
from jax.sharding import PartitionSpec as P


OMEGA = 0.7
KEEP = 0.3
FINE, MIDDLE, COARSE = 2.0, 0.5, 0.125
PX, PZ = 8, 2
REACH = 3
F32 = jnp.float32
BF16 = jnp.bfloat16


def place():
    position = lax.axis_index("dom")
    size_y = lax.axis_size("dom") // (PX * PZ)
    return position // (size_y * PZ), position // PZ % size_y, position % PZ


def dom_of(px, py, pz, size_y):
    return (px * size_y + py) * PZ + pz


def iota(shape, dimension):
    return lax.broadcasted_iota(jnp.int32, shape, dimension)


def along_x(planes):
    sublane = iota(planes[0].shape, 0)
    first = jnp.where(sublane == 0, 0.0, pltpu.roll(planes[-1], 1, 0))
    last = jnp.where(sublane == PX - 1, 0.0, pltpu.roll(planes[0], PX - 1, 0))
    below = [first] + planes[:-1]
    above = planes[1:] + [last]
    return [b + a for b, a in zip(below, above)]


def along_z(plane, open_end):
    width = plane.shape[1]
    left, right = pltpu.roll(plane, 1, 1), pltpu.roll(plane, width - 1, 1)
    if not open_end:
        lane = iota(plane.shape, 1)
        left = jnp.where(lane == 0, 0.0, left)
        right = jnp.where(lane == width - 1, 0.0, right)
    return left + right


def stencil(below, here, above, open_end=False):
    across = [a + b for a, b in zip(below, above)]
    wide = [a + (h + h) for a, h in zip(across, here)]
    turned = [e + w for e, w in zip(along_x(here), wide)]
    return [
        along_z(t, open_end) + (x + (a + a)) for t, x, a in zip(turned, along_x(wide), across)
    ]


def each(count, chunk, step):
    for base in range(0, count, chunk):
        step(base, min(chunk, count - base))


def take(ref, row):
    return [ref[row, i] for i in range(ref.shape[1])]


def sweep_row(rows, source, inverse, kinetic, open_end=False):
    total = stencil(*rows, open_end)
    return [
        KEEP * u + v * (s + (kinetic / 6.0) * t)
        for u, s, v, t in zip(rows[1], source, inverse, total)
    ]


def sweep(start, source, inverse, target, kinetic, count, chunk, offsets, open_end=False):
    to, of, at = offsets

    def step(base, rows):
        held = [take(start, base + (of + r - 1)) for r in range(rows + 2)]
        for r in range(rows):
            row = base + (at + r)
            new = sweep_row(held[r : r + 3], take(source, row), take(inverse, row), kinetic, open_end)
            for i, plane in enumerate(new):
                target[base + (to + r), i] = plane

    each(count, chunk, step)


def pooling(rows, columns):
    return jnp.where(iota((rows, columns), 0) // 2 == iota((rows, columns), 1), 0.5, 0.0).astype(F32)


def spreading(rows, columns):
    return jnp.where(iota((rows, columns), 0) == iota((rows, columns), 1) // 2, 1.0, 0.0).astype(F32)


def times(value, matrix):
    high = value.astype(BF16)
    rest = value - high.astype(F32)
    middle = rest.astype(BF16)
    low = (rest - middle.astype(F32)).astype(BF16)
    matrix = matrix.astype(BF16)
    parts = [jnp.dot(part, matrix, preferred_element_type=F32) for part in (high, middle, low)]
    return parts[0] + (parts[1] + parts[2])


def cubes(low, high):
    return [
        0.25 * ((low[2 * i] + low[2 * i + 1]) + (high[2 * i] + high[2 * i + 1]))
        for i in range(len(low) // 2)
    ]


def pack(residual, potential, shifts, out, shift, held, planes, numbers, arrived):
    copies = [
        pltpu.make_async_copy(potential, planes, arrived.at[PX]),
        pltpu.make_async_copy(shifts, numbers, arrived.at[PX + 1]),
    ]
    copies += [
        pltpu.make_async_copy(residual.at[i], held.at[i], arrived.at[i]) for i in range(PX)
    ]
    for copy in copies:
        copy.start()
    copies[0].wait()
    for c in range(PZ):
        for i in range(4):
            both = planes[i, 4 * c : 4 * c + 4]
            for orbital in range(PX):
                base = (orbital * PZ + c) * 48 + 32 + 4 * i
                out[base : base + 4] = both
    copies[1].wait()
    shift[...] = jnp.full((8, 128), numbers[place()[0]], F32)
    for orbital in range(PX):
        copies[2 + orbital].wait()
        for c in range(PZ):
            base = (orbital * PZ + c) * 48
            for i in range(8):
                out[base + 4 * i : base + 4 * i + 4] = held[orbital, i, 4 * c : 4 * c + 4]


def cut_out(slab, out):
    for piece in range(16):
        out[16 * piece : 16 * piece + 16] = slab[48 * piece + 32 : 48 * piece + 48]


def down(shifts, cores, beside, cores_half, beside_half, fine_out, source, inverse, cut, field, potential, start):
    px, py, c = place()
    size_y = lax.axis_size("dom") // (PX * PZ)
    shift = jnp.concatenate([shifts[...]] * 2, axis=1)
    band = lax.axis_index("band")

    def unpack(blocks, halves):
        for row in range(12):
            block, other_half = blocks[row // 4], halves[row // 4]
            for half in range(PZ):
                lanes = slice(128 * half, 128 * half + 128)
                for i in range(8):
                    at = 48 * half + 4 * i + row % 4
                    field[row, i, :, lanes] = block[pl.ds(at, PX, stride=96), :]
                if 1 <= row <= 10:
                    for i in range(4):
                        at = 48 * half + 32 + 4 * i + row % 4
                        potential[row - 1, 4 * band + i, :, lanes] = block[pl.ds(at, PX, stride=96), :]
                        at = 16 * half + 4 * i + row % 4
                        potential[row - 1, 4 * (1 - band) + i, :, lanes] = other_half[pl.ds(at, PX, stride=32), :]

    here = (cores.at[0], cores.at[1])
    here_half = (cores_half.at[0], cores_half.at[1])
    pl.when(c == 0)(lambda: unpack((beside, *here), (beside_half, *here_half)))
    pl.when(c == 1)(lambda: unpack((*here, beside), (*here_half, beside_half)))

    def first(base, rows):
        for r in range(rows):
            row = base + r
            y = py * 8 + 4 * c + row - 3
            inside = jnp.where((y >= 0) & (y < 8 * size_y), OMEGA, 0.0).astype(F32)
            below, here, above = [take(field, row + d) for d in range(3)]
            for i, (b, h, a, x) in enumerate(zip(below, here, above, along_x(here))):
                s = 0.5 * h + ((b + a) + (x + along_z(h, False))) * (1.0 / 12.0)
                v = inside / (potential[row, i] + (4.0 * FINE + shift))
                source[row, i] = s
                inverse[row, i] = v
                start[row, i] = v * s

    each(10, 2, first)
    sweep(start, source, inverse, fine_out, FINE, 8, 2, (0, 1, 1))

    pool = pooling(256, 128)
    means = []
    for pair in range(2):
        left = []
        for row in (2 * pair, 2 * pair + 1):
            rows = [take(fine_out, row + d) for d in (1, 2, 3)]
            weight = [v + (4.0 * FINE + shift) for v in take(potential, row + 3)]
            total = stencil(*rows)
            left.append(
                [s + (FINE / 6.0) * t - w * u for s, t, w, u in zip(take(source, row + 3), total, weight, rows[1])]
            )
        means += cubes(*left) + cubes(take(potential, 2 * pair + 3), take(potential, 2 * pair + 4))
    small = times(jnp.concatenate(means, axis=0), pool)
    for pair in range(2):
        for i in range(8):
            cut[pair, i] = small[64 * pair + 8 * i : 64 * pair + 8 * i + 8]


def up(shifts, fine, source, inverse, block, around, out, weight1, source1, inverse1, middle, other, source2, inverse2, coarse, coarser, work):
    px, py, c = place()
    size_y = lax.axis_size("dom") // (PX * PZ)
    shift = shifts[...]

    def inside(distance):
        return jnp.where((py + distance >= 0) & (py + distance < size_y), OMEGA, 0.0).astype(F32)

    for row in range(28):
        distance = row // 4 - REACH
        if distance == 0:
            at = lambda i: block[row % 4, i]
        else:
            side, step = (0, -distance - 1) if distance < 0 else (1, distance - 1)
            at = lambda i: around[side, step, row % 4, i]
        for i in range(4):
            s = at(i)
            w = at(4 + i) + (4.0 * MIDDLE + shift)
            v = inside(distance) / w
            source1[row, i] = s
            weight1[row, i] = w
            inverse1[row, i] = v
            other[row, i] = v * s

    sweep(other, source1, inverse1, middle, MIDDLE, 26, 4, (1, 1, 1))

    pool = pooling(128, 128)
    spread = spreading(128, 128)
    lane = iota((8, 128), 1)

    means = []
    for pair in range(12):
        left, weights = [], []
        for row in (2 * pair + 2, 2 * pair + 3):
            rows = [take(middle, row + d) for d in (-1, 0, 1)]
            w = take(weight1, row)
            total = stencil(*rows)
            left.append(
                [s + (MIDDLE / 6.0) * t - x * u for s, t, x, u in zip(take(source1, row), total, w, rows[1])]
            )
            weights.append(w)
        means += cubes(*left) + cubes(*weights)
    small = times(jnp.concatenate(means, axis=0), pool)
    for pair in range(12):
        for i in range(2):
            s = small[32 * pair + 8 * i : 32 * pair + 8 * i + 8]
            w = small[32 * pair + 8 * i + 16 : 32 * pair + 8 * i + 24] + (4.0 * COARSE - 4.0 * MIDDLE)
            v = jnp.where(lane < 64, inside((pair + 1) // 2 - REACH) / jnp.where(lane < 64, w, 1.0), 0.0)
            source2[pair, i] = s
            inverse2[pair, i] = v
            coarse[pair, i] = v * s

    sweep(coarse, source2, inverse2, coarser, COARSE, 10, 10, (1, 1, 1), True)
    sweep(coarser, source2, inverse2, coarse, COARSE, 8, 8, (2, 2, 2), True)
    sweep(coarse, source2, inverse2, coarser, COARSE, 6, 6, (3, 3, 3), True)

    wide = times(jnp.concatenate([p for row in range(3, 9) for p in take(coarser, row)], axis=0), spread)
    for row in range(8, 20):
        for i in range(4):
            at = 16 * (row // 2 - 4) + 8 * (i // 2)
            other[row, i] = middle[row, i] + wide[at : at + 8]

    sweep(other, source1, inverse1, middle, MIDDLE, 8, 4, (10, 10, 10))
    sweep(middle, source1, inverse1, other, MIDDLE, 6, 6, (11, 11, 11))

    spread = spreading(128, 256)
    wide = times(jnp.concatenate([p for row in range(4) for p in take(other, 11 + 2 * c + row)], axis=0), spread)
    for row in range(8):
        for i in range(8):
            at = 32 * (row // 2) + 8 * (i // 2)
            work[row, i] = fine[row, i] + wide[at : at + 8]

    final = work.at[8:14]
    sweep(work, source, inverse, final, FINE, 6, 2, (0, 1, 2))
    for row in range(4):
        new = sweep_row(
            [take(final, row + d) for d in range(3)], take(source, row + 3), take(inverse, row + 3), FINE
        )
        for i, plane in enumerate(new):
            at = (i // 2) * 8 + (i % 2) * 4 + row
            for half in range(PZ):
                out[pl.ds(half * 32 + at, PX, stride=64), :] = plane[:, 128 * half : 128 * half + 128]


def unpack(blocks, out):
    for orbital in range(PX):
        for c in range(PZ):
            for i in range(8):
                base = (orbital * PZ + c) * 32 + (i // 2) * 8 + (i % 2) * 4
                out[orbital, i, 4 * c : 4 * c + 4] = blocks[base : base + 4]


def call(kernel, outs, scratch=(), anywhere=False, others=()):
    vmem = pl.BlockSpec(memory_space=pltpu.VMEM)

    def run(*args):
        return pl.pallas_call(
            kernel,
            out_shape=[(pltpu.VMEM if anywhere else jax.ShapeDtypeStruct)(shape, F32) for shape in outs],
            in_specs=[pl.BlockSpec(memory_space=pl.ANY) if anywhere else vmem] * len(args),
            out_specs=[vmem] * len(outs),
            scratch_shapes=[pltpu.VMEM(shape, F32) for shape in scratch] + list(others),
            compiler_params=pltpu.CompilerParams(vmem_limit_bytes=40 * 1024 * 1024),
        )(*args)

    return run


def run_down(*args):
    return call(
        down,
        [(8, 8, 8, 256), (10, 8, 8, 256), (10, 8, 8, 256), (2, 8, 8, 128)],
        [(12, 8, 8, 256)] + [(10, 8, 8, 256)] * 2,
    )(*args)


def run_up(*args):
    return call(
        up,
        [(512, 128)],
        [(28, 4, 8, 128)] * 5 + [(12, 2, 8, 128)] * 4 + [(14, 8, 8, 256)],
    )(*args)[0]


def body(residual, potential, shifts):
    size_y = lax.axis_size("dom") // (PX * PZ)
    blocks = [(px, py, c) for px in range(PX) for py in range(size_y) for c in range(PZ)]
    lines = [
        [dom_of(px, py, c, size_y) for px in range(PX) for c in range(PZ)] for py in range(size_y)
    ]
    cores = [
        [dom_of(px, py, c, size_y) for c in range(PZ)] for px in range(PX) for py in range(size_y)
    ]

    def pairs(target, bands=False):
        found = [((px, py, c), target(px, py, c)) for px, py, c in blocks]
        found = [(dom_of(*a, size_y), dom_of(*b, size_y)) for a, b in found if 0 <= b[1] < size_y]
        return [(2 * a + n, 2 * b + 1 - n) for a, b in found for n in range(2)] if bands else found

    def swap_lines(value):
        return lax.all_to_all(value, "dom", 0, 0, axis_index_groups=lines, tiled=True)

    def to_beside(px, py, c):
        return (px, py - 1, 1) if c == 0 else (px, py + 1, 0)

    packed, shift = call(
        pack,
        [(768, 128), (8, 128)],
        [(8, 8, 8, 128), (4, 8, 128)],
        anywhere=True,
        others=[pltpu.SMEM((8,), F32), pltpu.SemaphoreType.DMA((PX + 2,))],
    )(*[pltpu.with_memory_space_constraint(x, pltpu.HBM) for x in (residual, potential, shifts)])
    own = swap_lines(packed)
    half = own.reshape(16, 48, 128)[:, 32:].reshape(256, 128)
    both = ("dom", "band")
    own_half = lax.ppermute(half, "band", [(0, 1), (1, 0)])
    beside = lax.ppermute(own, "dom", pairs(to_beside))
    (half,) = call(cut_out, [(256, 128)])(own)
    beside_half = lax.ppermute(half, both, pairs(to_beside, True))
    of_cores = lax.all_gather(own, "dom", axis_index_groups=cores, axis=0)
    of_cores_half = lax.all_gather(own_half, "dom", axis_index_groups=cores, axis=0)
    fine, source, inverse, cut = run_down(shift, of_cores, beside, of_cores_half, beside_half)
    block = lax.all_gather(cut, "dom", axis_index_groups=cores, axis=0, tiled=True)
    sent = [
        lax.ppermute(
            block,
            "dom",
            pairs(lambda px, py, c, k=k: (px, py + k, 0) if c == 0 else (px, py - k, 1)),
        )
        for k in range(REACH, 0, -1)
    ]
    around = lax.all_gather(jnp.stack(sent[::-1]), "dom", axis_index_groups=cores, axis=0)
    final = run_up(shift, fine, source, inverse, block, around)
    (correction,) = call(unpack, [(8, 8, 8, 128)])(swap_lines(final))
    return correction


def solution(mesh):
    return jax.shard_map(
        body,
        mesh=mesh,
        in_specs=(P("band", "dom", None, None), P(("dom", "band"), None, None), P("band")),
        out_specs=P("band", "dom", None, None),
        check_vma=False,
    )
```

```python
import jax
import jax.numpy as jnp
from jax import lax
from jax.experimental import pallas as pl
from jax.experimental.pallas import tpu as pltpu
from jax.sharding import PartitionSpec as P


OMEGA = 0.7
KEEP = 0.3
FINE, MIDDLE, COARSE = 2.0, 0.5, 0.125
PX, PZ = 8, 2
REACH = 3
F32 = jnp.float32
BF16 = jnp.bfloat16


def place():
    position = lax.axis_index("dom")
    size_y = lax.axis_size("dom") // (PX * PZ)
    return position // (size_y * PZ), position // PZ % size_y, position % PZ


def dom_of(px, py, pz, size_y):
    return (px * size_y + py) * PZ + pz


def iota(shape, dimension):
    return lax.broadcasted_iota(jnp.int32, shape, dimension)


def along_x(planes):
    sublane = iota(planes[0].shape, 0)
    first = jnp.where(sublane == 0, 0.0, pltpu.roll(planes[-1], 1, 0))
    last = jnp.where(sublane == PX - 1, 0.0, pltpu.roll(planes[0], PX - 1, 0))
    below = [first] + planes[:-1]
    above = planes[1:] + [last]
    return [b + a for b, a in zip(below, above)]


def along_z(plane, open_end):
    width = plane.shape[1]
    left, right = pltpu.roll(plane, 1, 1), pltpu.roll(plane, width - 1, 1)
    if not open_end:
        lane = iota(plane.shape, 1)
        left = jnp.where(lane == 0, 0.0, left)
        right = jnp.where(lane == width - 1, 0.0, right)
    return left + right


def stencil(below, here, above, open_end=False):
    across = [a + b for a, b in zip(below, above)]
    wide = [a + (h + h) for a, h in zip(across, here)]
    turned = [e + w for e, w in zip(along_x(here), wide)]
    return [
        along_z(t, open_end) + (x + (a + a)) for t, x, a in zip(turned, along_x(wide), across)
    ]


def each(count, chunk, step):
    for base in range(0, count, chunk):
        step(base, min(chunk, count - base))


def take(ref, row):
    return [ref[row, i] for i in range(ref.shape[1])]


def sweep_row(rows, source, inverse, kinetic, open_end=False):
    total = stencil(*rows, open_end)
    return [
        KEEP * u + v * (s + (kinetic / 6.0) * t)
        for u, s, v, t in zip(rows[1], source, inverse, total)
    ]


def sweep(start, source, inverse, target, kinetic, count, chunk, offsets, open_end=False):
    to, of, at = offsets

    def step(base, rows):
        held = [take(start, base + (of + r - 1)) for r in range(rows + 2)]
        for r in range(rows):
            row = base + (at + r)
            new = sweep_row(held[r : r + 3], take(source, row), take(inverse, row), kinetic, open_end)
            for i, plane in enumerate(new):
                target[base + (to + r), i] = plane

    each(count, chunk, step)


def pooling(rows, columns):
    return jnp.where(iota((rows, columns), 0) // 2 == iota((rows, columns), 1), 0.5, 0.0).astype(F32)


def spreading(rows, columns):
    return jnp.where(iota((rows, columns), 0) == iota((rows, columns), 1) // 2, 1.0, 0.0).astype(F32)


def times(value, matrix):
    high = value.astype(BF16)
    rest = value - high.astype(F32)
    middle = rest.astype(BF16)
    low = (rest - middle.astype(F32)).astype(BF16)
    matrix = matrix.astype(BF16)
    parts = [jnp.dot(part, matrix, preferred_element_type=F32) for part in (high, middle, low)]
    return parts[0] + (parts[1] + parts[2])


def cubes(low, high):
    return [
        0.25 * ((low[2 * i] + low[2 * i + 1]) + (high[2 * i] + high[2 * i + 1]))
        for i in range(len(low) // 2)
    ]


def pack(residual, potential, shifts, out, shift, held, planes, numbers, arrived):
    copies = [
        pltpu.make_async_copy(potential, planes, arrived.at[PX]),
        pltpu.make_async_copy(shifts, numbers, arrived.at[PX + 1]),
    ]
    copies += [
        pltpu.make_async_copy(residual.at[i], held.at[i], arrived.at[i]) for i in range(PX)
    ]
    for copy in copies:
        copy.start()
    copies[0].wait()
    for c in range(PZ):
        for i in range(4):
            both = planes[i, 4 * c : 4 * c + 4]
            for orbital in range(PX):
                base = (orbital * PZ + c) * 48 + 32 + i
                out[pl.ds(base, 4, stride=4), :] = both
    copies[1].wait()
    shift[...] = jnp.full((8, 128), numbers[place()[0]], F32)
    for orbital in range(PX):
        copies[2 + orbital].wait()
        for c in range(PZ):
            base = (orbital * PZ + c) * 48
            for i in range(8):
                out[base + 4 * i : base + 4 * i + 4] = held[orbital, i, 4 * c : 4 * c + 4]


def cut_out(slab, out, weights):
    _, _, c = place()

    def rows(first):
        for piece in range(16):
            out[32 * piece : 32 * piece + 32] = slab[48 * piece : 48 * piece + 32]
            near = slab[48 * piece + 32 + first : 48 * piece + 44 + first]
            out[512 + 12 * piece : 524 + 12 * piece] = near
            weights[12 * piece : 12 * piece + 12] = near

    pl.when(c == 0)(lambda: rows(0))
    pl.when(c == 1)(lambda: rows(4))


def down(shifts, cores, beside, cores_half, beside_half, fine_out, source, inverse, cut, field, potential, start):
    px, py, c = place()
    size_y = lax.axis_size("dom") // (PX * PZ)
    shift = jnp.concatenate([shifts[...]] * 2, axis=1)
    band = lax.axis_index("band")

    def unpack(blocks, halves):
        for row in range(12):
            block, other_half = blocks[row // 4], halves[row // 4]
            apart = block is beside
            piece, stride = (32, 64) if apart else (48, 96)
            near = row % 4 - (apart and row < 4)
            for half in range(PZ):
                lanes = slice(128 * half, 128 * half + 128)
                for i in range(8):
                    at = piece * half + 4 * i + row % 4
                    field[row, i, :, lanes] = block[pl.ds(at, PX, stride=stride), :]
                if 1 <= row <= 10:
                    for i in range(4):
                        if apart:
                            at, other, steps = 512 + 12 * half + 4 * near + i, 12 * half + 4 * near + i, (24, 24)
                        else:
                            at, other, steps = 48 * half + 32 + 4 * near + i, 16 * half + 4 * near + i, (96, 32)
                        potential[row - 1, 4 * band + i, :, lanes] = block[pl.ds(at, PX, stride=steps[0]), :]
                        potential[row - 1, 4 * (1 - band) + i, :, lanes] = other_half[
                            pl.ds(other, PX, stride=steps[1]), :
                        ]

    here = (cores.at[0], cores.at[1])
    here_half = (cores_half.at[0], cores_half.at[1])
    pl.when(c == 0)(lambda: unpack((beside, *here), (beside_half, *here_half)))
    pl.when(c == 1)(lambda: unpack((*here, beside), (*here_half, beside_half)))

    def first(base, rows):
        for r in range(rows):
            row = base + r
            y = py * 8 + 4 * c + row - 3
            inside = jnp.where((y >= 0) & (y < 8 * size_y), OMEGA, 0.0).astype(F32)
            below, here, above = [take(field, row + d) for d in range(3)]
            for i, (b, h, a, x) in enumerate(zip(below, here, above, along_x(here))):
                s = 0.5 * h + ((b + a) + (x + along_z(h, False))) * (1.0 / 12.0)
                v = inside / (potential[row, i] + (4.0 * FINE + shift))
                source[row, i] = s
                inverse[row, i] = v
                start[row, i] = v * s

    each(10, 2, first)
    sweep(start, source, inverse, fine_out, FINE, 8, 2, (0, 1, 1))

    pool = pooling(256, 128)
    means = []
    for pair in range(2):
        left = []
        for row in (2 * pair, 2 * pair + 1):
            rows = [take(fine_out, row + d) for d in (1, 2, 3)]
            weight = [v + (4.0 * FINE + shift) for v in take(potential, row + 3)]
            total = stencil(*rows)
            left.append(
                [s + (FINE / 6.0) * t - w * u for s, t, w, u in zip(take(source, row + 3), total, weight, rows[1])]
            )
        means += cubes(*left) + cubes(take(potential, 2 * pair + 3), take(potential, 2 * pair + 4))
    small = times(jnp.concatenate(means, axis=0), pool)
    for pair in range(2):
        for i in range(8):
            cut[pair, i] = small[64 * pair + 8 * i : 64 * pair + 8 * i + 8]


def up(shifts, fine, source, inverse, block, around, out, weight1, source1, inverse1, middle, other, source2, inverse2, coarse, coarser, work):
    px, py, c = place()
    size_y = lax.axis_size("dom") // (PX * PZ)
    shift = shifts[...]

    def inside(distance):
        return jnp.where((py + distance >= 0) & (py + distance < size_y), OMEGA, 0.0).astype(F32)

    for row in range(28):
        distance = row // 4 - REACH
        if distance == 0:
            at = lambda i: block[row % 4, i]
        else:
            side, step = (0, -distance - 1) if distance < 0 else (1, distance - 1)
            at = lambda i: around[side, step, row % 4, i]
        for i in range(4):
            s = at(i)
            w = at(4 + i) + (4.0 * MIDDLE + shift)
            v = inside(distance) / w
            source1[row, i] = s
            weight1[row, i] = w
            inverse1[row, i] = v
            other[row, i] = v * s

    sweep(other, source1, inverse1, middle, MIDDLE, 26, 4, (1, 1, 1))

    pool = pooling(128, 128)
    spread = spreading(128, 128)
    lane = iota((8, 128), 1)

    means = []
    for pair in range(12):
        left, weights = [], []
        for row in (2 * pair + 2, 2 * pair + 3):
            rows = [take(middle, row + d) for d in (-1, 0, 1)]
            w = take(weight1, row)
            total = stencil(*rows)
            left.append(
                [s + (MIDDLE / 6.0) * t - x * u for s, t, x, u in zip(take(source1, row), total, w, rows[1])]
            )
            weights.append(w)
        means += cubes(*left) + cubes(*weights)
    small = times(jnp.concatenate(means, axis=0), pool)
    for pair in range(12):
        for i in range(2):
            s = small[32 * pair + 8 * i : 32 * pair + 8 * i + 8]
            w = small[32 * pair + 8 * i + 16 : 32 * pair + 8 * i + 24] + (4.0 * COARSE - 4.0 * MIDDLE)
            v = jnp.where(lane < 64, inside((pair + 1) // 2 - REACH) / jnp.where(lane < 64, w, 1.0), 0.0)
            source2[pair, i] = s
            inverse2[pair, i] = v
            coarse[pair, i] = v * s

    sweep(coarse, source2, inverse2, coarser, COARSE, 10, 10, (1, 1, 1), True)
    sweep(coarser, source2, inverse2, coarse, COARSE, 8, 8, (2, 2, 2), True)
    sweep(coarse, source2, inverse2, coarser, COARSE, 6, 6, (3, 3, 3), True)

    wide = times(jnp.concatenate([p for row in range(3, 9) for p in take(coarser, row)], axis=0), spread)
    for row in range(8, 20):
        for i in range(4):
            at = 16 * (row // 2 - 4) + 8 * (i // 2)
            other[row, i] = middle[row, i] + wide[at : at + 8]

    sweep(other, source1, inverse1, middle, MIDDLE, 8, 4, (10, 10, 10))
    sweep(middle, source1, inverse1, other, MIDDLE, 6, 6, (11, 11, 11))

    spread = spreading(128, 256)
    wide = times(jnp.concatenate([p for row in range(4) for p in take(other, 11 + 2 * c + row)], axis=0), spread)
    for row in range(8):
        for i in range(8):
            at = 32 * (row // 2) + 8 * (i // 2)
            work[row, i] = fine[row, i] + wide[at : at + 8]

    final = work.at[8:14]
    sweep(work, source, inverse, final, FINE, 6, 2, (0, 1, 2))
    for row in range(4):
        new = sweep_row(
            [take(final, row + d) for d in range(3)], take(source, row + 3), take(inverse, row + 3), FINE
        )
        for i, plane in enumerate(new):
            at = (i // 2) * 8 + (i % 2) * 4 + row
            for half in range(PZ):
                out[pl.ds(half * 32 + at, PX, stride=64), :] = plane[:, 128 * half : 128 * half + 128]


def unpack(blocks, out):
    for orbital in range(PX):
        for c in range(PZ):
            for i in range(8):
                base = (orbital * PZ + c) * 32 + (i // 2) * 8 + (i % 2) * 4
                out[orbital, i, 4 * c : 4 * c + 4] = blocks[base : base + 4]


def call(kernel, outs, scratch=(), anywhere=False, others=()):
    vmem = pl.BlockSpec(memory_space=pltpu.VMEM)

    def run(*args):
        return pl.pallas_call(
            kernel,
            out_shape=[(pltpu.VMEM if anywhere else jax.ShapeDtypeStruct)(shape, F32) for shape in outs],
            in_specs=[pl.BlockSpec(memory_space=pl.ANY) if anywhere else vmem] * len(args),
            out_specs=[vmem] * len(outs),
            scratch_shapes=[pltpu.VMEM(shape, F32) for shape in scratch] + list(others),
            compiler_params=pltpu.CompilerParams(vmem_limit_bytes=40 * 1024 * 1024),
        )(*args)

    return run


def run_down(*args):
    return call(
        down,
        [(8, 8, 8, 256), (10, 8, 8, 256), (10, 8, 8, 256), (2, 8, 8, 128)],
        [(12, 8, 8, 256)] + [(10, 8, 8, 256)] * 2,
    )(*args)


def run_up(*args):
    return call(
        up,
        [(512, 128)],
        [(28, 4, 8, 128)] * 5 + [(12, 2, 8, 128)] * 4 + [(14, 8, 8, 256)],
    )(*args)[0]


def body(residual, potential, shifts):
    size_y = lax.axis_size("dom") // (PX * PZ)
    blocks = [(px, py, c) for px in range(PX) for py in range(size_y) for c in range(PZ)]
    lines = [
        [dom_of(px, py, c, size_y) for px in range(PX) for c in range(PZ)] for py in range(size_y)
    ]
    cores = [
        [dom_of(px, py, c, size_y) for c in range(PZ)] for px in range(PX) for py in range(size_y)
    ]

    def pairs(target, bands=False):
        found = [((px, py, c), target(px, py, c)) for px, py, c in blocks]
        found = [(dom_of(*a, size_y), dom_of(*b, size_y)) for a, b in found if 0 <= b[1] < size_y]
        return [(2 * a + n, 2 * b + 1 - n) for a, b in found for n in range(2)] if bands else found

    def swap_lines(value):
        return lax.all_to_all(value, "dom", 0, 0, axis_index_groups=lines, tiled=True)

    def to_beside(px, py, c):
        return (px, py - 1, 1) if c == 0 else (px, py + 1, 0)

    packed, shift = call(
        pack,
        [(768, 128), (8, 128)],
        [(8, 8, 8, 128), (4, 8, 128)],
        anywhere=True,
        others=[pltpu.SMEM((8,), F32), pltpu.SemaphoreType.DMA((PX + 2,))],
    )(*[pltpu.with_memory_space_constraint(x, pltpu.HBM) for x in (residual, potential, shifts)])
    own = swap_lines(packed)
    half = own.reshape(16, 48, 128)[:, 32:].reshape(256, 128)
    both = ("dom", "band")
    own_half = lax.ppermute(half, "band", [(0, 1), (1, 0)])
    given, half = call(cut_out, [(704, 128), (192, 128)])(own)
    beside = lax.ppermute(given, "dom", pairs(to_beside))
    beside_half = lax.ppermute(half, both, pairs(to_beside, True))
    of_cores = lax.all_gather(own, "dom", axis_index_groups=cores, axis=0)
    of_cores_half = lax.all_gather(own_half, "dom", axis_index_groups=cores, axis=0)
    fine, source, inverse, cut = run_down(shift, of_cores, beside, of_cores_half, beside_half)
    block = lax.all_gather(cut, "dom", axis_index_groups=cores, axis=0, tiled=True)
    sent = [
        lax.ppermute(
            block,
            "dom",
            pairs(lambda px, py, c, k=k: (px, py + k, 0) if c == 0 else (px, py - k, 1)),
        )
        for k in range(REACH, 0, -1)
    ]
    around = lax.all_gather(jnp.stack(sent[::-1]), "dom", axis_index_groups=cores, axis=0)
    final = run_up(shift, fine, source, inverse, block, around)
    (correction,) = call(unpack, [(8, 8, 8, 128)])(swap_lines(final))
    return correction


def solution(mesh):
    return jax.shard_map(
        body,
        mesh=mesh,
        in_specs=(P("band", "dom", None, None), P(("dom", "band"), None, None), P("band")),
        out_specs=P("band", "dom", None, None),
        check_vma=False,
    )
```

```python
import jax
import jax.numpy as jnp
from jax import lax
from jax.experimental import pallas as pl
from jax.experimental.pallas import tpu as pltpu
from jax.sharding import PartitionSpec as P


OMEGA = 0.7
KEEP = 0.3
FINE, MIDDLE, COARSE = 2.0, 0.5, 0.125
PX, PZ = 8, 2
REACH = 3
F32 = jnp.float32
BF16 = jnp.bfloat16


def place():
    position = lax.axis_index("dom")
    size_y = lax.axis_size("dom") // (PX * PZ)
    return position // (size_y * PZ), position // PZ % size_y, position % PZ


def dom_of(px, py, pz, size_y):
    return (px * size_y + py) * PZ + pz


def iota(shape, dimension):
    return lax.broadcasted_iota(jnp.int32, shape, dimension)


def along_x(planes):
    sublane = iota(planes[0].shape, 0)
    first = jnp.where(sublane == 0, 0.0, pltpu.roll(planes[-1], 1, 0))
    last = jnp.where(sublane == PX - 1, 0.0, pltpu.roll(planes[0], PX - 1, 0))
    below = [first] + planes[:-1]
    above = planes[1:] + [last]
    return [b + a for b, a in zip(below, above)]


def along_z(plane, open_end):
    width = plane.shape[1]
    left, right = pltpu.roll(plane, 1, 1), pltpu.roll(plane, width - 1, 1)
    if not open_end:
        lane = iota(plane.shape, 1)
        left = jnp.where(lane == 0, 0.0, left)
        right = jnp.where(lane == width - 1, 0.0, right)
    return left + right


def stencil(below, here, above, open_end=False):
    across = [a + b for a, b in zip(below, above)]
    wide = [a + (h + h) for a, h in zip(across, here)]
    turned = [e + w for e, w in zip(along_x(here), wide)]
    return [
        along_z(t, open_end) + (x + (a + a)) for t, x, a in zip(turned, along_x(wide), across)
    ]


def each(count, chunk, step):
    for base in range(0, count, chunk):
        step(base, min(chunk, count - base))


def take(ref, row):
    return [ref[row, i] for i in range(ref.shape[1])]


def sweep_row(rows, source, inverse, kinetic, open_end=False):
    total = stencil(*rows, open_end)
    return [
        KEEP * u + v * (s + (kinetic / 6.0) * t)
        for u, s, v, t in zip(rows[1], source, inverse, total)
    ]


def sweep(start, source, inverse, target, kinetic, count, chunk, offsets, open_end=False):
    to, of, at = offsets

    def step(base, rows):
        held = [take(start, base + (of + r - 1)) for r in range(rows + 2)]
        for r in range(rows):
            row = base + (at + r)
            new = sweep_row(held[r : r + 3], take(source, row), take(inverse, row), kinetic, open_end)
            for i, plane in enumerate(new):
                target[base + (to + r), i] = plane

    each(count, chunk, step)


def pooling(rows, columns):
    return jnp.where(iota((rows, columns), 0) // 2 == iota((rows, columns), 1), 0.5, 0.0).astype(F32)


def spreading(rows, columns):
    return jnp.where(iota((rows, columns), 0) == iota((rows, columns), 1) // 2, 1.0, 0.0).astype(F32)


def times(value, matrix):
    high = value.astype(BF16)
    rest = value - high.astype(F32)
    middle = rest.astype(BF16)
    low = (rest - middle.astype(F32)).astype(BF16)
    matrix = matrix.astype(BF16)
    parts = [jnp.dot(part, matrix, preferred_element_type=F32) for part in (high, middle, low)]
    return parts[0] + (parts[1] + parts[2])


def cubes(low, high):
    return [
        0.25 * ((low[2 * i] + low[2 * i + 1]) + (high[2 * i] + high[2 * i + 1]))
        for i in range(len(low) // 2)
    ]


def pack(residual, potential, shifts, out, shift, held, planes, numbers, arrived):
    copies = [
        pltpu.make_async_copy(potential, planes, arrived.at[PX]),
        pltpu.make_async_copy(shifts, numbers, arrived.at[PX + 1]),
    ]
    copies += [
        pltpu.make_async_copy(residual.at[i], held.at[i], arrived.at[i]) for i in range(PX)
    ]
    for copy in copies:
        copy.start()
    copies[0].wait()
    for c in range(PZ):
        for i in range(4):
            both = planes[i, 4 * c : 4 * c + 4]
            for orbital in range(PX):
                base = (orbital * PZ + c) * 48 + 32 + i
                out[pl.ds(base, 4, stride=4), :] = both
    copies[1].wait()
    shift[...] = jnp.full((8, 128), numbers[place()[0]], F32)
    for orbital in range(PX):
        copies[2 + orbital].wait()
        for c in range(PZ):
            base = (orbital * PZ + c) * 48
            for i in range(8):
                out[base + 4 * i : base + 4 * i + 4] = held[orbital, i, 4 * c : 4 * c + 4]


def cut_out(slab, out, weights):
    _, _, c = place()

    def rows(first):
        for piece in range(16):
            out[32 * piece : 32 * piece + 32] = slab[48 * piece : 48 * piece + 32]
            near = slab[48 * piece + 32 + first : 48 * piece + 44 + first]
            out[512 + 12 * piece : 524 + 12 * piece] = near
            weights[12 * piece : 12 * piece + 12] = near

    pl.when(c == 0)(lambda: rows(0))
    pl.when(c == 1)(lambda: rows(4))


def begin(cores, beside, source, weights, field):
    _, _, c = place()

    def unpack(*blocks):
        for row in range(12):
            block = blocks[row // 4]
            apart = block is beside
            piece, stride = (32, 64) if apart else (48, 96)
            near = row % 4 - (apart and row < 4)
            for half in range(PZ):
                lanes = slice(128 * half, 128 * half + 128)
                for i in range(8):
                    at = piece * half + 4 * i + row % 4
                    field[row, i, :, lanes] = block[pl.ds(at, PX, stride=stride), :]
                if 1 <= row <= 10:
                    for i in range(4):
                        at, step = (512 + 12 * half, 24) if apart else (48 * half + 32, 96)
                        weights[row - 1, i, :, lanes] = block[pl.ds(at + 4 * near + i, PX, stride=step), :]

    pl.when(c == 0)(lambda: unpack(beside, cores.at[0], cores.at[1]))
    pl.when(c == 1)(lambda: unpack(cores.at[0], cores.at[1], beside))
    for row in range(10):
        below, here, above = [take(field, row + d) for d in range(3)]
        for i, (b, h, a, x) in enumerate(zip(below, here, above, along_x(here))):
            source[row, i] = 0.5 * h + ((b + a) + (x + along_z(h, False))) * (1.0 / 12.0)


def down(shifts, source, weights, cores_half, beside_half, fine_out, inverse, cut, potential, start):
    px, py, c = place()
    size_y = lax.axis_size("dom") // (PX * PZ)
    shift = jnp.concatenate([shifts[...]] * 2, axis=1)
    band = lax.axis_index("band")

    def unpack(*halves):
        for row in range(1, 11):
            other_half = halves[row // 4]
            apart = other_half is beside_half
            near = row % 4 - (apart and row < 4)
            for i in range(4):
                potential[row - 1, 4 * band + i] = weights[row - 1, i]
                for half in range(PZ):
                    lanes = slice(128 * half, 128 * half + 128)
                    at, step = (12 * half, 24) if apart else (16 * half, 32)
                    potential[row - 1, 4 * (1 - band) + i, :, lanes] = other_half[
                        pl.ds(at + 4 * near + i, PX, stride=step), :
                    ]

    pl.when(c == 0)(lambda: unpack(beside_half, cores_half.at[0], cores_half.at[1]))
    pl.when(c == 1)(lambda: unpack(cores_half.at[0], cores_half.at[1], beside_half))

    def first(base, rows):
        for r in range(rows):
            row = base + r
            y = py * 8 + 4 * c + row - 3
            inside = jnp.where((y >= 0) & (y < 8 * size_y), OMEGA, 0.0).astype(F32)
            for i in range(8):
                v = inside / (potential[row, i] + (4.0 * FINE + shift))
                inverse[row, i] = v
                start[row, i] = v * source[row, i]

    each(10, 2, first)
    sweep(start, source, inverse, fine_out, FINE, 8, 2, (0, 1, 1))

    pool = pooling(256, 128)
    means = []
    for pair in range(2):
        left = []
        for row in (2 * pair, 2 * pair + 1):
            rows = [take(fine_out, row + d) for d in (1, 2, 3)]
            weight = [v + (4.0 * FINE + shift) for v in take(potential, row + 3)]
            total = stencil(*rows)
            left.append(
                [s + (FINE / 6.0) * t - w * u for s, t, w, u in zip(take(source, row + 3), total, weight, rows[1])]
            )
        means += cubes(*left) + cubes(take(potential, 2 * pair + 3), take(potential, 2 * pair + 4))
    small = times(jnp.concatenate(means, axis=0), pool)
    for pair in range(2):
        for i in range(8):
            cut[pair, i] = small[64 * pair + 8 * i : 64 * pair + 8 * i + 8]


def up(shifts, fine, source, inverse, block, around, out, weight1, source1, inverse1, middle, other, source2, inverse2, coarse, coarser, work):
    px, py, c = place()
    size_y = lax.axis_size("dom") // (PX * PZ)
    shift = shifts[...]

    def inside(distance):
        return jnp.where((py + distance >= 0) & (py + distance < size_y), OMEGA, 0.0).astype(F32)

    for row in range(28):
        distance = row // 4 - REACH
        if distance == 0:
            at = lambda i: block[row % 4, i]
        else:
            side, step = (0, -distance - 1) if distance < 0 else (1, distance - 1)
            at = lambda i: around[side, step, row % 4, i]
        for i in range(4):
            s = at(i)
            w = at(4 + i) + (4.0 * MIDDLE + shift)
            v = inside(distance) / w
            source1[row, i] = s
            weight1[row, i] = w
            inverse1[row, i] = v
            other[row, i] = v * s

    sweep(other, source1, inverse1, middle, MIDDLE, 26, 4, (1, 1, 1))

    pool = pooling(128, 128)
    spread = spreading(128, 128)
    lane = iota((8, 128), 1)

    means = []
    for pair in range(12):
        left, weights = [], []
        for row in (2 * pair + 2, 2 * pair + 3):
            rows = [take(middle, row + d) for d in (-1, 0, 1)]
            w = take(weight1, row)
            total = stencil(*rows)
            left.append(
                [s + (MIDDLE / 6.0) * t - x * u for s, t, x, u in zip(take(source1, row), total, w, rows[1])]
            )
            weights.append(w)
        means += cubes(*left) + cubes(*weights)
    small = times(jnp.concatenate(means, axis=0), pool)
    for pair in range(12):
        for i in range(2):
            s = small[32 * pair + 8 * i : 32 * pair + 8 * i + 8]
            w = small[32 * pair + 8 * i + 16 : 32 * pair + 8 * i + 24] + (4.0 * COARSE - 4.0 * MIDDLE)
            v = jnp.where(lane < 64, inside((pair + 1) // 2 - REACH) / jnp.where(lane < 64, w, 1.0), 0.0)
            source2[pair, i] = s
            inverse2[pair, i] = v
            coarse[pair, i] = v * s

    sweep(coarse, source2, inverse2, coarser, COARSE, 10, 10, (1, 1, 1), True)
    sweep(coarser, source2, inverse2, coarse, COARSE, 8, 8, (2, 2, 2), True)
    sweep(coarse, source2, inverse2, coarser, COARSE, 6, 6, (3, 3, 3), True)

    wide = times(jnp.concatenate([p for row in range(3, 9) for p in take(coarser, row)], axis=0), spread)
    for row in range(8, 20):
        for i in range(4):
            at = 16 * (row // 2 - 4) + 8 * (i // 2)
            other[row, i] = middle[row, i] + wide[at : at + 8]

    sweep(other, source1, inverse1, middle, MIDDLE, 8, 4, (10, 10, 10))
    sweep(middle, source1, inverse1, other, MIDDLE, 6, 6, (11, 11, 11))

    spread = spreading(128, 256)
    wide = times(jnp.concatenate([p for row in range(4) for p in take(other, 11 + 2 * c + row)], axis=0), spread)
    for row in range(8):
        for i in range(8):
            at = 32 * (row // 2) + 8 * (i // 2)
            work[row, i] = fine[row, i] + wide[at : at + 8]

    final = work.at[8:14]
    sweep(work, source, inverse, final, FINE, 6, 2, (0, 1, 2))
    for row in range(4):
        new = sweep_row(
            [take(final, row + d) for d in range(3)], take(source, row + 3), take(inverse, row + 3), FINE
        )
        for i, plane in enumerate(new):
            at = (i // 2) * 8 + (i % 2) * 4 + row
            for half in range(PZ):
                out[pl.ds(half * 32 + at, PX, stride=64), :] = plane[:, 128 * half : 128 * half + 128]


def unpack(blocks, out):
    for orbital in range(PX):
        for c in range(PZ):
            for i in range(8):
                base = (orbital * PZ + c) * 32 + (i // 2) * 8 + (i % 2) * 4
                out[orbital, i, 4 * c : 4 * c + 4] = blocks[base : base + 4]


def call(kernel, outs, scratch=(), anywhere=False, others=()):
    vmem = pl.BlockSpec(memory_space=pltpu.VMEM)

    def run(*args):
        return pl.pallas_call(
            kernel,
            out_shape=[(pltpu.VMEM if anywhere else jax.ShapeDtypeStruct)(shape, F32) for shape in outs],
            in_specs=[pl.BlockSpec(memory_space=pl.ANY) if anywhere else vmem] * len(args),
            out_specs=[vmem] * len(outs),
            scratch_shapes=[pltpu.VMEM(shape, F32) for shape in scratch] + list(others),
            compiler_params=pltpu.CompilerParams(vmem_limit_bytes=40 * 1024 * 1024),
        )(*args)

    return run


def run_begin(cores, beside):
    return call(begin, [(10, 8, 8, 256), (10, 4, 8, 256)], [(12, 8, 8, 256)])(cores, beside)


def run_down(*args):
    return call(
        down,
        [(8, 8, 8, 256), (10, 8, 8, 256), (2, 8, 8, 128)],
        [(10, 8, 8, 256)] * 2,
    )(*args)


def run_up(*args):
    return call(
        up,
        [(512, 128)],
        [(28, 4, 8, 128)] * 5 + [(12, 2, 8, 128)] * 4 + [(14, 8, 8, 256)],
    )(*args)[0]


def body(residual, potential, shifts):
    size_y = lax.axis_size("dom") // (PX * PZ)
    blocks = [(px, py, c) for px in range(PX) for py in range(size_y) for c in range(PZ)]
    lines = [
        [dom_of(px, py, c, size_y) for px in range(PX) for c in range(PZ)] for py in range(size_y)
    ]
    cores = [
        [dom_of(px, py, c, size_y) for c in range(PZ)] for px in range(PX) for py in range(size_y)
    ]

    def pairs(target, bands=False):
        found = [((px, py, c), target(px, py, c)) for px, py, c in blocks]
        found = [(dom_of(*a, size_y), dom_of(*b, size_y)) for a, b in found if 0 <= b[1] < size_y]
        return [(2 * a + n, 2 * b + 1 - n) for a, b in found for n in range(2)] if bands else found

    def swap_lines(value):
        return lax.all_to_all(value, "dom", 0, 0, axis_index_groups=lines, tiled=True)

    def to_beside(px, py, c):
        return (px, py - 1, 1) if c == 0 else (px, py + 1, 0)

    packed, shift = call(
        pack,
        [(768, 128), (8, 128)],
        [(8, 8, 8, 128), (4, 8, 128)],
        anywhere=True,
        others=[pltpu.SMEM((8,), F32), pltpu.SemaphoreType.DMA((PX + 2,))],
    )(*[pltpu.with_memory_space_constraint(x, pltpu.HBM) for x in (residual, potential, shifts)])
    own = swap_lines(packed)
    half = own.reshape(16, 48, 128)[:, 32:].reshape(256, 128)
    both = ("dom", "band")
    own_half = lax.ppermute(half, "band", [(0, 1), (1, 0)])
    given, half = call(cut_out, [(704, 128), (192, 128)])(own)
    beside = lax.ppermute(given, "dom", pairs(to_beside))
    beside_half = lax.ppermute(half, both, pairs(to_beside, True))
    of_cores = lax.all_gather(own, "dom", axis_index_groups=cores, axis=0)
    source, weights = run_begin(of_cores, beside)
    source, own_half = lax.optimization_barrier((source, own_half))
    of_cores_half = lax.all_gather(own_half, "dom", axis_index_groups=cores, axis=0)
    fine, inverse, cut = run_down(shift, source, weights, of_cores_half, beside_half)
    block = lax.all_gather(cut, "dom", axis_index_groups=cores, axis=0, tiled=True)
    sent = [
        lax.ppermute(
            block,
            "dom",
            pairs(lambda px, py, c, k=k: (px, py + k, 0) if c == 0 else (px, py - k, 1)),
        )
        for k in range(REACH, 0, -1)
    ]
    around = lax.all_gather(jnp.stack(sent[::-1]), "dom", axis_index_groups=cores, axis=0)
    final = run_up(shift, fine, source, inverse, block, around)
    (correction,) = call(unpack, [(8, 8, 8, 128)])(swap_lines(final))
    return correction


def solution(mesh):
    return jax.shard_map(
        body,
        mesh=mesh,
        in_specs=(P("band", "dom", None, None), P(("dom", "band"), None, None), P("band")),
        out_specs=P("band", "dom", None, None),
        check_vma=False,
    )
```

```python
import jax
import jax.numpy as jnp
from jax import lax
from jax.experimental import pallas as pl
from jax.experimental.pallas import tpu as pltpu
from jax.sharding import PartitionSpec as P


OMEGA = 0.7
KEEP = 0.3
FINE, MIDDLE, COARSE = 2.0, 0.5, 0.125
PX, PZ = 8, 2
REACH = 3
F32 = jnp.float32
BF16 = jnp.bfloat16


def place():
    position = lax.axis_index("dom")
    size_y = lax.axis_size("dom") // (PX * PZ)
    return position // (size_y * PZ), position // PZ % size_y, position % PZ


def dom_of(px, py, pz, size_y):
    return (px * size_y + py) * PZ + pz


def iota(shape, dimension):
    return lax.broadcasted_iota(jnp.int32, shape, dimension)


def along_x(planes):
    sublane = iota(planes[0].shape, 0)
    first = jnp.where(sublane == 0, 0.0, pltpu.roll(planes[-1], 1, 0))
    last = jnp.where(sublane == PX - 1, 0.0, pltpu.roll(planes[0], PX - 1, 0))
    below = [first] + planes[:-1]
    above = planes[1:] + [last]
    return [b + a for b, a in zip(below, above)]


def along_z(plane, open_end):
    width = plane.shape[1]
    left, right = pltpu.roll(plane, 1, 1), pltpu.roll(plane, width - 1, 1)
    if not open_end:
        lane = iota(plane.shape, 1)
        left = jnp.where(lane == 0, 0.0, left)
        right = jnp.where(lane == width - 1, 0.0, right)
    return left + right


def stencil(below, here, above, open_end=False):
    across = [a + b for a, b in zip(below, above)]
    wide = [a + (h + h) for a, h in zip(across, here)]
    turned = [e + w for e, w in zip(along_x(here), wide)]
    return [
        along_z(t, open_end) + (x + (a + a)) for t, x, a in zip(turned, along_x(wide), across)
    ]


def each(count, chunk, step):
    for base in range(0, count, chunk):
        step(base, min(chunk, count - base))


def take(ref, row):
    return [ref[row, i] for i in range(ref.shape[1])]


def sweep_row(rows, source, inverse, kinetic, open_end=False):
    total = stencil(*rows, open_end)
    return [
        KEEP * u + v * (s + (kinetic / 6.0) * t)
        for u, s, v, t in zip(rows[1], source, inverse, total)
    ]


def sweep(start, source, inverse, target, kinetic, count, chunk, offsets, open_end=False):
    to, of, at = offsets

    def step(base, rows):
        held = [take(start, base + (of + r - 1)) for r in range(rows + 2)]
        for r in range(rows):
            row = base + (at + r)
            new = sweep_row(held[r : r + 3], take(source, row), take(inverse, row), kinetic, open_end)
            for i, plane in enumerate(new):
                target[base + (to + r), i] = plane

    each(count, chunk, step)


def pooling(rows, columns):
    return jnp.where(iota((rows, columns), 0) // 2 == iota((rows, columns), 1), 0.5, 0.0).astype(F32)


def spreading(rows, columns):
    return jnp.where(iota((rows, columns), 0) == iota((rows, columns), 1) // 2, 1.0, 0.0).astype(F32)


def times(value, matrix):
    high = value.astype(BF16)
    rest = value - high.astype(F32)
    middle = rest.astype(BF16)
    low = (rest - middle.astype(F32)).astype(BF16)
    matrix = matrix.astype(BF16)
    parts = [jnp.dot(part, matrix, preferred_element_type=F32) for part in (high, middle, low)]
    return parts[0] + (parts[1] + parts[2])


def cubes(low, high):
    return [
        0.25 * ((low[2 * i] + low[2 * i + 1]) + (high[2 * i] + high[2 * i + 1]))
        for i in range(len(low) // 2)
    ]


def pack(residual, potential, shifts, out, shift, held, planes, numbers, arrived):
    copies = [
        pltpu.make_async_copy(potential, planes, arrived.at[PX]),
        pltpu.make_async_copy(shifts, numbers, arrived.at[PX + 1]),
    ]
    copies += [
        pltpu.make_async_copy(residual.at[i], held.at[i], arrived.at[i]) for i in range(PX)
    ]
    for copy in copies:
        copy.start()
    copies[0].wait()
    for c in range(PZ):
        for i in range(4):
            both = planes[i, 4 * c : 4 * c + 4]
            for orbital in range(PX):
                base = (orbital * PZ + c) * 48 + 32 + i
                out[pl.ds(base, 4, stride=4), :] = both
    copies[1].wait()
    shift[...] = jnp.full((8, 128), numbers[place()[0]], F32)
    for orbital in range(PX):
        copies[2 + orbital].wait()
        for c in range(PZ):
            base = (orbital * PZ + c) * 48
            for i in range(8):
                out[base + 4 * i : base + 4 * i + 4] = held[orbital, i, 4 * c : 4 * c + 4]


def cut_out(slab, out, weights):
    _, _, c = place()

    def rows(first):
        for piece in range(16):
            out[32 * piece : 32 * piece + 32] = slab[48 * piece : 48 * piece + 32]
            near = slab[48 * piece + 32 + first : 48 * piece + 44 + first]
            out[512 + 12 * piece : 524 + 12 * piece] = near
            weights[12 * piece : 12 * piece + 12] = near

    pl.when(c == 0)(lambda: rows(0))
    pl.when(c == 1)(lambda: rows(4))


def down(shifts, cores, beside, cores_half, beside_half, fine_out, source, inverse, cut, field, potential, start):
    px, py, c = place()
    size_y = lax.axis_size("dom") // (PX * PZ)
    shift = jnp.concatenate([shifts[...]] * 2, axis=1)
    band = lax.axis_index("band")

    def unpack(blocks, halves):
        for row in range(12):
            block, other_half = blocks[row // 4], halves[row // 4]
            apart = block is beside
            piece, stride = (32, 64) if apart else (48, 96)
            near = row % 4 - (apart and row < 4)
            for half in range(PZ):
                lanes = slice(128 * half, 128 * half + 128)
                for i in range(8):
                    at = piece * half + 4 * i + row % 4
                    field[row, i, :, lanes] = block[pl.ds(at, PX, stride=stride), :]
                if 1 <= row <= 10:
                    for i in range(4):
                        if apart:
                            at, other, steps = 512 + 12 * half + 4 * near + i, 12 * half + 4 * near + i, (24, 24)
                        else:
                            at, other, steps = 48 * half + 32 + 4 * near + i, 16 * half + 4 * near + i, (96, 32)
                        potential[row - 1, 4 * band + i, :, lanes] = block[pl.ds(at, PX, stride=steps[0]), :]
                        potential[row - 1, 4 * (1 - band) + i, :, lanes] = other_half[
                            pl.ds(other, PX, stride=steps[1]), :
                        ]

    here = (cores.at[0], cores.at[1])
    here_half = (cores_half.at[0], cores_half.at[1])
    pl.when(c == 0)(lambda: unpack((beside, *here), (beside_half, *here_half)))
    pl.when(c == 1)(lambda: unpack((*here, beside), (*here_half, beside_half)))

    def first(base, rows):
        for r in range(rows):
            row = base + r
            y = py * 8 + 4 * c + row - 3
            inside = jnp.where((y >= 0) & (y < 8 * size_y), OMEGA, 0.0).astype(F32)
            below, here, above = [take(field, row + d) for d in range(3)]
            for i, (b, h, a, x) in enumerate(zip(below, here, above, along_x(here))):
                s = 0.5 * h + ((b + a) + (x + along_z(h, False))) * (1.0 / 12.0)
                v = inside / (potential[row, i] + (4.0 * FINE + shift))
                source[row, i] = s
                inverse[row, i] = v
                start[row, i] = v * s

    each(10, 2, first)
    sweep(start, source, inverse, fine_out, FINE, 8, 2, (0, 1, 1))

    pool = pooling(256, 128)
    means = []
    for pair in range(2):
        left = []
        for row in (2 * pair, 2 * pair + 1):
            rows = [take(fine_out, row + d) for d in (1, 2, 3)]
            weight = [v + (4.0 * FINE + shift) for v in take(potential, row + 3)]
            total = stencil(*rows)
            left.append(
                [s + (FINE / 6.0) * t - w * u for s, t, w, u in zip(take(source, row + 3), total, weight, rows[1])]
            )
        means += cubes(*left) + cubes(take(potential, 2 * pair + 3), take(potential, 2 * pair + 4))
    small = times(jnp.concatenate(means, axis=0), pool)
    for pair in range(2):
        for i in range(8):
            cut[pair, i] = small[64 * pair + 8 * i : 64 * pair + 8 * i + 8]


def up(shifts, fine, source, inverse, block, around, out, weight1, source1, inverse1, middle, other, source2, inverse2, coarse, coarser, work):
    px, py, c = place()
    size_y = lax.axis_size("dom") // (PX * PZ)
    shift = shifts[...]

    def inside(distance):
        return jnp.where((py + distance >= 0) & (py + distance < size_y), OMEGA, 0.0).astype(F32)

    for row in range(28):
        distance = row // 4 - REACH
        if distance == 0:
            at = lambda i: block[row % 4, i]
        else:
            side, step = (0, -distance - 1) if distance < 0 else (1, distance - 1)
            at = lambda i: around[side, step, row % 4, i]
        for i in range(4):
            s = at(i)
            w = at(4 + i) + (4.0 * MIDDLE + shift)
            v = inside(distance) / w
            source1[row, i] = s
            weight1[row, i] = w
            inverse1[row, i] = v
            other[row, i] = v * s

    sweep(other, source1, inverse1, middle, MIDDLE, 26, 4, (1, 1, 1))

    pool = pooling(128, 128)
    spread = spreading(128, 128)
    lane = iota((8, 128), 1)

    means = []
    for pair in range(12):
        left, weights = [], []
        for row in (2 * pair + 2, 2 * pair + 3):
            rows = [take(middle, row + d) for d in (-1, 0, 1)]
            w = take(weight1, row)
            total = stencil(*rows)
            left.append(
                [s + (MIDDLE / 6.0) * t - x * u for s, t, x, u in zip(take(source1, row), total, w, rows[1])]
            )
            weights.append(w)
        means += cubes(*left) + cubes(*weights)
    small = times(jnp.concatenate(means, axis=0), pool)
    for pair in range(12):
        for i in range(2):
            s = small[32 * pair + 8 * i : 32 * pair + 8 * i + 8]
            w = small[32 * pair + 8 * i + 16 : 32 * pair + 8 * i + 24] + (4.0 * COARSE - 4.0 * MIDDLE)
            v = jnp.where(lane < 64, inside((pair + 1) // 2 - REACH) / jnp.where(lane < 64, w, 1.0), 0.0)
            source2[pair, i] = s
            inverse2[pair, i] = v
            coarse[pair, i] = v * s

    sweep(coarse, source2, inverse2, coarser, COARSE, 10, 10, (1, 1, 1), True)
    sweep(coarser, source2, inverse2, coarse, COARSE, 8, 8, (2, 2, 2), True)
    sweep(coarse, source2, inverse2, coarser, COARSE, 6, 6, (3, 3, 3), True)

    wide = times(jnp.concatenate([p for row in range(3, 9) for p in take(coarser, row)], axis=0), spread)
    for row in range(8, 20):
        for i in range(4):
            at = 16 * (row // 2 - 4) + 8 * (i // 2)
            other[row, i] = middle[row, i] + wide[at : at + 8]

    sweep(other, source1, inverse1, middle, MIDDLE, 8, 4, (10, 10, 10))
    sweep(middle, source1, inverse1, other, MIDDLE, 6, 6, (11, 11, 11))

    spread = spreading(128, 256)
    wide = times(jnp.concatenate([p for row in range(4) for p in take(other, 11 + 2 * c + row)], axis=0), spread)
    for row in range(8):
        for i in range(8):
            at = 32 * (row // 2) + 8 * (i // 2)
            work[row, i] = fine[row, i] + wide[at : at + 8]

    final = work.at[8:14]
    sweep(work, source, inverse, final, FINE, 6, 2, (0, 1, 2))
    for row in range(4):
        new = sweep_row(
            [take(final, row + d) for d in range(3)], take(source, row + 3), take(inverse, row + 3), FINE
        )
        for i, plane in enumerate(new):
            at = (i // 2) * 8 + (i % 2) * 4 + row
            for half in range(PZ):
                out[pl.ds(half * 32 + at, PX, stride=64), :] = plane[:, 128 * half : 128 * half + 128]


def unpack(blocks, out):
    for orbital in range(PX):
        for c in range(PZ):
            for i in range(8):
                base = (orbital * PZ + c) * 32 + (i // 2) * 8 + (i % 2) * 4
                out[orbital, i, 4 * c : 4 * c + 4] = blocks[base : base + 4]


def call(kernel, outs, scratch=(), anywhere=False, others=()):
    vmem = pl.BlockSpec(memory_space=pltpu.VMEM)

    def run(*args):
        return pl.pallas_call(
            kernel,
            out_shape=[(pltpu.VMEM if anywhere else jax.ShapeDtypeStruct)(shape, F32) for shape in outs],
            in_specs=[pl.BlockSpec(memory_space=pl.ANY) if anywhere else vmem] * len(args),
            out_specs=[vmem] * len(outs),
            scratch_shapes=[pltpu.VMEM(shape, F32) for shape in scratch] + list(others),
            compiler_params=pltpu.CompilerParams(vmem_limit_bytes=40 * 1024 * 1024),
        )(*args)

    return run


def run_down(*args):
    return call(
        down,
        [(8, 8, 8, 256), (10, 8, 8, 256), (10, 8, 8, 256), (2, 8, 8, 128)],
        [(12, 8, 8, 256)] + [(10, 8, 8, 256)] * 2,
    )(*args)


def run_up(*args):
    return call(
        up,
        [(512, 128)],
        [(28, 4, 8, 128)] * 5 + [(12, 2, 8, 128)] * 4 + [(14, 8, 8, 256)],
    )(*args)[0]


def body(residual, potential, shifts):
    size_y = lax.axis_size("dom") // (PX * PZ)
    blocks = [(px, py, c) for px in range(PX) for py in range(size_y) for c in range(PZ)]
    lines = [
        [dom_of(px, py, c, size_y) for px in range(PX) for c in range(PZ)] for py in range(size_y)
    ]
    cores = [
        [dom_of(px, py, c, size_y) for c in range(PZ)] for px in range(PX) for py in range(size_y)
    ]

    def pairs(target, bands=False):
        found = [((px, py, c), target(px, py, c)) for px, py, c in blocks]
        found = [(dom_of(*a, size_y), dom_of(*b, size_y)) for a, b in found if 0 <= b[1] < size_y]
        return [(2 * a + n, 2 * b + 1 - n) for a, b in found for n in range(2)] if bands else found

    def swap_lines(value):
        return lax.all_to_all(value, "dom", 0, 0, axis_index_groups=lines, tiled=True)

    def to_beside(px, py, c):
        return (px, py - 1, 1) if c == 0 else (px, py + 1, 0)

    packed, shift = call(
        pack,
        [(768, 128), (8, 128)],
        [(8, 8, 8, 128), (4, 8, 128)],
        anywhere=True,
        others=[pltpu.SMEM((8,), F32), pltpu.SemaphoreType.DMA((PX + 2,))],
    )(*[pltpu.with_memory_space_constraint(x, pltpu.HBM) for x in (residual, potential, shifts)])
    own = swap_lines(packed)
    half = own.reshape(16, 48, 128)[:, 32:].reshape(256, 128)
    both = ("dom", "band")
    own_half = lax.ppermute(half, "band", [(0, 1), (1, 0)])
    given, half = call(cut_out, [(704, 128), (192, 128)])(own)
    beside = lax.ppermute(given, "dom", pairs(to_beside))
    beside_half = lax.ppermute(half, both, pairs(to_beside, True))
    of_cores = lax.all_gather(own, "dom", axis_index_groups=cores, axis=0)
    of_cores_half = lax.all_gather(own_half, "dom", axis_index_groups=cores, axis=0)
    fine, source, inverse, cut = run_down(shift, of_cores, beside, of_cores_half, beside_half)
    block = lax.all_gather(cut, "dom", axis_index_groups=cores, axis=0, tiled=True)
    sent = [
        lax.ppermute(
            block,
            "dom",
            pairs(lambda px, py, c, k=k: (px, py + k, 0) if c == 0 else (px, py - k, 1)),
        )
        for k in (3, 1, 2)
    ]
    around = lax.all_gather(jnp.stack([sent[1], sent[2], sent[0]]), "dom", axis_index_groups=cores, axis=0)
    final = run_up(shift, fine, source, inverse, block, around)
    (correction,) = call(unpack, [(8, 8, 8, 128)])(swap_lines(final))
    return correction


def solution(mesh):
    return jax.shard_map(
        body,
        mesh=mesh,
        in_specs=(P("band", "dom", None, None), P(("dom", "band"), None, None), P("band")),
        out_specs=P("band", "dom", None, None),
        check_vma=False,
    )
```

```python
import jax
import jax.numpy as jnp
from jax import lax
from jax.experimental import pallas as pl
from jax.experimental.pallas import tpu as pltpu
from jax.sharding import PartitionSpec as P


OMEGA = 0.7
KEEP = 0.3
FINE, MIDDLE, COARSE = 2.0, 0.5, 0.125
PX, PZ = 8, 2
REACH = 3
F32 = jnp.float32
BF16 = jnp.bfloat16


def place():
    position = lax.axis_index("dom")
    size_y = lax.axis_size("dom") // (PX * PZ)
    return position // (size_y * PZ), position // PZ % size_y, position % PZ


def dom_of(px, py, pz, size_y):
    return (px * size_y + py) * PZ + pz


def iota(shape, dimension):
    return lax.broadcasted_iota(jnp.int32, shape, dimension)


def along_x(planes):
    sublane = iota(planes[0].shape, 0)
    first = jnp.where(sublane == 0, 0.0, pltpu.roll(planes[-1], 1, 0))
    last = jnp.where(sublane == PX - 1, 0.0, pltpu.roll(planes[0], PX - 1, 0))
    below = [first] + planes[:-1]
    above = planes[1:] + [last]
    return [b + a for b, a in zip(below, above)]


def along_z(plane, open_end):
    width = plane.shape[1]
    left, right = pltpu.roll(plane, 1, 1), pltpu.roll(plane, width - 1, 1)
    if not open_end:
        lane = iota(plane.shape, 1)
        left = jnp.where(lane == 0, 0.0, left)
        right = jnp.where(lane == width - 1, 0.0, right)
    return left + right


def stencil(below, here, above, open_end=False):
    across = [a + b for a, b in zip(below, above)]
    wide = [a + (h + h) for a, h in zip(across, here)]
    turned = [e + w for e, w in zip(along_x(here), wide)]
    return [
        along_z(t, open_end) + (x + (a + a)) for t, x, a in zip(turned, along_x(wide), across)
    ]


def each(count, chunk, step):
    for base in range(0, count, chunk):
        step(base, min(chunk, count - base))


def take(ref, row):
    return [ref[row, i] for i in range(ref.shape[1])]


def sweep_row(rows, source, inverse, kinetic, open_end=False):
    total = stencil(*rows, open_end)
    return [
        KEEP * u + v * (s + (kinetic / 6.0) * t)
        for u, s, v, t in zip(rows[1], source, inverse, total)
    ]


def sweep(start, source, inverse, target, kinetic, count, chunk, offsets, open_end=False):
    to, of, at = offsets

    def step(base, rows):
        held = [take(start, base + (of + r - 1)) for r in range(rows + 2)]
        for r in range(rows):
            row = base + (at + r)
            new = sweep_row(held[r : r + 3], take(source, row), take(inverse, row), kinetic, open_end)
            for i, plane in enumerate(new):
                target[base + (to + r), i] = plane

    each(count, chunk, step)


def pooling(rows, columns):
    return jnp.where(iota((rows, columns), 0) // 2 == iota((rows, columns), 1), 0.5, 0.0).astype(F32)


def spreading(rows, columns):
    return jnp.where(iota((rows, columns), 0) == iota((rows, columns), 1) // 2, 1.0, 0.0).astype(F32)


def times(value, matrix):
    high = value.astype(BF16)
    rest = value - high.astype(F32)
    middle = rest.astype(BF16)
    low = (rest - middle.astype(F32)).astype(BF16)
    matrix = matrix.astype(BF16)
    parts = [jnp.dot(part, matrix, preferred_element_type=F32) for part in (high, middle, low)]
    return parts[0] + (parts[1] + parts[2])


def cubes(low, high):
    return [
        0.25 * ((low[2 * i] + low[2 * i + 1]) + (high[2 * i] + high[2 * i + 1]))
        for i in range(len(low) // 2)
    ]


def pack(residual, potential, shifts, out, shift, held, planes, numbers, arrived):
    copies = [
        pltpu.make_async_copy(potential, planes, arrived.at[PX]),
        pltpu.make_async_copy(shifts, numbers, arrived.at[PX + 1]),
    ]
    copies += [
        pltpu.make_async_copy(residual.at[i], held.at[i], arrived.at[i]) for i in range(PX)
    ]
    for copy in copies:
        copy.start()
    copies[0].wait()
    for c in range(PZ):
        for i in range(4):
            both = planes[i, 4 * c : 4 * c + 4]
            for orbital in range(PX):
                base = (orbital * PZ + c) * 48 + 32 + i
                out[pl.ds(base, 4, stride=4), :] = both
    copies[1].wait()
    shift[...] = jnp.full((8, 128), numbers[place()[0]], F32)
    for orbital in range(PX):
        copies[2 + orbital].wait()
        for c in range(PZ):
            base = (orbital * PZ + c) * 48
            for i in range(8):
                out[base + 4 * i : base + 4 * i + 4] = held[orbital, i, 4 * c : 4 * c + 4]


def cut_out(slab, out, weights):
    _, _, c = place()

    def rows(first):
        for piece in range(16):
            out[32 * piece : 32 * piece + 32] = slab[48 * piece : 48 * piece + 32]
            near = slab[48 * piece + 32 + first : 48 * piece + 44 + first]
            out[512 + 12 * piece : 524 + 12 * piece] = near
            weights[12 * piece : 12 * piece + 12] = near

    pl.when(c == 0)(lambda: rows(0))
    pl.when(c == 1)(lambda: rows(4))


def down(shifts, cores, beside, cores_half, beside_half, fine_out, source, inverse, cut, field, potential, start):
    px, py, c = place()
    size_y = lax.axis_size("dom") // (PX * PZ)
    shift = jnp.concatenate([shifts[...]] * 2, axis=1)
    band = lax.axis_index("band")

    def unpack(blocks, halves):
        for row in range(12):
            block, other_half = blocks[row // 4], halves[row // 4]
            apart = block is beside
            piece, stride = (32, 64) if apart else (48, 96)
            near = row % 4 - (apart and row < 4)
            for half in range(PZ):
                lanes = slice(128 * half, 128 * half + 128)
                for i in range(8):
                    at = piece * half + 4 * i + row % 4
                    field[row, i, :, lanes] = block[pl.ds(at, PX, stride=stride), :]
                if 1 <= row <= 10:
                    for i in range(4):
                        if apart:
                            at, other, steps = 512 + 12 * half + 4 * near + i, 12 * half + 4 * near + i, (24, 24)
                        else:
                            at, other, steps = 48 * half + 32 + 4 * near + i, 16 * half + 4 * near + i, (96, 32)
                        potential[row - 1, 4 * band + i, :, lanes] = block[pl.ds(at, PX, stride=steps[0]), :]
                        potential[row - 1, 4 * (1 - band) + i, :, lanes] = other_half[
                            pl.ds(other, PX, stride=steps[1]), :
                        ]

    here = (cores.at[0], cores.at[1])
    here_half = (cores_half.at[0], cores_half.at[1])
    pl.when(c == 0)(lambda: unpack((beside, *here), (beside_half, *here_half)))
    pl.when(c == 1)(lambda: unpack((*here, beside), (*here_half, beside_half)))

    def first(base, rows):
        for r in range(rows):
            row = base + r
            y = py * 8 + 4 * c + row - 3
            inside = jnp.where((y >= 0) & (y < 8 * size_y), OMEGA, 0.0).astype(F32)
            below, here, above = [take(field, row + d) for d in range(3)]
            for i, (b, h, a, x) in enumerate(zip(below, here, above, along_x(here))):
                s = 0.5 * h + ((b + a) + (x + along_z(h, False))) * (1.0 / 12.0)
                v = inside / (potential[row, i] + (4.0 * FINE + shift))
                source[row, i] = s
                inverse[row, i] = v
                start[row, i] = v * s

    each(10, 2, first)
    sweep(start, source, inverse, fine_out, FINE, 8, 4, (0, 1, 1))

    pool = pooling(256, 128)
    means = []
    for pair in range(2):
        left = []
        for row in (2 * pair, 2 * pair + 1):
            rows = [take(fine_out, row + d) for d in (1, 2, 3)]
            weight = [v + (4.0 * FINE + shift) for v in take(potential, row + 3)]
            total = stencil(*rows)
            left.append(
                [s + (FINE / 6.0) * t - w * u for s, t, w, u in zip(take(source, row + 3), total, weight, rows[1])]
            )
        means += cubes(*left) + cubes(take(potential, 2 * pair + 3), take(potential, 2 * pair + 4))
    small = times(jnp.concatenate(means, axis=0), pool)
    for pair in range(2):
        for i in range(8):
            cut[pair, i] = small[64 * pair + 8 * i : 64 * pair + 8 * i + 8]


def up(shifts, fine, source, inverse, block, around, out, weight1, source1, inverse1, middle, other, source2, inverse2, coarse, coarser, work):
    px, py, c = place()
    size_y = lax.axis_size("dom") // (PX * PZ)
    shift = shifts[...]

    def inside(distance):
        return jnp.where((py + distance >= 0) & (py + distance < size_y), OMEGA, 0.0).astype(F32)

    for row in range(28):
        distance = row // 4 - REACH
        if distance == 0:
            at = lambda i: block[row % 4, i]
        else:
            side, step = (0, -distance - 1) if distance < 0 else (1, distance - 1)
            at = lambda i: around[side, step, row % 4, i]
        for i in range(4):
            s = at(i)
            w = at(4 + i) + (4.0 * MIDDLE + shift)
            v = inside(distance) / w
            source1[row, i] = s
            weight1[row, i] = w
            inverse1[row, i] = v
            other[row, i] = v * s

    sweep(other, source1, inverse1, middle, MIDDLE, 26, 13, (1, 1, 1))

    pool = pooling(128, 128)
    spread = spreading(128, 128)
    lane = iota((8, 128), 1)

    means = []
    for pair in range(12):
        left, weights = [], []
        for row in (2 * pair + 2, 2 * pair + 3):
            rows = [take(middle, row + d) for d in (-1, 0, 1)]
            w = take(weight1, row)
            total = stencil(*rows)
            left.append(
                [s + (MIDDLE / 6.0) * t - x * u for s, t, x, u in zip(take(source1, row), total, w, rows[1])]
            )
            weights.append(w)
        means += cubes(*left) + cubes(*weights)
    small = times(jnp.concatenate(means, axis=0), pool)
    for pair in range(12):
        for i in range(2):
            s = small[32 * pair + 8 * i : 32 * pair + 8 * i + 8]
            w = small[32 * pair + 8 * i + 16 : 32 * pair + 8 * i + 24] + (4.0 * COARSE - 4.0 * MIDDLE)
            v = jnp.where(lane < 64, inside((pair + 1) // 2 - REACH) / jnp.where(lane < 64, w, 1.0), 0.0)
            source2[pair, i] = s
            inverse2[pair, i] = v
            coarse[pair, i] = v * s

    sweep(coarse, source2, inverse2, coarser, COARSE, 10, 10, (1, 1, 1), True)
    sweep(coarser, source2, inverse2, coarse, COARSE, 8, 8, (2, 2, 2), True)
    sweep(coarse, source2, inverse2, coarser, COARSE, 6, 6, (3, 3, 3), True)

    wide = times(jnp.concatenate([p for row in range(3, 9) for p in take(coarser, row)], axis=0), spread)
    for row in range(8, 20):
        for i in range(4):
            at = 16 * (row // 2 - 4) + 8 * (i // 2)
            other[row, i] = middle[row, i] + wide[at : at + 8]

    sweep(other, source1, inverse1, middle, MIDDLE, 8, 4, (10, 10, 10))
    sweep(middle, source1, inverse1, other, MIDDLE, 6, 6, (11, 11, 11))

    spread = spreading(128, 256)
    wide = times(jnp.concatenate([p for row in range(4) for p in take(other, 11 + 2 * c + row)], axis=0), spread)
    for row in range(8):
        for i in range(8):
            at = 32 * (row // 2) + 8 * (i // 2)
            work[row, i] = fine[row, i] + wide[at : at + 8]

    final = work.at[8:14]
    sweep(work, source, inverse, final, FINE, 6, 3, (0, 1, 2))
    for row in range(4):
        new = sweep_row(
            [take(final, row + d) for d in range(3)], take(source, row + 3), take(inverse, row + 3), FINE
        )
        for i, plane in enumerate(new):
            at = (i // 2) * 8 + (i % 2) * 4 + row
            for half in range(PZ):
                out[pl.ds(half * 32 + at, PX, stride=64), :] = plane[:, 128 * half : 128 * half + 128]


def unpack(blocks, out):
    for orbital in range(PX):
        for c in range(PZ):
            for i in range(8):
                base = (orbital * PZ + c) * 32 + (i // 2) * 8 + (i % 2) * 4
                out[orbital, i, 4 * c : 4 * c + 4] = blocks[base : base + 4]


def call(kernel, outs, scratch=(), anywhere=False, others=()):
    vmem = pl.BlockSpec(memory_space=pltpu.VMEM)

    def run(*args):
        return pl.pallas_call(
            kernel,
            out_shape=[(pltpu.VMEM if anywhere else jax.ShapeDtypeStruct)(shape, F32) for shape in outs],
            in_specs=[pl.BlockSpec(memory_space=pl.ANY) if anywhere else vmem] * len(args),
            out_specs=[vmem] * len(outs),
            scratch_shapes=[pltpu.VMEM(shape, F32) for shape in scratch] + list(others),
            compiler_params=pltpu.CompilerParams(vmem_limit_bytes=40 * 1024 * 1024),
        )(*args)

    return run


def run_down(*args):
    return call(
        down,
        [(8, 8, 8, 256), (10, 8, 8, 256), (10, 8, 8, 256), (2, 8, 8, 128)],
        [(12, 8, 8, 256)] + [(10, 8, 8, 256)] * 2,
    )(*args)


def run_up(*args):
    return call(
        up,
        [(512, 128)],
        [(28, 4, 8, 128)] * 5 + [(12, 2, 8, 128)] * 4 + [(14, 8, 8, 256)],
    )(*args)[0]


def body(residual, potential, shifts):
    size_y = lax.axis_size("dom") // (PX * PZ)
    blocks = [(px, py, c) for px in range(PX) for py in range(size_y) for c in range(PZ)]
    lines = [
        [dom_of(px, py, c, size_y) for px in range(PX) for c in range(PZ)] for py in range(size_y)
    ]
    cores = [
        [dom_of(px, py, c, size_y) for c in range(PZ)] for px in range(PX) for py in range(size_y)
    ]

    def pairs(target, bands=False):
        found = [((px, py, c), target(px, py, c)) for px, py, c in blocks]
        found = [(dom_of(*a, size_y), dom_of(*b, size_y)) for a, b in found if 0 <= b[1] < size_y]
        return [(2 * a + n, 2 * b + 1 - n) for a, b in found for n in range(2)] if bands else found

    def swap_lines(value):
        return lax.all_to_all(value, "dom", 0, 0, axis_index_groups=lines, tiled=True)

    def to_beside(px, py, c):
        return (px, py - 1, 1) if c == 0 else (px, py + 1, 0)

    packed, shift = call(
        pack,
        [(768, 128), (8, 128)],
        [(8, 8, 8, 128), (4, 8, 128)],
        anywhere=True,
        others=[pltpu.SMEM((8,), F32), pltpu.SemaphoreType.DMA((PX + 2,))],
    )(*[pltpu.with_memory_space_constraint(x, pltpu.HBM) for x in (residual, potential, shifts)])
    own = swap_lines(packed)
    half = own.reshape(16, 48, 128)[:, 32:].reshape(256, 128)
    both = ("dom", "band")
    own_half = lax.ppermute(half, "band", [(0, 1), (1, 0)])
    given, half = call(cut_out, [(704, 128), (192, 128)])(own)
    beside = lax.ppermute(given, "dom", pairs(to_beside))
    beside_half = lax.ppermute(half, both, pairs(to_beside, True))
    of_cores = lax.all_gather(own, "dom", axis_index_groups=cores, axis=0)
    of_cores_half = lax.all_gather(own_half, "dom", axis_index_groups=cores, axis=0)
    fine, source, inverse, cut = run_down(shift, of_cores, beside, of_cores_half, beside_half)
    block = lax.all_gather(cut, "dom", axis_index_groups=cores, axis=0, tiled=True)
    sent = [
        lax.ppermute(
            block,
            "dom",
            pairs(lambda px, py, c, k=k: (px, py + k, 0) if c == 0 else (px, py - k, 1)),
        )
        for k in range(REACH, 0, -1)
    ]
    around = lax.all_gather(jnp.stack(sent[::-1]), "dom", axis_index_groups=cores, axis=0)
    final = run_up(shift, fine, source, inverse, block, around)
    (correction,) = call(unpack, [(8, 8, 8, 128)])(swap_lines(final))
    return correction


def solution(mesh):
    return jax.shard_map(
        body,
        mesh=mesh,
        in_specs=(P("band", "dom", None, None), P(("dom", "band"), None, None), P("band")),
        out_specs=P("band", "dom", None, None),
        check_vma=False,
    )
```

```python
import jax
import jax.numpy as jnp
from jax import lax
from jax.experimental import pallas as pl
from jax.experimental.pallas import tpu as pltpu
from jax.sharding import PartitionSpec as P


OMEGA = 0.7
KEEP = 0.3
FINE, MIDDLE, COARSE = 2.0, 0.5, 0.125
PX, PZ = 8, 2
REACH = 3
F32 = jnp.float32
BF16 = jnp.bfloat16


def place():
    position = lax.axis_index("dom")
    size_y = lax.axis_size("dom") // (PX * PZ)
    return position // (size_y * PZ), position // PZ % size_y, position % PZ


def dom_of(px, py, pz, size_y):
    return (px * size_y + py) * PZ + pz


def iota(shape, dimension):
    return lax.broadcasted_iota(jnp.int32, shape, dimension)


def along_x(planes):
    sublane = iota(planes[0].shape, 0)
    first = jnp.where(sublane == 0, 0.0, pltpu.roll(planes[-1], 1, 0))
    last = jnp.where(sublane == PX - 1, 0.0, pltpu.roll(planes[0], PX - 1, 0))
    below = [first] + planes[:-1]
    above = planes[1:] + [last]
    return [b + a for b, a in zip(below, above)]


def along_z(plane, open_end):
    width = plane.shape[1]
    left, right = pltpu.roll(plane, 1, 1), pltpu.roll(plane, width - 1, 1)
    if not open_end:
        lane = iota(plane.shape, 1)
        left = jnp.where(lane == 0, 0.0, left)
        right = jnp.where(lane == width - 1, 0.0, right)
    return left + right


def stencil(below, here, above, open_end=False):
    across = [a + b for a, b in zip(below, above)]
    wide = [a + (h + h) for a, h in zip(across, here)]
    turned = [e + w for e, w in zip(along_x(here), wide)]
    return [
        along_z(t, open_end) + (x + (a + a)) for t, x, a in zip(turned, along_x(wide), across)
    ]


def each(count, chunk, step):
    for base in range(0, count, chunk):
        step(base, min(chunk, count - base))


def take(ref, row):
    return [ref[row, i] for i in range(ref.shape[1])]


def sweep_row(rows, source, inverse, kinetic, open_end=False):
    total = stencil(*rows, open_end)
    return [
        KEEP * u + v * (s + (kinetic / 6.0) * t)
        for u, s, v, t in zip(rows[1], source, inverse, total)
    ]


def sweep(start, source, inverse, target, kinetic, count, chunk, offsets, open_end=False):
    to, of, at = offsets

    def step(base, rows):
        held = [take(start, base + (of + r - 1)) for r in range(rows + 2)]
        for r in range(rows):
            row = base + (at + r)
            new = sweep_row(held[r : r + 3], take(source, row), take(inverse, row), kinetic, open_end)
            for i, plane in enumerate(new):
                target[base + (to + r), i] = plane

    each(count, chunk, step)


def pooling(rows, columns):
    return jnp.where(iota((rows, columns), 0) // 2 == iota((rows, columns), 1), 0.5, 0.0).astype(F32)


def spreading(rows, columns):
    return jnp.where(iota((rows, columns), 0) == iota((rows, columns), 1) // 2, 1.0, 0.0).astype(F32)


def times(value, matrix):
    high = value.astype(BF16)
    rest = value - high.astype(F32)
    middle = rest.astype(BF16)
    low = (rest - middle.astype(F32)).astype(BF16)
    matrix = matrix.astype(BF16)
    parts = [jnp.dot(part, matrix, preferred_element_type=F32) for part in (high, middle, low)]
    return parts[0] + (parts[1] + parts[2])


def cubes(low, high):
    return [
        0.25 * ((low[2 * i] + low[2 * i + 1]) + (high[2 * i] + high[2 * i + 1]))
        for i in range(len(low) // 2)
    ]


def pack(residual, potential, shifts, out, shift, held, planes, numbers, arrived):
    copies = [
        pltpu.make_async_copy(potential, planes, arrived.at[PX]),
        pltpu.make_async_copy(shifts, numbers, arrived.at[PX + 1]),
    ]
    copies += [
        pltpu.make_async_copy(residual.at[i], held.at[i], arrived.at[i]) for i in range(PX)
    ]
    for copy in copies:
        copy.start()
    copies[0].wait()
    for c in range(PZ):
        for i in range(4):
            both = planes[i, 4 * c : 4 * c + 4]
            for orbital in range(PX):
                base = (orbital * PZ + c) * 48 + 32 + i
                out[pl.ds(base, 4, stride=4), :] = both
    copies[1].wait()
    shift[...] = jnp.full((8, 128), numbers[place()[0]], F32)
    for orbital in range(PX):
        copies[2 + orbital].wait()
        for c in range(PZ):
            base = (orbital * PZ + c) * 48
            for i in range(8):
                out[base + 4 * i : base + 4 * i + 4] = held[orbital, i, 4 * c : 4 * c + 4]


def cut_out(slab, out, weights):
    _, _, c = place()

    def rows(first):
        for piece in range(16):
            out[32 * piece : 32 * piece + 32] = slab[48 * piece : 48 * piece + 32]
            near = slab[48 * piece + 32 + first : 48 * piece + 44 + first]
            out[512 + 12 * piece : 524 + 12 * piece] = near
            weights[12 * piece : 12 * piece + 12] = near

    pl.when(c == 0)(lambda: rows(0))
    pl.when(c == 1)(lambda: rows(4))


def down(shifts, cores, beside, cores_half, beside_half, fine_out, source, inverse, cut, field, potential, start):
    px, py, c = place()
    size_y = lax.axis_size("dom") // (PX * PZ)
    shift = jnp.concatenate([shifts[...]] * 2, axis=1)
    band = lax.axis_index("band")

    def unpack(blocks, halves):
        for row in range(12):
            block, other_half = blocks[row // 4], halves[row // 4]
            apart = block is beside
            piece, stride = (32, 64) if apart else (48, 96)
            near = row % 4 - (apart and row < 4)
            for half in range(PZ):
                lanes = slice(128 * half, 128 * half + 128)
                for i in range(8):
                    at = piece * half + 4 * i + row % 4
                    field[row, i, :, lanes] = block[pl.ds(at, PX, stride=stride), :]
                if 1 <= row <= 10:
                    for i in range(4):
                        if apart:
                            at, other, steps = 512 + 12 * half + 4 * near + i, 12 * half + 4 * near + i, (24, 24)
                        else:
                            at, other, steps = 48 * half + 32 + 4 * near + i, 16 * half + 4 * near + i, (96, 32)
                        potential[row - 1, 4 * band + i, :, lanes] = block[pl.ds(at, PX, stride=steps[0]), :]
                        potential[row - 1, 4 * (1 - band) + i, :, lanes] = other_half[
                            pl.ds(other, PX, stride=steps[1]), :
                        ]

    here = (cores.at[0], cores.at[1])
    here_half = (cores_half.at[0], cores_half.at[1])
    pl.when(c == 0)(lambda: unpack((beside, *here), (beside_half, *here_half)))
    pl.when(c == 1)(lambda: unpack((*here, beside), (*here_half, beside_half)))

    def first(base, rows):
        for r in range(rows):
            row = base + r
            y = py * 8 + 4 * c + row - 3
            inside = jnp.where((y >= 0) & (y < 8 * size_y), OMEGA, 0.0).astype(F32)
            below, here, above = [take(field, row + d) for d in range(3)]
            for i, (b, h, a, x) in enumerate(zip(below, here, above, along_x(here))):
                s = 0.5 * h + ((b + a) + (x + along_z(h, False))) * (1.0 / 12.0)
                v = inside / (potential[row, i] + (4.0 * FINE + shift))
                source[row, i] = s
                inverse[row, i] = v
                start[row, i] = v * s

    each(10, 2, first)
    sweep(start, source, inverse, fine_out, FINE, 8, 2, (0, 1, 1))

    pool = pooling(256, 128)
    means = []
    for pair in range(2):
        left = []
        for row in (2 * pair, 2 * pair + 1):
            rows = [take(fine_out, row + d) for d in (1, 2, 3)]
            weight = [v + (4.0 * FINE + shift) for v in take(potential, row + 3)]
            total = stencil(*rows)
            left.append(
                [s + (FINE / 6.0) * t - w * u for s, t, w, u in zip(take(source, row + 3), total, weight, rows[1])]
            )
        means += cubes(*left) + cubes(take(potential, 2 * pair + 3), take(potential, 2 * pair + 4))
    small = times(jnp.concatenate(means, axis=0), pool)
    for pair in range(2):
        for i in range(8):
            cut[pair, i] = small[64 * pair + 8 * i : 64 * pair + 8 * i + 8]


def up(shifts, fine, source, inverse, block, around, out, weight1, source1, inverse1, middle, other, source2, inverse2, coarse, coarser, work):
    px, py, c = place()
    size_y = lax.axis_size("dom") // (PX * PZ)
    shift = shifts[...]

    def inside(distance):
        return jnp.where((py + distance >= 0) & (py + distance < size_y), OMEGA, 0.0).astype(F32)

    for row in range(28):
        distance = row // 4 - REACH
        if distance == 0:
            at = lambda i: block[row % 4, i]
        else:
            side, step = (0, -distance - 1) if distance < 0 else (1, distance - 1)
            at = lambda i: around[side, step, row % 4, i]
        for i in range(4):
            s = at(i)
            w = at(4 + i) + (4.0 * MIDDLE + shift)
            v = inside(distance) / w
            source1[row, i] = s
            weight1[row, i] = w
            inverse1[row, i] = v
            other[row, i] = v * s

    sweep(other, source1, inverse1, middle, MIDDLE, 26, 4, (1, 1, 1))

    pool = pooling(128, 128)
    spread = spreading(128, 128)
    lane = iota((8, 128), 1)

    means = []
    for pair in range(12):
        left, weights = [], []
        for row in (2 * pair + 2, 2 * pair + 3):
            rows = [take(middle, row + d) for d in (-1, 0, 1)]
            w = take(weight1, row)
            total = stencil(*rows)
            left.append(
                [s + (MIDDLE / 6.0) * t - x * u for s, t, x, u in zip(take(source1, row), total, w, rows[1])]
            )
            weights.append(w)
        means += cubes(*left) + cubes(*weights)
    small = times(jnp.concatenate(means, axis=0), pool)
    for pair in range(12):
        for i in range(2):
            s = small[32 * pair + 8 * i : 32 * pair + 8 * i + 8]
            w = small[32 * pair + 8 * i + 16 : 32 * pair + 8 * i + 24] + (4.0 * COARSE - 4.0 * MIDDLE)
            v = jnp.where(lane < 64, inside((pair + 1) // 2 - REACH) / jnp.where(lane < 64, w, 1.0), 0.0)
            source2[pair, i] = s
            inverse2[pair, i] = v
            coarse[pair, i] = v * s

    sweep(coarse, source2, inverse2, coarser, COARSE, 10, 10, (1, 1, 1), True)
    sweep(coarser, source2, inverse2, coarse, COARSE, 8, 8, (2, 2, 2), True)
    sweep(coarse, source2, inverse2, coarser, COARSE, 6, 6, (3, 3, 3), True)

    wide = times(jnp.concatenate([p for row in range(3, 9) for p in take(coarser, row)], axis=0), spread)
    for row in range(8, 20):
        for i in range(4):
            at = 16 * (row // 2 - 4) + 8 * (i // 2)
            other[row, i] = middle[row, i] + wide[at : at + 8]

    sweep(other, source1, inverse1, middle, MIDDLE, 8, 8, (10, 10, 10))
    sweep(middle, source1, inverse1, other, MIDDLE, 6, 6, (11, 11, 11))

    spread = spreading(128, 256)
    wide = times(jnp.concatenate([p for row in range(4) for p in take(other, 11 + 2 * c + row)], axis=0), spread)
    for row in range(8):
        for i in range(8):
            at = 32 * (row // 2) + 8 * (i // 2)
            work[row, i] = fine[row, i] + wide[at : at + 8]

    final = work.at[8:14]
    sweep(work, source, inverse, final, FINE, 6, 2, (0, 1, 2))
    for row in range(4):
        new = sweep_row(
            [take(final, row + d) for d in range(3)], take(source, row + 3), take(inverse, row + 3), FINE
        )
        for i, plane in enumerate(new):
            at = (i // 2) * 8 + (i % 2) * 4 + row
            for half in range(PZ):
                out[pl.ds(half * 32 + at, PX, stride=64), :] = plane[:, 128 * half : 128 * half + 128]


def unpack(blocks, out):
    for orbital in range(PX):
        for c in range(PZ):
            for i in range(8):
                base = (orbital * PZ + c) * 32 + (i // 2) * 8 + (i % 2) * 4
                out[orbital, i, 4 * c : 4 * c + 4] = blocks[base : base + 4]


def call(kernel, outs, scratch=(), anywhere=False, others=()):
    vmem = pl.BlockSpec(memory_space=pltpu.VMEM)

    def run(*args):
        return pl.pallas_call(
            kernel,
            out_shape=[(pltpu.VMEM if anywhere else jax.ShapeDtypeStruct)(shape, F32) for shape in outs],
            in_specs=[pl.BlockSpec(memory_space=pl.ANY) if anywhere else vmem] * len(args),
            out_specs=[vmem] * len(outs),
            scratch_shapes=[pltpu.VMEM(shape, F32) for shape in scratch] + list(others),
            compiler_params=pltpu.CompilerParams(vmem_limit_bytes=40 * 1024 * 1024),
        )(*args)

    return run


def run_down(*args):
    return call(
        down,
        [(8, 8, 8, 256), (10, 8, 8, 256), (10, 8, 8, 256), (2, 8, 8, 128)],
        [(12, 8, 8, 256)] + [(10, 8, 8, 256)] * 2,
    )(*args)


def run_up(*args):
    return call(
        up,
        [(512, 128)],
        [(28, 4, 8, 128)] * 5 + [(12, 2, 8, 128)] * 4 + [(14, 8, 8, 256)],
    )(*args)[0]


def body(residual, potential, shifts):
    size_y = lax.axis_size("dom") // (PX * PZ)
    blocks = [(px, py, c) for px in range(PX) for py in range(size_y) for c in range(PZ)]
    lines = [
        [dom_of(px, py, c, size_y) for px in range(PX) for c in range(PZ)] for py in range(size_y)
    ]
    cores = [
        [dom_of(px, py, c, size_y) for c in range(PZ)] for px in range(PX) for py in range(size_y)
    ]

    def pairs(target, bands=False):
        found = [((px, py, c), target(px, py, c)) for px, py, c in blocks]
        found = [(dom_of(*a, size_y), dom_of(*b, size_y)) for a, b in found if 0 <= b[1] < size_y]
        return [(2 * a + n, 2 * b + 1 - n) for a, b in found for n in range(2)] if bands else found

    def swap_lines(value):
        return lax.all_to_all(value, "dom", 0, 0, axis_index_groups=lines, tiled=True)

    def to_beside(px, py, c):
        return (px, py - 1, 1) if c == 0 else (px, py + 1, 0)

    packed, shift = call(
        pack,
        [(768, 128), (8, 128)],
        [(8, 8, 8, 128), (4, 8, 128)],
        anywhere=True,
        others=[pltpu.SMEM((8,), F32), pltpu.SemaphoreType.DMA((PX + 2,))],
    )(*[pltpu.with_memory_space_constraint(x, pltpu.HBM) for x in (residual, potential, shifts)])
    own = swap_lines(packed)
    half = own.reshape(16, 48, 128)[:, 32:].reshape(256, 128)
    both = ("dom", "band")
    own_half = lax.ppermute(half, "band", [(0, 1), (1, 0)])
    given, half = call(cut_out, [(704, 128), (192, 128)])(own)
    beside = lax.ppermute(given, "dom", pairs(to_beside))
    beside_half = lax.ppermute(half, both, pairs(to_beside, True))
    of_cores = lax.all_gather(own, "dom", axis_index_groups=cores, axis=0)
    of_cores_half = lax.all_gather(own_half, "dom", axis_index_groups=cores, axis=0)
    fine, source, inverse, cut = run_down(shift, of_cores, beside, of_cores_half, beside_half)
    block = lax.all_gather(cut, "dom", axis_index_groups=cores, axis=0, tiled=True)
    sent = [
        lax.ppermute(
            block,
            "dom",
            pairs(lambda px, py, c, k=k: (px, py + k, 0) if c == 0 else (px, py - k, 1)),
        )
        for k in range(REACH, 0, -1)
    ]
    around = lax.all_gather(jnp.stack(sent[::-1]), "dom", axis_index_groups=cores, axis=0)
    final = run_up(shift, fine, source, inverse, block, around)
    (correction,) = call(unpack, [(8, 8, 8, 128)])(swap_lines(final))
    return correction


def solution(mesh):
    return jax.shard_map(
        body,
        mesh=mesh,
        in_specs=(P("band", "dom", None, None), P(("dom", "band"), None, None), P("band")),
        out_specs=P("band", "dom", None, None),
        check_vma=False,
    )
```
